32 devices in a mesh: dp: 2 (over x), ep: 16 (over z, y, core).
Axes of the slice: x: 2, y: 2, z: 4, core: 2. Of those that a mesh axis runs over, the one named last changes fastest.
Arguments:
- hidden: bfloat16 [6, 1536, 1024], P('dp', 'ep'), may hold values from -6 to 6
- lengths: int32 [6], P('dp'), may hold values from 192 to 1536, as said below
- expert_ids: int32 [6, 1536, 8], P('dp', 'ep'), may hold values from 0 to 15, all different within a row
- pair_keep: int32 [6, 1536, 8], P('dp', 'ep'), may hold values 0 or 1
- attn_gain: bfloat16 [1024], P(('dp', 'ep')), may hold values from 0.25 to 1.75
- query_weight_matrix: bfloat16 [1024, 1024], P(('dp', 'ep')), may hold values from -0.1875 to 0.1875
- key_weight_matrix: bfloat16 [1024, 512], P(('dp', 'ep')), may hold values from -0.1875 to 0.1875
- value_weight_matrix: bfloat16 [1024, 512], P(('dp', 'ep')), may hold values from -0.1875 to 0.1875
- attention_output_weight: bfloat16 [1024, 1024], P(('dp', 'ep')), may hold values from -1.5 to 1.5
- moe_gain: bfloat16 [1024], P(('dp', 'ep')), may hold values from 0.25 to 1.75
- router_weight_matrix: bfloat16 [1024, 16], P(('dp', 'ep')), may hold values from -0.09375 to 0.09375
- w_gate_up: bfloat16 [16, 1024, 1024], P('ep'), may hold values from -0.1875 to 0.1875
- w_down: bfloat16 [16, 512, 1024], P('ep'), may hold values from -1 to 1
- out_grad: bfloat16 [6, 1536, 1024], P('dp', 'ep'), may hold values from -6 to 6
Outputs:
- output: bfloat16 [6, 1536, 1024], P('dp', 'ep')
- input_grad: float32 [6, 1536, 1024], P('dp', 'ep')
- attn_gain_grad: float32 [1024], P(('dp', 'ep'))
- w_query_grad: float32 [1024, 1024], P(('dp', 'ep'))
- w_key_grad: float32 [1024, 512], P(('dp', 'ep'))
- w_value_grad: float32 [1024, 512], P(('dp', 'ep'))
- w_out_grad: float32 [1024, 1024], P(('dp', 'ep'))
- moe_gain_grad: float32 [1024], P(('dp', 'ep'))
- w_router_grad: float32 [1024, 16], P(('dp', 'ep'))
- w_gate_up_grad: float32 [16, 1024, 1024], P('ep')
- w_down_grad: float32 [16, 512, 1024], P('ep')
The draws below stay inside these ranges and needn't reach their ends.
Inputs may be any that keep to these rules, and one draw needn't show every extreme that they name: `lengths`: in every group of 3 consecutive sequences (one index of dp) one has length 1536. `expert_ids`: the 8 ids of a token are distinct.
All inputs are finite; a program needn't handle non-finite values. No bound on the sum of `pair_keep` on one device may be relied on, other than what follows from the above.
Results may differ from the reference program's by a relative error of at most 0.019.
Values may be sent and summed in bfloat16 or wider, within the bound.
No kernel may reach another device: no remote copies, remote signals or barrier semaphores. Data moves between devices by JAX's collectives and lax.ppermute only.
A program may use at most 256 MiB of HBM per device.

```python
import math
import jax
import jax.numpy as jnp
from jax import lax

D = 1024
HQ = 16
HK = 8
HD = 64
FF = 512
TOP = 8
SEQ_DEV = 3
PAD_LEN = 1536
TOK_DEV = 96
SEQS = 6
EXPERTS = 16
CAP = 144
N_DP = 2
N_EP = 16


def draw_lengths(key, part):
    key = jax.random.fold_in(key, 7)
    first_key, second_key = jax.random.split(key)
    groups = SEQS // SEQ_DEV
    random_len = jax.random.randint(first_key, (groups, SEQ_DEV), PAD_LEN // 8, PAD_LEN + 1, dtype=jnp.int32)
    picked = jax.random.randint(second_key, (groups, 1), 0, SEQ_DEV, dtype=jnp.int32)
    column = jnp.arange(SEQ_DEV, dtype=jnp.int32)[None, :]
    return jnp.where(column == picked, PAD_LEN, random_len).reshape(SEQS).astype(jnp.int32)


def touch_ends(drawn, rng, low, largest):
    longest = drawn.shape.index(max(drawn.shape))
    spots = []
    for shift in (0, 1):
        where = [jax.random.randint(jax.random.fold_in(rng, axis), (), 0, length) for axis, length in enumerate(drawn.shape)]
        where[longest] = (where[longest] + shift) % drawn.shape[longest]
        spots.append(tuple(where))
    return drawn.at[spots[0]].set(low).at[spots[1]].set(largest)


def steps_of(rng, dims, cuts, least, top_value):
    factor_of, own = 1.0, jax.random.fold_in(rng, 6)
    for position, blocks in cuts:
        steps = jnp.exp(jax.random.uniform(jax.random.fold_in(own, position), (blocks,), jnp.float32, least / len(cuts), top_value / len(cuts)))
        factor_of = factor_of * jnp.repeat(steps, dims[position] // blocks).reshape([-1 if axis == position else 1 for axis in range(len(dims))])
    return factor_of


def picks_of(rng, rows, amount, top, lift):
    ranking = jax.random.permutation(jax.random.fold_in(rng, 1), amount)
    pull = ranking
    for power in range(3):
        pull = pull * pull // amount
    pull = pull * lift // amount
    chance = jax.random.randint(jax.random.fold_in(rng, 2), (rows, amount), 0, 4096) + pull
    fixed_rows = jax.random.permutation(jax.random.fold_in(rng, 3), rows)[jnp.arange(amount) % rows]
    chance = jnp.where(jnp.arange(rows)[:, None] == fixed_rows[None, :], 1 << 14, chance)
    score = chance * amount + jnp.arange(amount)
    return lax.top_k(score.astype(jnp.int32), top)[1].astype(jnp.int32)


def scatter_about(stream_key, extent, scale, most, cuts=(), held_as=jnp.bfloat16):
    drawn = scale * jax.random.normal(stream_key, extent, jnp.float32)
    if cuts:
        drawn = drawn * steps_of(stream_key, extent, cuts, -0.22, 0.18)
    return jnp.clip(drawn, -most, most).astype(held_as)


def setup_inputs(seed: int = 0) -> dict:
    keys = jax.random.split(jax.random.key(seed), 15)
    return {
        "hidden": scatter_about(keys[0], (SEQS, PAD_LEN, D), 1.0, 6.0, ((0, 2), (1, 16))),
        "lengths": draw_lengths(jax.random.fold_in(keys[14], 71), 0),
        "expert_ids": picks_of(keys[2], SEQS * PAD_LEN, EXPERTS, TOP, 4096).reshape((SEQS, PAD_LEN, TOP)),
        "pair_keep": touch_ends((jax.random.randint(keys[3], (SEQS, PAD_LEN, TOP), 0, 8) < 7).astype(jnp.int32), jax.random.fold_in(keys[3], 1), 0, 1),
        "attn_gain": jnp.clip(1.0 + 0.15 * jax.random.normal(keys[4], (D,), jnp.float32), 0.25, 1.75).astype(jnp.bfloat16),
        "query_weight_matrix": scatter_about(keys[5], (D, HQ * HD), D ** -0.5, 0.1875, ((0, 32),)),
        "key_weight_matrix": scatter_about(keys[6], (D, HK * HD), D ** -0.5, 0.1875, ((0, 32),)),
        "value_weight_matrix": scatter_about(keys[7], (D, HK * HD), D ** -0.5, 0.1875, ((0, 32),)),
        "attention_output_weight": scatter_about(keys[8], (HQ * HD, D), (HQ * HD // 64) ** -0.5, 1.5, ((0, 32),)),
        "moe_gain": jnp.clip(1.0 + 0.15 * jax.random.normal(keys[9], (D,), jnp.float32), 0.25, 1.75).astype(jnp.bfloat16),
        "router_weight_matrix": scatter_about(keys[10], (D, EXPERTS), (4 * D) ** -0.5, 0.09375, ((0, 32),)),
        "w_gate_up": scatter_about(keys[11], (EXPERTS, D, 2 * FF), D ** -0.5, 0.1875, ((0, 16),)),
        "w_down": scatter_about(keys[12], (EXPERTS, FF, D), (FF // 16) ** -0.5, 1.0, ((0, 16),)),
        "out_grad": scatter_about(keys[13], (SEQS, PAD_LEN, D), 1.0, 6.0, ((0, 2), (1, 16))),
    }


eps = 1e-05
theta_base = 10000.0
highest_precision = lax.Precision.HIGHEST

@jax.custom_vjp
def low(v):
    return lax.optimization_barrier(v.astype(jnp.bfloat16)).astype(jnp.float32)

@jax.custom_vjp
def lowered_backward(v):
    return v

def low_keep(v):
    return (low(v), None)

def low_pass(kept, grad):
    return (grad,)

def back_keep(v):
    return (v, None)

def back_low(kept, grad):
    return (low(grad),)
low.defvjp(low_keep, low_pass)
lowered_backward.defvjp(back_keep, back_low)

def angles(positions, head_size):
    half_size = head_size // 2
    rates = theta_base ** (-2.0 * jnp.arange(half_size, dtype=jnp.float32) / head_size)
    return positions.astype(jnp.float32)[:, None] * rates[None, :]

def rotate(field, angle_table):
    half_size = field.shape[-1] // 2
    cosine = jnp.cos(angle_table)[:, None, :]
    sine = jnp.sin(angle_table)[:, None, :]
    first = field[..., :half_size]
    second = field[..., half_size:]
    return jnp.concatenate([first * cosine - second * sine, second * cosine + first * sine], axis=-1)

def rms_scale(values_in):
    return lax.rsqrt(lax.optimization_barrier(jnp.mean(values_in * values_in, axis=-1, keepdims=True)) + eps)

def attend_sequence(item_in):
    queries, key_rows, value_rows, seq_length = item_in
    group_size = queries.shape[1] // key_rows.shape[1]
    key_full = jnp.repeat(key_rows, group_size, axis=1)
    value_full = jnp.repeat(value_rows, group_size, axis=1)
    total_len = queries.shape[0]
    block_len = math.gcd(total_len, 512)
    key_pos = jnp.arange(total_len, dtype=jnp.int32)

    def one_block(first_row):
        query_block = lax.dynamic_slice_in_dim(queries, first_row, block_len, 0)
        query_pos = first_row + jnp.arange(block_len, dtype=jnp.int32)
        scores = jnp.einsum('qhd,khd->hqk', query_block, key_full, precision=highest_precision) * HD ** (-0.5)
        scores = lowered_backward(scores)
        allowed = (key_pos[None, :] <= query_pos[:, None]) & (key_pos[None, :] < seq_length)
        scores = jnp.where(allowed[None], scores, -jnp.inf)
        weights = low(jax.nn.softmax(scores, axis=-1))
        return jnp.einsum('hqk,khd->qhd', weights, value_full, precision=highest_precision)
    first_rows = (jnp.arange(total_len // block_len, dtype=jnp.int32) * block_len).astype(jnp.int32)
    blocks = lax.map(jax.checkpoint(one_block), first_rows)
    return blocks.reshape(total_len, queries.shape[1], queries.shape[2])

def to_blocks(array):
    tail_shape = array.shape[2:]
    array = array.reshape((N_DP, SEQ_DEV, N_EP, TOK_DEV) + tail_shape)
    array = jnp.moveaxis(array, 2, 1)
    return array.reshape((N_DP * N_EP, SEQ_DEV * TOK_DEV) + tail_shape)

def from_blocks(array):
    tail_shape = array.shape[2:]
    array = array.reshape((N_DP, N_EP, SEQ_DEV, TOK_DEV) + tail_shape)
    array = jnp.moveaxis(array, 1, 2)
    return array.reshape((SEQS, PAD_LEN) + tail_shape)

def device_experts(normed_rows, gate_probs, expert_ids, live_pairs, w_gate_up, w_down):
    row_count, top_k = expert_ids.shape
    expert_count = w_gate_up.shape[0]
    pair_count = row_count * top_k
    pair_ids = expert_ids.reshape(pair_count)
    pair_live = live_pairs.reshape(pair_count)
    expert_marks = (pair_ids[:, None] == jnp.arange(expert_count, dtype=jnp.int32)[None, :]).astype(jnp.int32) * pair_live[:, None]
    before = jnp.cumsum(expert_marks, axis=0) - expert_marks
    slot_index = lax.optimization_barrier(jnp.sum(before * expert_marks, axis=1))
    is_sent = (pair_live > 0) & (slot_index < CAP)
    slot_dest = jnp.where(is_sent, pair_ids * CAP + slot_index, expert_count * CAP).astype(jnp.int32)
    slot_owner = jnp.full((expert_count * CAP,), pair_count, jnp.int32).at[slot_dest].set(jnp.arange(pair_count, dtype=jnp.int32), mode='drop')
    token_of = jnp.where(slot_owner < pair_count, slot_owner // top_k, row_count).astype(jnp.int32)
    buffer = jnp.take(normed_rows, token_of, axis=0, mode='fill', fill_value=0.0)
    buffer = lowered_backward(buffer.reshape(expert_count, CAP, -1))
    gate_up_out = lowered_backward(jnp.einsum('ecd,edf->ecf', buffer, w_gate_up, precision=highest_precision))
    active = low(jax.nn.silu(gate_up_out[..., :FF]) * gate_up_out[..., FF:])
    produced = jnp.einsum('ecf,efd->ecd', active, w_down, precision=highest_precision)
    produced = low(lowered_backward(produced)).reshape(expert_count * CAP, -1)
    picked = jnp.take(produced, slot_dest, axis=0, mode='fill', fill_value=0.0).reshape(row_count, top_k, -1)
    pair_coef = gate_probs * is_sent.reshape(row_count, top_k).astype(jnp.float32)
    return lax.optimization_barrier(jnp.sum(pair_coef[..., None] * picked, axis=1))

def forward_layer(hidden, attn_gain, query_weight_matrix, key_weight_matrix, value_weight_matrix, attention_output_weight, moe_gain, router_weight_matrix, w_gate_up, w_down, lengths, expert_ids, pair_keep):
    seq_count, total_len, model_width = hidden.shape
    normalized_input = low(hidden * rms_scale(hidden) * attn_gain)
    positions = jnp.arange(total_len, dtype=jnp.int32)
    angle_table = angles(positions, HD)
    unrotated_queries = jnp.einsum('rqj,jb->rqb', normalized_input, query_weight_matrix, precision=highest_precision)
    unrotated_keys = jnp.einsum('rqj,jb->rqb', normalized_input, key_weight_matrix, precision=highest_precision)
    projected_values = jnp.einsum('rqj,jb->rqb', normalized_input, value_weight_matrix, precision=highest_precision)
    queries = low(rotate(lowered_backward(unrotated_queries).reshape(seq_count, total_len, HQ, HD), angle_table))
    key_rows = low(rotate(lowered_backward(unrotated_keys).reshape(seq_count, total_len, HK, HD), angle_table))
    value_rows = low(lowered_backward(projected_values)).reshape(seq_count, total_len, HK, HD)
    attention_blended = lax.map(attend_sequence, (queries, key_rows, value_rows, lengths))
    attention_blended = low(lowered_backward(attention_blended.reshape(seq_count, total_len, HQ * HD)))
    branch_output = lowered_backward(jnp.einsum('ajg,gc->ajc', attention_blended, attention_output_weight, precision=highest_precision))
    residual = hidden + branch_output
    normalized_second = low(residual * rms_scale(residual) * moe_gain)
    router_logits = jnp.einsum('coj,jp->cop', normalized_second, router_weight_matrix, precision=highest_precision)
    chosen = jnp.take_along_axis(router_logits, expert_ids, axis=-1)
    gate_probs = jax.nn.softmax(chosen, axis=-1)
    is_valid = positions[None, :] < lengths[:, None]
    live_pairs = pair_keep * is_valid.astype(jnp.int32)[..., None]

    def one_device(item_in):
        return device_experts(item_in[0], item_in[1], item_in[2], item_in[3], w_gate_up, w_down)
    moe_out = lax.map(jax.checkpoint(one_device), (to_blocks(normalized_second), to_blocks(gate_probs), to_blocks(expert_ids), to_blocks(live_pairs)))
    moe_out = from_blocks(moe_out)
    return (residual + moe_out) * is_valid.astype(jnp.float32)[..., None]

def reference(hidden, lengths, expert_ids, pair_keep, attn_gain, query_weight_matrix, key_weight_matrix, value_weight_matrix, attention_output_weight, moe_gain, router_weight_matrix, w_gate_up, w_down, out_grad):
    floats = tuple((array.astype(jnp.float32) for array in (hidden, attn_gain, query_weight_matrix, key_weight_matrix, value_weight_matrix, attention_output_weight, moe_gain, router_weight_matrix, w_gate_up, w_down)))

    def wrapped(*arrays):
        return forward_layer(*arrays, lengths, expert_ids, pair_keep)
    output, pullback = jax.vjp(wrapped, *floats)
    grads = pullback(out_grad.astype(jnp.float32))
    return (output.astype(jnp.bfloat16), grads[0], grads[1], grads[2], grads[3], grads[4], grads[5], grads[6], grads[7], grads[8], grads[9])
```

```python
import functools

import jax
import jax.numpy as jnp
from jax import lax
from jax.experimental import pallas as pl
from jax.experimental.pallas import tpu as pltpu
from jax.sharding import PartitionSpec as P

HD = 64
LANES = 128
SLAB = 256
PACK = 256
eps = 1e-05
theta_base = 10000.0
f32 = jnp.float32
bf16 = jnp.bfloat16
VMEM_LIMIT = 56 * 1024 * 1024


def dot(a, b):
    return lax.dot_general(a, b, (((1,), (0,)), ((), ())), preferred_element_type=f32)


def dot_nt(a, b):
    return lax.dot_general(a, b, (((1,), (1,)), ((), ())), preferred_element_type=f32)


def dot_tn(a, b):
    return lax.dot_general(a, b, (((0,), (0,)), ((), ())), preferred_element_type=f32)


def lanes_of(rows, width=LANES):
    return lax.broadcasted_iota(jnp.int32, (rows, width), 1)


def half_swap(x):
    lane = lanes_of(x.shape[0])
    return jnp.where(lane % HD < HD // 2, pltpu.roll(x, LANES - HD // 2, 1), pltpu.roll(x, HD // 2, 1))


def ep_shape(ep):
    zs = 4 if ep % 8 == 0 else 1
    return zs, ep // (2 * zs), 2


def fetch_from(ep, dz=0, dy=0, dc=0):
    zs, ys, cs = ep_shape(ep)
    pairs = []
    for z in range(zs):
        for y in range(ys):
            for c in range(cs):
                src = (((z + dz) % zs) * ys + (y + dy) % ys) * cs + (c + dc) % cs
                pairs.append((src, (z * ys + y) * cs + c))
    return pairs


def send_to(ep, **offset):
    return [(dst, src) for src, dst in fetch_from(ep, **offset)]


def gather_blocks(x, ep):
    zs, ys, _ = ep_shape(ep)
    column = jnp.stack([x] + [lax.ppermute(x, "ep", fetch_from(ep, dz=d)) for d in range(1, zs)])
    near = jnp.stack(
        [column] + [lax.ppermute(column, "ep", fetch_from(ep, dy=d)) for d in range(1, ys)]
    )
    far = lax.ppermute(near, "ep", fetch_from(ep, dc=1))
    return near, far


def reduce_blocks(near, far, ep):
    zs, ys, _ = ep_shape(ep)
    got = lax.ppermute(far, "ep", send_to(ep, dc=1))
    chip = [(near[d].astype(f32) + got[d].astype(f32)).astype(bf16) for d in range(ys)]
    moved = [lax.ppermute(chip[d], "ep", send_to(ep, dy=d)) for d in range(1, ys)]
    own = []
    for d in range(zs):
        total = chip[0][d].astype(f32)
        for part in moved:
            total = total + part[d].astype(f32)
        own.append(total.astype(bf16))
    return [own[0]] + [lax.ppermute(own[d], "ep", send_to(ep, dz=d)) for d in range(1, zs)]


META_HEAD = 3


def group_rows(near_ref, far_ref, dz):
    ys = near_ref.shape[0]
    return jnp.concatenate(
        [near_ref[d, dz] for d in range(ys)] + [far_ref[d, dz] for d in range(ys)], axis=0
    )


def front_kernel(
    replicas,
    meta,
    near_ref,
    far_ref,
    w_ref,
    gain_ref,
    cos_ref,
    sin_ref,
    out_ref,
    normed_ref,
    qk_ref,
    v_ref,
    qkt_ref,
    stat_ref,
    raw_ref,
    vt_ref,
    wide_ref,
):
    ys, zs, span, _ = near_ref.shape
    total = normed_ref.shape[0]
    blocks = 2 * ys
    length = meta[0]
    for dz in range(zs):
        start = pl.multiple_of(meta[META_HEAD + dz], 32)

        @pl.when(start < length)
        def _():
            x = group_rows(near_ref, far_ref, dz).astype(f32)
            scale = lax.rsqrt(jnp.mean(x * x, axis=-1, keepdims=True) + eps)
            normed = (x * scale * gain_ref[...]).astype(bf16)
            raw = dot(normed, w_ref[...])
            for j in range(blocks):
                row = pl.multiple_of(start + meta[META_HEAD + 2 * zs + j] * span, 32)
                normed_ref[pl.ds(row, span), :] = normed[j * span : (j + 1) * span]
                raw_ref[pl.ds(row, span), :] = raw[j * span : (j + 1) * span]

        @pl.when(start >= length)
        def _():
            normed_ref[pl.ds(start, blocks * span), :] = jnp.zeros(
                (blocks * span, normed_ref.shape[1]), bf16
            )
            raw_ref[pl.ds(start, blocks * span), :] = jnp.zeros((blocks * span, PACK), f32)

    for lo in range(0, total, SLAB):
        rows = slice(lo, lo + SLAB)
        raw = raw_ref[rows, 0:LANES]
        turned = raw * cos_ref[rows, :] + half_swap(raw) * sin_ref[rows, :]
        turned = turned.astype(bf16).astype(f32)
        turned = jnp.where(lanes_of(SLAB) < HD, turned * HD ** (-0.5), turned)
        qk_ref[rows, :] = turned.astype(bf16)
        qkt_ref[:, rows] = turned.T.astype(bf16)
        value = raw_ref[rows, LANES : 2 * LANES]
        value = jnp.where(lanes_of(SLAB) < HD, value, 0.0)
        v_ref[rows, :] = value.astype(bf16)
        vt_ref[:, rows] = value.T.astype(bf16)

    key_row = lax.broadcasted_iota(jnp.int32, (SLAB, SLAB), 0)
    query_col = lax.broadcasted_iota(jnp.int32, (SLAB, SLAB), 1)
    for i, lo in enumerate(range(0, total, SLAB)):
        hi = lo + SLAB
        mine = lo < length
        if replicas > 1:
            mine = mine & (meta[1] == i % replicas)

        @pl.when(mine)
        def _():
            qt = qkt_ref[0:HD, lo:hi]
            diag = dot(qk_ref[lo:hi, HD:LANES], qt)
            diag = jnp.where(key_row <= query_col, diag, -jnp.inf)
            top = jnp.max(diag, axis=0, keepdims=True)
            if lo:
                full = dot(qk_ref[0:lo, HD:LANES], qt)
                top = jnp.maximum(top, jnp.max(full, axis=0, keepdims=True))
            p_diag = jnp.exp(diag - top)
            row_total = jnp.sum(p_diag, axis=0, keepdims=True)
            out = dot(vt_ref[:, lo:hi], p_diag.astype(bf16))
            if lo:
                p_full = jnp.exp(full - top)
                row_total = row_total + jnp.sum(p_full, axis=0, keepdims=True)
                out = out + dot(vt_ref[:, 0:lo], p_full.astype(bf16))
            out = out[0:HD] / row_total
            stat_ref[0:HD, lo:hi] = out
            stat_ref[HD : HD + 8, lo:hi] = jnp.broadcast_to(top + jnp.log(row_total), (8, SLAB))
            wide_ref[lo:hi, :] = jnp.concatenate([out, out], axis=0).T

        @pl.when(jnp.logical_not(mine))
        def _():
            stat_ref[:, lo:hi] = jnp.zeros((HD + 8, SLAB), f32)
            wide_ref[lo:hi, :] = jnp.zeros((SLAB, LANES), f32)

    half = span // 2
    for e in range(total // span):
        upper = wide_ref[e * span : e * span + half, :]
        lower = wide_ref[e * span + half : (e + 1) * span, :]
        out_ref[e] = jnp.where(lanes_of(half) < HD, upper, lower).astype(bf16)


def front(meta, near, far, w, gain, cos, sin, replicas):
    ys, zs, span, width = near.shape
    total = 2 * ys * zs * span
    vmem = pl.BlockSpec(memory_space=pltpu.VMEM)
    return pl.pallas_call(
        functools.partial(front_kernel, replicas),
        out_shape=(
            jax.ShapeDtypeStruct((total // span, span // 2, LANES), bf16),
            jax.ShapeDtypeStruct((total, width), bf16),
            jax.ShapeDtypeStruct((total, LANES), bf16),
            jax.ShapeDtypeStruct((total, LANES), bf16),
            jax.ShapeDtypeStruct((LANES, total), bf16),
            jax.ShapeDtypeStruct((HD + 8, total), f32),
        ),
        in_specs=[pl.BlockSpec(memory_space=pltpu.SMEM)] + [vmem] * 6,
        out_specs=(vmem,) * 6,
        scratch_shapes=[
            pltpu.VMEM((total, PACK), f32),
            pltpu.VMEM((LANES, total), bf16),
            pltpu.VMEM((total, LANES), f32),
        ],
        compiler_params=pltpu.CompilerParams(vmem_limit_bytes=VMEM_LIMIT),
        cost_estimate=pl.CostEstimate(
            flops=2 * total * width * PACK + 4 * total * total * LANES,
            bytes_accessed=6 * total * width,
            transcendentals=total * total // 2,
        ),
        name="attend_forward",
    )(meta, near, far, w, gain, cos, sin)


def middle_kernel(
    recv_ref,
    hid_ref,
    wo_ref,
    gain_ref,
    wr_ref,
    chosen_ref,
    sent_ref,
    res_ref,
    pay_ref,
    mixed_ref,
    gate_ref,
):
    heads, half, _ = recv_ref.shape
    span, width = hid_ref.shape
    low = lanes_of(half) < HD
    uppers, lowers = [], []
    for j in range(heads // 2):
        a = recv_ref[2 * j].astype(f32)
        b = recv_ref[2 * j + 1].astype(f32)
        uppers.append(jnp.where(low, a, pltpu.roll(b, HD, 1)).astype(bf16))
        lowers.append(jnp.where(low, pltpu.roll(a, HD, 1), b).astype(bf16))
    mixed = jnp.concatenate(
        [jnp.concatenate(uppers, axis=1), jnp.concatenate(lowers, axis=1)], axis=0
    )
    mixed_ref[...] = mixed
    res = hid_ref[...].astype(f32) + dot(mixed, wo_ref[...])
    res_ref[...] = res
    scale = lax.rsqrt(jnp.mean(res * res, axis=-1, keepdims=True) + eps)
    normed = (res * scale * gain_ref[...]).astype(bf16)
    logits = dot(normed, wr_ref[...])
    logits = jnp.where(chosen_ref[...] > 0, logits, -jnp.inf)
    powers = jnp.exp(logits - jnp.max(logits, axis=-1, keepdims=True))
    gates = powers / jnp.sum(powers, axis=-1, keepdims=True)
    gate_ref[...] = gates
    used = gates * sent_ref[...]
    upper = used.astype(bf16).astype(f32)
    pay_ref[:, 0:width] = normed
    pay_ref[:, width:] = (upper + pltpu.roll(used - upper, HD, 1)).astype(bf16)


def middle(recv, hid, wo, gain, wr, chosen, sent):
    span, width = hid.shape
    vmem = pl.BlockSpec(memory_space=pltpu.VMEM)
    return pl.pallas_call(
        middle_kernel,
        out_shape=(
            jax.ShapeDtypeStruct((span, width), f32),
            jax.ShapeDtypeStruct((span, width + LANES), bf16),
            jax.ShapeDtypeStruct((span, width), bf16),
            jax.ShapeDtypeStruct((span, LANES), f32),
        ),
        in_specs=[vmem] * 7,
        out_specs=(vmem,) * 4,
        compiler_params=pltpu.CompilerParams(vmem_limit_bytes=VMEM_LIMIT),
        cost_estimate=pl.CostEstimate(
            flops=4 * span * width * width, bytes_accessed=4 * width * width, transcendentals=0
        ),
        name="project_out",
    )(recv, hid, wo, gain, wr, chosen, sent)


def expert_kernel(
    first, meta, near_ref, far_ref, up_ref, wgu_ref, wd_ref, *rest
):
    if first:
        rnear_ref, rfar_ref, moe_ref, dgu_ref, dd_ref = rest
    else:
        _, gu_in, d_in, rnear_ref, rfar_ref, moe_ref, dgu_ref, dd_ref = rest
    ys, _, span, wide = near_ref.shape
    width = wide - LANES
    blocks = 2 * ys
    rows = blocks * span
    dz = pl.program_id(0)
    zs = pl.num_programs(0)

    @pl.when(dz == 0)
    def _():
        if first:
            dgu_ref[...] = jnp.zeros_like(dgu_ref)
            dd_ref[...] = jnp.zeros_like(dd_ref)
        else:
            dgu_ref[...] = gu_in[...]
            dd_ref[...] = d_in[...]

    live = meta[META_HEAD + dz] < meta[0]
    places = [meta[META_HEAD + 2 * zs + j] for j in range(blocks)]

    @pl.when(live)
    def _():
        hidden_units = wd_ref.shape[0]
        x = group_rows(near_ref, far_ref, 0)
        normed = x[:, 0:width]
        lane = lanes_of(rows)
        mine = (lane == meta[2]) | (lane == meta[2] + HD)
        gate_prob = jnp.sum(
            jnp.where(mine, x[:, width:].astype(f32), 0.0), axis=-1, keepdims=True
        )
        upstream = jnp.concatenate([up_ref[places[j], 0] for j in range(blocks)], axis=0).astype(f32)
        gate_up = dot(normed, wgu_ref[...])
        gate = gate_up[:, 0:hidden_units]
        up = gate_up[:, hidden_units:]
        sig = jax.nn.sigmoid(gate)
        silu = gate * sig
        act = (silu * up).astype(bf16)
        made = dot(act, wd_ref[...]).astype(bf16).astype(f32)
        gate_grad = jnp.sum(made * upstream, axis=-1, keepdims=True)
        moe = (made * gate_prob).astype(bf16)
        pair_grad = (upstream * gate_prob).astype(bf16)
        act_grad = dot_nt(pair_grad, wd_ref[...])
        both = jnp.concatenate(
            [act_grad * up * (sig * (1.0 + gate * (1.0 - sig))), act_grad * silu], axis=1
        ).astype(bf16)
        back = dot_nt(both, wgu_ref[...]).astype(bf16)
        dgu_ref[...] += dot_tn(normed, both)
        dd_ref[...] += dot_tn(act, pair_grad)
        upper = gate_grad.astype(bf16).astype(f32)
        extra = jnp.where(lane == meta[2], upper, 0.0)
        extra = jnp.where(lane == meta[2] + HD, gate_grad - upper, extra).astype(bf16)
        for d in range(ys):
            for ref, j in ((rnear_ref, d), (rfar_ref, ys + d)):
                ref[d, 0, :, 0:width] = back[j * span : (j + 1) * span]
                ref[d, 0, :, width:] = extra[j * span : (j + 1) * span]
        for j in range(blocks):
            moe_ref[places[j], 0] = moe[j * span : (j + 1) * span]

    @pl.when(jnp.logical_not(live))
    def _():
        rnear_ref[...] = jnp.zeros_like(rnear_ref)
        rfar_ref[...] = jnp.zeros_like(rfar_ref)
        moe_ref[...] = jnp.zeros_like(moe_ref)


def experts(meta, near, far, upstream, wgu, wd, seq, carried):
    ys, zs, span, wide = near.shape
    ep, seqs, _, width = upstream.shape
    units = wd.shape[0]
    first = carried is None
    block = pl.BlockSpec((ys, 1, span, wide), lambda i, m: (0, i, 0, 0))
    natural = pl.BlockSpec((2 * ys, 1, span, width), lambda i, m: (m[META_HEAD + zs + i], seq, 0, 0))
    once = pl.Buffered(1)
    gu_spec = pl.BlockSpec((width, 2 * units), lambda i, m: (0, 0), pipeline_mode=once)
    d_spec = pl.BlockSpec((units, width), lambda i, m: (0, 0), pipeline_mode=once)
    in_specs = [block, block, natural, gu_spec, d_spec]
    args = [near, far, upstream, wgu, wd]
    aliases = {}
    if not first:
        in_specs += [pl.BlockSpec(memory_space=pl.ANY), gu_spec, d_spec]
        args += list(carried)
        aliases = {6: 2, 7: 3, 8: 4}
    out_gu = pl.BlockSpec((width, 2 * units), lambda i, m: (0, 0))
    out_d = pl.BlockSpec((units, width), lambda i, m: (0, 0))
    rows = 2 * ys * zs * span
    return pl.pallas_call(
        functools.partial(expert_kernel, first),
        grid_spec=pltpu.PrefetchScalarGridSpec(
            num_scalar_prefetch=1,
            grid=(zs,),
            in_specs=in_specs,
            out_specs=(block, block, natural, out_gu, out_d),
        ),
        out_shape=(
            jax.ShapeDtypeStruct(near.shape, bf16),
            jax.ShapeDtypeStruct(near.shape, bf16),
            jax.ShapeDtypeStruct(upstream.shape, bf16),
            jax.ShapeDtypeStruct((width, 2 * units), f32),
            jax.ShapeDtypeStruct((units, width), f32),
        ),
        input_output_aliases=aliases,
        compiler_params=pltpu.CompilerParams(vmem_limit_bytes=VMEM_LIMIT),
        cost_estimate=pl.CostEstimate(
            flops=18 * rows * width * units, bytes_accessed=12 * rows * width, transcendentals=0
        ),
        name="experts",
    )(meta, *args)


def turn_kernel(
    nparts,
    meta,
    *refs,
):
    parts = refs[:nparts]
    (
        res_ref,
        pay_ref,
        up_ref,
        gate_ref,
        sent_ref,
        wr_ref,
        gain_ref,
        wo_ref,
        resgrad_ref,
        branch_ref,
        out_ref,
        logit_ref,
        gaingrad_ref,
    ) = refs[nparts:]
    span, width = res_ref.shape
    total = parts[0][...].astype(f32)
    for part in parts[1:]:
        total = total + part[...].astype(f32)
    extra = total[:, width:]
    gate_grad = (extra + pltpu.roll(extra, HD, 1)) * sent_ref[...]
    gates = gate_ref[...]
    logit_grad = gates * (gate_grad - jnp.sum(gates * gate_grad, axis=-1, keepdims=True))
    logit_ref[...] = logit_grad
    normed_grad = total[:, 0:width] + lax.dot_general(
        logit_grad,
        wr_ref[...].astype(f32),
        (((1,), (1,)), ((), ())),
        preferred_element_type=f32,
        precision=lax.Precision.HIGHEST,
    )
    res = res_ref[...]
    scale = lax.rsqrt(jnp.mean(res * res, axis=-1, keepdims=True) + eps)
    gaingrad_ref[...] = jnp.sum(normed_grad * (res * scale), axis=0, keepdims=True)
    scaled = normed_grad * gain_ref[...]
    row = meta[1] + lax.broadcasted_iota(jnp.int32, (span, 1), 0)
    upstream = jnp.where(row < meta[0], up_ref[...].astype(f32), 0.0)
    centre = jnp.mean(scaled * res, axis=-1, keepdims=True)
    res_grad = upstream + scaled * scale - res * (scale * scale * scale * centre)
    resgrad_ref[...] = res_grad
    branch = res_grad.astype(bf16)
    branch_ref[...] = branch
    mixed = dot_nt(branch, wo_ref[...]).astype(bf16).astype(f32)
    half = span // 2
    low = lanes_of(half) < HD
    for j in range(out_ref.shape[0] // 2):
        upper = mixed[0:half, j * LANES : (j + 1) * LANES]
        lower = mixed[half:, j * LANES : (j + 1) * LANES]
        out_ref[2 * j] = jnp.where(low, upper, pltpu.roll(lower, HD, 1)).astype(bf16)
        out_ref[2 * j + 1] = jnp.where(low, pltpu.roll(upper, HD, 1), lower).astype(bf16)


def turn(meta, parts, res, pay, up, gates, sent, wr, gain, wo):
    span, width = res.shape
    heads = wo.shape[0] // HD
    vmem = pl.BlockSpec(memory_space=pltpu.VMEM)
    return pl.pallas_call(
        functools.partial(turn_kernel, len(parts)),
        out_shape=(
            jax.ShapeDtypeStruct((span, width), f32),
            jax.ShapeDtypeStruct((span, width), bf16),
            jax.ShapeDtypeStruct((heads, span // 2, LANES), bf16),
            jax.ShapeDtypeStruct((span, LANES), f32),
            jax.ShapeDtypeStruct((1, width), f32),
        ),
        in_specs=[pl.BlockSpec(memory_space=pltpu.SMEM)] + [vmem] * (len(parts) + 8),
        out_specs=(vmem,) * 5,
        compiler_params=pltpu.CompilerParams(vmem_limit_bytes=VMEM_LIMIT),
        cost_estimate=pl.CostEstimate(
            flops=4 * span * width * width, bytes_accessed=4 * width * width, transcendentals=0
        ),
        name="turn_back",
    )(meta, *parts, res, pay, up, gates, sent, wr, gain, wo)


def back_kernel(
    replicas,
    meta,
    grad_ref,
    qk_ref,
    v_ref,
    qkt_ref,
    stat_ref,
    w_ref,
    cos_ref,
    sin_ref,
    near_ref,
    far_ref,
    dqkv_ref,
    do_ref,
    dot_ref,
    delta_ref,
    dk_ref,
    dv_ref,
    dqt_ref,
    group_ref,
):
    ys, zs, span, width = near_ref.shape
    total = qk_ref.shape[0]
    length = meta[0]
    half = span // 2
    for e in range(total // span):
        chunk = grad_ref[e].astype(f32)
        do_ref[e * span : e * span + half, :] = chunk
        do_ref[e * span + half : (e + 1) * span, :] = pltpu.roll(chunk, HD, 1)
    dk_ref[...] = jnp.zeros_like(dk_ref)
    dv_ref[...] = jnp.zeros_like(dv_ref)
    key_row = lax.broadcasted_iota(jnp.int32, (SLAB, SLAB), 0)
    query_col = lax.broadcasted_iota(jnp.int32, (SLAB, SLAB), 1)
    for i, lo in enumerate(range(0, total, SLAB)):
        hi = lo + SLAB
        mine = lo < length
        if replicas > 1:
            mine = mine & (meta[1] == i % replicas)

        @pl.when(mine)
        def _():
            qt = qkt_ref[0:HD, lo:hi]
            qk = qk_ref[lo:hi, :]
            grad = do_ref[lo:hi, :]
            grad_low = grad.astype(bf16)
            grad_t = grad.T[0:HD]
            delta = jnp.sum(grad_t * stat_ref[0:HD, lo:hi], axis=0, keepdims=True)
            grad_t = grad_t.astype(bf16)
            log_total = stat_ref[HD : HD + 1, lo:hi]

            def piece(start, stop, masked):
                scores = dot(qk_ref[start:stop, HD:LANES], qt)
                probs = jnp.exp(scores - log_total)
                if masked:
                    probs = jnp.where(key_row <= query_col, probs, 0.0)
                prob_grad = dot(v_ref[start:stop, 0:HD], grad_t)
                score_grad = (probs * (prob_grad - delta)).astype(bf16)
                dv_ref[start:stop, :] += dot(probs.astype(bf16), grad_low)
                dk_ref[start:stop, :] += dot(score_grad, qk)
                return dot(qkt_ref[:, start:stop], score_grad)

            moved = piece(lo, hi, True)
            if lo:
                moved = moved + piece(0, lo, False)
            dqt_ref[:, lo:hi] = moved

        @pl.when(jnp.logical_not(mine))
        def _():
            dqt_ref[:, lo:hi] = jnp.zeros((LANES, SLAB), f32)

    low = lanes_of(SLAB) < HD
    for lo in range(0, total, SLAB):
        rows = slice(lo, lo + SLAB)
        both = jnp.where(low, dk_ref[rows, :], dqt_ref[:, rows].T * HD ** (-0.5))
        both = pltpu.roll(both, HD, 1)
        both = both * cos_ref[rows, :] - half_swap(both) * sin_ref[rows, :]
        dqkv_ref[rows, 0:LANES] = both.astype(bf16)
        dqkv_ref[rows, LANES:PACK] = jnp.where(low, dv_ref[rows, :], 0.0).astype(bf16)

    blocks = 2 * ys
    for dz in range(zs):
        start = pl.multiple_of(meta[META_HEAD + dz], 32)

        @pl.when(start < length)
        def _():
            group_ref[...] = dot_nt(
                dqkv_ref[pl.ds(start, blocks * span), :], w_ref[...]
            ).astype(bf16)
            for d in range(ys):
                for ref, j in ((near_ref, d), (far_ref, ys + d)):
                    row = pl.multiple_of(meta[META_HEAD + 2 * zs + j] * span, 32)
                    ref[d, dz] = group_ref[pl.ds(row, span), :]

        @pl.when(start >= length)
        def _():
            near_ref[:, dz] = jnp.zeros((ys, span, width), bf16)
            far_ref[:, dz] = jnp.zeros((ys, span, width), bf16)


def back(meta, grads, qk, v, qkt, stat, w, cos, sin, shape, replicas):
    ys, zs, span, width = shape
    total = qk.shape[0]
    vmem = pl.BlockSpec(memory_space=pltpu.VMEM)
    return pl.pallas_call(
        functools.partial(back_kernel, replicas),
        out_shape=(
            jax.ShapeDtypeStruct(shape, bf16),
            jax.ShapeDtypeStruct(shape, bf16),
            jax.ShapeDtypeStruct((total, PACK), bf16),
        ),
        in_specs=[pl.BlockSpec(memory_space=pltpu.SMEM)] + [vmem] * 8,
        out_specs=(vmem,) * 3,
        scratch_shapes=[
            pltpu.VMEM((total, LANES), f32),
            pltpu.VMEM((8, LANES), f32),
            pltpu.VMEM((8, LANES), f32),
            pltpu.VMEM((total, LANES), f32),
            pltpu.VMEM((total, LANES), f32),
            pltpu.VMEM((LANES, total), f32),
            pltpu.VMEM((2 * ys * span, width), bf16),
        ],
        compiler_params=pltpu.CompilerParams(vmem_limit_bytes=VMEM_LIMIT),
        cost_estimate=pl.CostEstimate(
            flops=2 * total * width * PACK + 10 * total * total * LANES,
            bytes_accessed=6 * total * width,
            transcendentals=total * total // 2,
        ),
        name="attend_backward",
    )(meta, grads, qk, v, qkt, stat, w, cos, sin)


def finish_kernel(seqs, nparts, *refs):
    hid_ref, gain_ref = refs[0:2]
    resgrads = refs[2 : 2 + seqs]
    parts = refs[2 + seqs : 2 + seqs + seqs * nparts]
    out_ref = refs[-1]
    for s in range(seqs):
        mine = parts[s * nparts : (s + 1) * nparts]
        total = mine[0][...].astype(f32)
        for part in mine[1:]:
            total = total + part[...].astype(f32)
        x = hid_ref[s].astype(f32)
        scale = lax.rsqrt(jnp.mean(x * x, axis=-1, keepdims=True) + eps)
        scaled = total * gain_ref[...]
        centre = jnp.mean(scaled * x, axis=-1, keepdims=True)
        out_ref[s] = resgrads[s][...] + scaled * scale - x * (scale * scale * scale * centre)


def finish(hidden, gain, resgrads, parts):
    seqs, span, width = hidden.shape
    vmem = pl.BlockSpec(memory_space=pltpu.VMEM)
    flat = [p for group in parts for p in group]
    return pl.pallas_call(
        functools.partial(finish_kernel, seqs, len(parts[0])),
        out_shape=jax.ShapeDtypeStruct(hidden.shape, f32),
        in_specs=[vmem] * (2 + seqs + len(flat)),
        out_specs=vmem,
        compiler_params=pltpu.CompilerParams(vmem_limit_bytes=VMEM_LIMIT),
        name="input_grad",
    )(hidden, gain, *resgrads, *flat)


def body(
    hidden,
    lengths,
    expert_ids,
    pair_keep,
    attn_gain,
    query_weight_matrix,
    key_weight_matrix,
    value_weight_matrix,
    attention_output_weight,
    moe_gain,
    router_weight_matrix,
    w_gate_up,
    w_down,
    out_grad,
):
    seqs, span, width = hidden.shape
    rows = seqs * span
    top_k = expert_ids.shape[2]
    ep = lax.axis_size("ep")
    dp = lax.axis_size("dp")
    zs, ys, _ = ep_shape(ep)
    me = lax.axis_index("ep").astype(jnp.int32)
    expert_count = w_gate_up.shape[0] * ep
    capacity = max(2, rows * top_k // expert_count)
    heads = query_weight_matrix.shape[1] // HD
    kv_heads = key_weight_matrix.shape[1] // HD
    replicas = ep // heads
    total = span * ep
    own_rows = query_weight_matrix.shape[0]

    def per_head(weight, count):
        split = weight.reshape(own_rows, count, HD).transpose(1, 0, 2)
        return jnp.repeat(split, heads // count, axis=0)

    small = jnp.concatenate(
        [router_weight_matrix, attn_gain[:, None], moe_gain[:, None]], axis=1
    )
    small = jnp.pad(small, ((0, 0), (0, PACK - 3 * HD - small.shape[1])))
    packed = jnp.concatenate(
        [
            per_head(query_weight_matrix, heads),
            per_head(key_weight_matrix, kv_heads),
            per_head(value_weight_matrix, kv_heads),
            jnp.broadcast_to(small[None], (heads,) + small.shape),
        ],
        axis=2,
    )
    packed = jnp.repeat(packed, replicas, axis=0)
    packed = jnp.broadcast_to(packed[None], (dp,) + packed.shape).reshape(
        dp * ep, own_rows, PACK
    )
    packed = lax.all_to_all(packed, ("dp", "ep"), split_axis=0, concat_axis=0, tiled=True)
    head_w = packed.reshape(dp * ep * own_rows, PACK)
    at = 3 * HD
    wr = jnp.pad(head_w[:, at : at + expert_count], ((0, 0), (0, LANES - expert_count)))
    gains = head_w[:, at + expert_count : at + expert_count + 2].astype(f32)
    gain_one = gains[:, 0].reshape(1, width)
    gain_two = gains[:, 1].reshape(1, width)
    head_w = jnp.where(jnp.arange(PACK)[None, :] < at, head_w, jnp.zeros((), bf16))
    wo = lax.all_gather(attention_output_weight, ("dp", "ep"), axis=0, tiled=True)
    upstream = lax.all_gather(out_grad, "ep", axis=0)

    positions = me * span + jnp.arange(span, dtype=jnp.int32)
    is_valid = positions[None, :] < lengths[:, None]
    expert_range = jnp.arange(LANES, dtype=jnp.int32)
    hit = expert_ids[..., None] == expert_range
    chosen = jnp.any(hit, axis=2).reshape(rows, LANES)
    live = jnp.any(hit & (pair_keep[..., None] > 0), axis=2) & is_valid[..., None]
    live = live.reshape(rows, LANES).astype(bf16)
    earlier = jnp.arange(rows)[:, None] > jnp.arange(rows)[None, :]
    slot = jnp.dot(earlier.astype(bf16), live, preferred_element_type=f32)
    sent = jnp.where(slot < capacity, live.astype(f32), 0.0).reshape(seqs, span, LANES)
    chosen = chosen.astype(f32).reshape(seqs, span, LANES)

    rates = theta_base ** (-2.0 * jnp.arange(HD // 2, dtype=f32) / HD)
    angle = jnp.arange(total, dtype=jnp.int32).astype(f32)[:, None] * rates[None, :]
    cos = jnp.tile(jnp.cos(angle), (1, 4))
    sin = jnp.sin(angle)
    sin = jnp.concatenate([-sin, sin, -sin, sin], axis=1)
    core = me % 2
    col = (me // 2) % ys
    plane = me // (2 * ys)
    planes = (plane + jnp.arange(zs, dtype=jnp.int32)) % zs
    rows_at = (col + jnp.arange(ys, dtype=jnp.int32)) % ys
    places = jnp.concatenate([rows_at * 2 + core, rows_at * 2 + 1 - core])
    meta_tail = jnp.concatenate([planes * (2 * ys * span), planes, places])
    replica = me % replicas if replicas > 1 else jnp.zeros((), jnp.int32)

    def meta_of(s):
        return jnp.concatenate([jnp.stack([lengths[s], replica, me]), meta_tail]).astype(jnp.int32)

    metas = [meta_of(s) for s in range(seqs)]

    fronts, recvs = [], []
    for s in range(seqs):
        near, far = gather_blocks(hidden[s], ep)
        made = front(metas[s], near, far, head_w, gain_one, cos, sin, replicas)
        recv = lax.all_to_all(made[0], "ep", split_axis=0, concat_axis=0, tiled=True)
        if replicas > 1:
            recv = recv.reshape((heads, replicas) + recv.shape[1:]).sum(axis=1).astype(bf16)
        fronts.append(made)
        recvs.append(recv)

    middles, carried, reduced = [], None, []
    for s in range(seqs):
        mid = middle(recvs[s], hidden[s], wo, gain_two, wr, chosen[s], sent[s])
        middles.append(mid)
        near, far = gather_blocks(mid[1], ep)
        out = experts(metas[s], near, far, upstream, w_gate_up[0], w_down[0], s, carried)
        carried = out[2:]
        reduced.append(reduce_blocks(out[0], out[1], ep))
    moe_all, gate_up_grad, down_grad = carried
    moe_own = lax.psum_scatter(moe_all, "ep", scatter_dimension=0, tiled=True)[0]

    turns, parts, dqkvs = [], [], []
    for s in range(seqs):
        here = jnp.stack([lengths[s], me * span]).astype(jnp.int32)
        res, pay, mixed, gates = middles[s]
        made = turn(here, reduced[s], res, pay, out_grad[s], gates, sent[s], wr, gain_two, wo)
        turns.append(made)
        grads = made[2]
        if replicas > 1:
            grads = jnp.repeat(grads, replicas, axis=0)
        grads = lax.all_to_all(grads, "ep", split_axis=0, concat_axis=0, tiled=True)
        _, _, qk, v, qkt, stat = fronts[s]
        near, far, dqkv = back(
            metas[s], grads, qk, v, qkt, stat, head_w, cos, sin, (ys, zs, span, width), replicas
        )
        dqkvs.append(dqkv)
        parts.append(reduce_blocks(near, far, ep))

    input_grad = finish(hidden, gain_one, [m[0] for m in turns], parts)

    gate_up_low = gate_up_grad.astype(bf16)
    down_low = down_grad.astype(bf16)
    gu_total = gate_up_low.astype(f32)
    d_total = down_low.astype(f32)
    for d in range(1, dp):
        ring = [(i, (i + d) % dp) for i in range(dp)]
        gu_total = gu_total + lax.ppermute(gate_up_low, "dp", ring).astype(f32)
        d_total = d_total + lax.ppermute(down_low, "dp", ring).astype(f32)

    mixed_all = jnp.concatenate([m[2] for m in middles])
    branch_all = jnp.concatenate([m[1] for m in turns])
    normed_two = jnp.concatenate([m[1][:, 0:width] for m in middles])
    logit_grad = jnp.concatenate([m[3] for m in turns])
    out_w_grad = dot_tn(mixed_all, branch_all)
    logit_high = logit_grad.astype(bf16)
    logit_low = (logit_grad - logit_high.astype(f32)).astype(bf16)
    router_grad = dot_tn(normed_two, logit_high) + dot_tn(normed_two, logit_low)
    gain_two_grad = sum(m[4] for m in turns).reshape(width, 1)
    late = jnp.concatenate([out_w_grad, router_grad[:, 0:expert_count], gain_two_grad], axis=1)
    late = jnp.pad(late, ((0, 0), (0, -late.shape[1] % LANES)))
    late = lax.psum_scatter(late, ("dp", "ep"), scatter_dimension=0, tiled=True)

    head_grad = sum(dot_tn(fronts[s][1], dqkvs[s]) for s in range(seqs))
    head_grad = head_grad.reshape(dp * ep, own_rows, PACK).astype(bf16)
    head_grad = lax.all_to_all(head_grad, ("dp", "ep"), split_axis=0, concat_axis=0, tiled=True)
    head_grad = head_grad.astype(f32).reshape(dp, heads, replicas, own_rows, PACK).sum(axis=(0, 2))

    def rows_of(part, count):
        part = part.reshape(count, heads // count, own_rows, HD).sum(axis=1)
        return part.transpose(1, 0, 2).reshape(own_rows, count * HD)

    query_w_grad = rows_of(head_grad[..., 0:HD], heads)
    key_w_grad = rows_of(head_grad[..., HD : 2 * HD], kv_heads)
    value_w_grad = rows_of(head_grad[..., 2 * HD : 3 * HD], kv_heads)
    gain_one_grad = (
        jnp.sum(query_w_grad * query_weight_matrix.astype(f32), axis=1)
        + jnp.sum(key_w_grad * key_weight_matrix.astype(f32), axis=1)
        + jnp.sum(value_w_grad * value_weight_matrix.astype(f32), axis=1)
    ) / attn_gain.astype(f32)

    residual = jnp.stack([m[0] for m in middles])
    output = jnp.where(is_valid[..., None], residual + moe_own.astype(f32), 0.0).astype(bf16)
    model = out_w_grad.shape[1]
    return (
        output,
        input_grad,
        gain_one_grad,
        query_w_grad,
        key_w_grad,
        value_w_grad,
        late[:, 0:model],
        late[:, model + expert_count],
        late[:, model : model + expert_count],
        gu_total[None],
        d_total[None],
    )


def solution(mesh):
    return jax.shard_map(
        body,
        mesh=mesh,
        in_specs=(
            P("dp", "ep", None),
            P("dp"),
            P("dp", "ep", None),
            P("dp", "ep", None),
            P(("dp", "ep")),
            P(("dp", "ep"), None),
            P(("dp", "ep"), None),
            P(("dp", "ep"), None),
            P(("dp", "ep"), None),
            P(("dp", "ep")),
            P(("dp", "ep"), None),
            P("ep", None, None),
            P("ep", None, None),
            P("dp", "ep", None),
        ),
        out_specs=(
            P("dp", "ep", None),
            P("dp", "ep", None),
            P(("dp", "ep")),
            P(("dp", "ep"), None),
            P(("dp", "ep"), None),
            P(("dp", "ep"), None),
            P(("dp", "ep"), None),
            P(("dp", "ep")),
            P(("dp", "ep"), None),
            P("ep", None, None),
            P("ep", None, None),
        ),
        check_vma=False,
    )
```

```python
import functools

import jax
import jax.numpy as jnp
from jax import lax
from jax.experimental import pallas as pl
from jax.experimental.pallas import tpu as pltpu
from jax.sharding import PartitionSpec as P

HD = 64
LANES = 128
SLAB = 256
PACK = 256
LOW = 32
SLOT = 64
eps = 1e-05
theta_base = 10000.0
f32 = jnp.float32
bf16 = jnp.bfloat16
VMEM_LIMIT = 56 * 1024 * 1024


def dot(a, b):
    return lax.dot_general(a, b, (((1,), (0,)), ((), ())), preferred_element_type=f32)


def dot_nt(a, b):
    return lax.dot_general(a, b, (((1,), (1,)), ((), ())), preferred_element_type=f32)


def dot_tn(a, b):
    return lax.dot_general(a, b, (((0,), (0,)), ((), ())), preferred_element_type=f32)


def lanes_of(rows, width=LANES):
    return lax.broadcasted_iota(jnp.int32, (rows, width), 1)


def half_swap(x):
    lane = lanes_of(x.shape[0])
    return jnp.where(lane % HD < HD // 2, pltpu.roll(x, LANES - HD // 2, 1), pltpu.roll(x, HD // 2, 1))


def ep_shape(ep):
    zs = 4 if ep % 8 == 0 else 1
    return zs, ep // (2 * zs), 2


def fetch_from(ep, dz=0, dy=0, dc=0):
    zs, ys, cs = ep_shape(ep)
    pairs = []
    for z in range(zs):
        for y in range(ys):
            for c in range(cs):
                src = (((z + dz) % zs) * ys + (y + dy) % ys) * cs + (c + dc) % cs
                pairs.append((src, (z * ys + y) * cs + c))
    return pairs


def send_to(ep, **offset):
    return [(dst, src) for src, dst in fetch_from(ep, **offset)]


def phase(*values):
    return lax.optimization_barrier(values)


def phase_tree(*values):
    flat, tree = jax.tree.flatten(values)
    return jax.tree.unflatten(tree, phase(*flat))


def add_low(*parts):
    total = parts[0].astype(f32)
    for part in parts[1:]:
        total = total + part.astype(f32)
    return total.astype(bf16)


def project_kernel(place, carry, meta, *refs):
    blocks = refs[:place]
    w_ref, gain_ref, cos_ref, sin_ref = refs[place : place + 4]
    normed_ref, qkv_ref = refs[-2:]
    rows, _ = blocks[0].shape
    span = cos_ref.shape[0] // place
    seqs = rows // span
    lane = lanes_of(rows)
    for j in range(place):
        x = blocks[j][...].astype(f32)
        scale = lax.rsqrt(jnp.mean(x * x, axis=-1, keepdims=True) + eps)
        normed = (x * scale * gain_ref[...]).astype(bf16)
        normed_ref[0, j] = normed
        raw = dot(normed, w_ref[...])
        at = pl.ds(pl.multiple_of(meta[1 + j] * span, 32), span)
        cos = jnp.concatenate([cos_ref[at, :]] * seqs, axis=0)
        sin = jnp.concatenate([sin_ref[at, :]] * seqs, axis=0)
        both = raw[:, 0:LANES]
        both = (both * cos + half_swap(both) * sin).astype(bf16).astype(f32)
        both = jnp.where(lane < HD, both * HD ** (-0.5), both)
        qkv_ref[0, j, :, 0:LANES] = both.astype(bf16)
        qkv_ref[0, j, :, LANES:PACK] = jnp.where(lane < HD, raw[:, LANES:PACK], 0.0).astype(bf16)


def project(meta, blocks, w, gain, cos, sin, zs, dz, carried):
    rows, width = blocks[0].shape
    place = len(blocks)
    span = cos.shape[0] // (zs * place)

    def whole(a):
        return pl.BlockSpec(a.shape, lambda i, m: (0,) * a.ndim)

    table = pl.BlockSpec((place * span, LANES), lambda i, m: (lax.rem(m[0] + dz, zs), 0))
    args = list(blocks) + [w, gain, cos, sin]
    in_specs = [whole(a) for a in blocks] + [whole(w), whole(gain), table, table]
    aliases = {}
    if carried is not None:
        aliases = {1 + len(args): 0, 2 + len(args): 1}
        args += list(carried)
        in_specs += [pl.BlockSpec(memory_space=pl.ANY)] * 2
    return pl.pallas_call(
        functools.partial(project_kernel, place, carried is not None),
        grid_spec=pltpu.PrefetchScalarGridSpec(
            num_scalar_prefetch=1,
            grid=(1,),
            in_specs=in_specs,
            out_specs=(
                pl.BlockSpec((1, place, rows, width), lambda i, m: (dz, 0, 0, 0)),
                pl.BlockSpec((1, place, rows, PACK), lambda i, m: (dz, 0, 0, 0)),
            ),
        ),
        out_shape=(
            jax.ShapeDtypeStruct((zs, place, rows, width), bf16),
            jax.ShapeDtypeStruct((zs, place, rows, PACK), bf16),
        ),
        input_output_aliases=aliases,
        compiler_params=pltpu.CompilerParams(vmem_limit_bytes=VMEM_LIMIT),
        cost_estimate=pl.CostEstimate(
            flops=2 * place * rows * width * PACK,
            bytes_accessed=4 * place * rows * width,
            transcendentals=0,
        ),
        name="project_in",
    )(meta, *args)


def attend_kernel(
    replicas,
    meta,
    qkv_ref,
    out_ref,
    qk_ref,
    v_ref,
    qkt_ref,
    stat_ref,
    vt_ref,
    wide_ref,
):
    zs, place, rows, _ = qkv_ref.shape
    total = qk_ref.shape[1]
    span = total // (zs * place)
    s = pl.program_id(0)
    seqs = rows // span
    length = meta[s]
    source = pl.ds(pl.multiple_of(s * span, 32), span)
    for d in range(zs):
        for j in range(place):
            at = pl.multiple_of((meta[seqs + 1 + d] * place + meta[seqs + 1 + zs + j]) * span, 32)
            qk_ref[0, pl.ds(at, span), :] = qkv_ref[d, j, source, 0:LANES]
            v_ref[0, pl.ds(at, span), :] = qkv_ref[d, j, source, LANES:PACK]
    for lo in range(0, total, SLAB):
        at = slice(lo, lo + SLAB)
        qkt_ref[0, :, at] = qk_ref[0, at, :].astype(f32).T.astype(bf16)
        vt_ref[:, at] = v_ref[0, at, :].astype(f32).T.astype(bf16)

    key_row = lax.broadcasted_iota(jnp.int32, (SLAB, SLAB), 0)
    query_col = lax.broadcasted_iota(jnp.int32, (SLAB, SLAB), 1)
    for i, lo in enumerate(range(0, total, SLAB)):
        hi = lo + SLAB
        mine = lo < length
        if replicas > 1:
            mine = mine & (meta[seqs] == i % replicas)

        @pl.when(mine)
        def _():
            qt = qkt_ref[0, 0:HD, lo:hi]
            diag = dot(qk_ref[0, lo:hi, HD:LANES], qt)
            diag = jnp.where(key_row <= query_col, diag, -jnp.inf)
            top = jnp.max(diag, axis=0, keepdims=True)
            if lo:
                full = dot(qk_ref[0, 0:lo, HD:LANES], qt)
                top = jnp.maximum(top, jnp.max(full, axis=0, keepdims=True))
            p_diag = jnp.exp(diag - top)
            row_total = jnp.sum(p_diag, axis=0, keepdims=True)
            out = dot(vt_ref[:, lo:hi], p_diag.astype(bf16))
            if lo:
                p_full = jnp.exp(full - top)
                row_total = row_total + jnp.sum(p_full, axis=0, keepdims=True)
                out = out + dot(vt_ref[:, 0:lo], p_full.astype(bf16))
            out = out[0:HD] / row_total
            stat_ref[0, 0:HD, lo:hi] = out
            stat_ref[0, HD : HD + 8, lo:hi] = jnp.broadcast_to(top + jnp.log(row_total), (8, SLAB))
            wide_ref[lo:hi, :] = jnp.concatenate([out, out], axis=0).T

        @pl.when(jnp.logical_not(mine))
        def _():
            stat_ref[0, :, lo:hi] = jnp.zeros((HD + 8, SLAB), f32)
            wide_ref[lo:hi, :] = jnp.zeros((SLAB, LANES), f32)

    half = span // 2
    for e in range(total // span):
        upper = wide_ref[e * span : e * span + half, :]
        lower = wide_ref[e * span + half : (e + 1) * span, :]
        out_ref[e] = jnp.where(lanes_of(half) < HD, upper, lower).astype(bf16)


def attend(meta, qkv, seqs, replicas):
    zs, place, rows, _ = qkv.shape
    span = rows // seqs
    total = zs * place * span
    return pl.pallas_call(
        functools.partial(attend_kernel, replicas),
        grid=(seqs,),
        out_shape=(
            jax.ShapeDtypeStruct((total // span, seqs * (span // 2), LANES), bf16),
            jax.ShapeDtypeStruct((seqs, total, LANES), bf16),
            jax.ShapeDtypeStruct((seqs, total, LANES), bf16),
            jax.ShapeDtypeStruct((seqs, LANES, total), bf16),
            jax.ShapeDtypeStruct((seqs, HD + 8, total), f32),
        ),
        in_specs=[
            pl.BlockSpec(memory_space=pltpu.SMEM),
            pl.BlockSpec(qkv.shape, lambda s: (0, 0, 0, 0)),
        ],
        out_specs=(
            pl.BlockSpec((total // span, span // 2, LANES), lambda s: (0, s, 0)),
            pl.BlockSpec((1, total, LANES), lambda s: (s, 0, 0)),
            pl.BlockSpec((1, total, LANES), lambda s: (s, 0, 0)),
            pl.BlockSpec((1, LANES, total), lambda s: (s, 0, 0)),
            pl.BlockSpec((1, HD + 8, total), lambda s: (s, 0, 0)),
        ),
        scratch_shapes=[pltpu.VMEM((LANES, total), bf16), pltpu.VMEM((total, LANES), f32)],
        compiler_params=pltpu.CompilerParams(vmem_limit_bytes=VMEM_LIMIT),
        cost_estimate=pl.CostEstimate(
            flops=4 * seqs * total * total * LANES,
            bytes_accessed=4 * seqs * total * PACK,
            transcendentals=seqs * total * total // 2,
        ),
        name="attend_forward",
    )(meta, qkv)


def middle_kernel(
    seqs,
    recv_ref,
    hid_ref,
    wo_ref,
    gain_ref,
    wr_ref,
    chosen_ref,
    code_ref,
    res_ref,
    pay_ref,
    mixed_ref,
    gate_ref,
):
    heads, half_rows, _ = recv_ref.shape
    width = hid_ref.shape[1]
    half = half_rows // seqs
    low = lanes_of(half_rows) < HD
    uppers, lowers = [], []
    for j in range(heads // 2):
        a = recv_ref[2 * j].astype(f32)
        b = recv_ref[2 * j + 1].astype(f32)
        uppers.append(jnp.where(low, a, pltpu.roll(b, HD, 1)).astype(bf16))
        lowers.append(jnp.where(low, pltpu.roll(a, HD, 1), b).astype(bf16))
    upper = jnp.concatenate(uppers, axis=1)
    lower = jnp.concatenate(lowers, axis=1)
    pieces = []
    for s in range(seqs):
        pieces += [upper[s * half : (s + 1) * half], lower[s * half : (s + 1) * half]]
    mixed = jnp.concatenate(pieces, axis=0)
    mixed_ref[...] = mixed
    res = hid_ref[...].astype(f32) + dot(mixed, wo_ref[...])
    res_ref[...] = res
    scale = lax.rsqrt(jnp.mean(res * res, axis=-1, keepdims=True) + eps)
    normed = (res * scale * gain_ref[...]).astype(bf16)
    logits = dot(normed, wr_ref[...])
    logits = jnp.where(chosen_ref[...] > 0, logits, -jnp.inf)
    powers = jnp.exp(logits - jnp.max(logits, axis=-1, keepdims=True))
    gates = powers / jnp.sum(powers, axis=-1, keepdims=True)
    gate_ref[...] = gates
    code = code_ref[...]
    used = jnp.where(code > 0, gates, 0.0)
    upper = used.astype(bf16).astype(f32)
    pay_ref[:, 0:width] = normed
    pay_ref[:, width:] = (
        upper + pltpu.roll(used - upper, LOW, 1) + pltpu.roll(code, SLOT, 1)
    ).astype(bf16)


def middle(seqs, recv, hid, wo, gain, wr, chosen, code):
    rows, width = hid.shape
    vmem = pl.BlockSpec(memory_space=pltpu.VMEM)
    return pl.pallas_call(
        functools.partial(middle_kernel, seqs),
        out_shape=(
            jax.ShapeDtypeStruct((rows, width), f32),
            jax.ShapeDtypeStruct((rows, width + LANES), bf16),
            jax.ShapeDtypeStruct((rows, width), bf16),
            jax.ShapeDtypeStruct((rows, LANES), f32),
        ),
        in_specs=[vmem] * 7,
        out_specs=(vmem,) * 4,
        compiler_params=pltpu.CompilerParams(vmem_limit_bytes=VMEM_LIMIT),
        cost_estimate=pl.CostEstimate(
            flops=4 * rows * width * width, bytes_accessed=4 * width * width, transcendentals=0
        ),
        name="project_out",
    )(recv, hid, wo, gain, wr, chosen, code)


def expert_kernel(place, cap, zs, dz, first, meta, *refs):
    pay_in = refs[0:place]
    up_in = refs[place]
    wgu_in, wd_in = refs[place + 1 : place + 3]
    rest = refs[place + 3 + (0 if first else 6) :]
    near_out, far_out, mnear_out, mfar_out, x_out, pg_out, act_out, both_out = rest[:8]
    pay, up, wgu, wd, back_s, moe_s, x_s, pg_s, act_s, both_s, in_sem, out_sem = rest[8:]
    rows, wide = pay_in[0].shape
    width = wide - LANES
    units = wd.shape[0]
    halves = place // 2
    expert = meta[0]
    plane = lax.rem(meta[1] + dz, zs)
    loads = {}
    order = []
    for j in range(place):
        loads["p", j] = pltpu.make_async_copy(pay_in[j], pay.at[j], in_sem.at[2 * j])
        loads["u", j] = pltpu.make_async_copy(
            up_in.at[plane * place + meta[2 + j]], up.at[j], in_sem.at[2 * j + 1]
        )
    loads["gu"] = pltpu.make_async_copy(wgu_in, wgu, in_sem.at[2 * place])
    loads["d"] = pltpu.make_async_copy(wd_in, wd, in_sem.at[2 * place + 1])
    order = [("p", j) for j in range(halves)] + ["gu", "d"]
    order += [("u", j) for j in range(halves)]
    order += [("p", j) for j in range(halves, place)] + [("u", j) for j in range(halves, place)]
    for key in order:
        loads[key].start()
    stores = []

    def store(src, dst):
        copy = pltpu.make_async_copy(src, dst, out_sem.at[len(stores)])
        copy.start()
        stores.append(copy)

    lane = lanes_of(rows)
    slot_row = lax.broadcasted_iota(jnp.int32, (cap, rows), 0)
    slot_col = lax.broadcasted_iota(jnp.int32, (rows, cap), 1)
    code_row = lax.broadcasted_iota(jnp.int32, (LANES, rows), 0)
    cap_lane = lanes_of(cap)
    for h in range(2):
        mine = range(h * halves, (h + 1) * halves)
        for j in mine:
            loads["p", j].wait()
        outs_of, xs, gates = [], [], []
        into = []
        for j in mine:
            codes = pay[j, :, width:].astype(f32)
            column = jnp.sum(jnp.where(lane == expert + SLOT, codes, 0.0), axis=1, keepdims=True)
            line = jnp.sum(jnp.where(code_row == expert + SLOT, codes.T, 0.0), axis=0, keepdims=True)
            into.append(jnp.where(line.astype(jnp.int32) == slot_row + 1, 1.0, 0.0).astype(bf16))
            outs_of.append(
                jnp.where(column.astype(jnp.int32) == slot_col + 1, 1.0, 0.0).astype(bf16)
            )
            taken = dot(into[-1], pay[j])
            xs.append(taken[:, 0:width].astype(bf16))
            hits = (cap_lane == expert) | (cap_lane == expert + LOW)
            gates.append(jnp.sum(jnp.where(hits, taken[:, width:], 0.0), axis=1, keepdims=True))
        x = jnp.concatenate(xs, axis=0)
        gate_prob = jnp.concatenate(gates, axis=0)
        if h == 0:
            loads["gu"].wait()
        gate_up = dot(x, wgu[...])
        gate = gate_up[:, 0:units]
        high = gate_up[:, units:]
        sig = jax.nn.sigmoid(gate)
        silu = gate * sig
        act = (silu * high).astype(bf16)
        if h == 0:
            loads["d"].wait()
        made = dot(act, wd[...]).astype(bf16).astype(f32)
        for j in mine:
            loads["u", j].wait()
        upstream = jnp.concatenate([dot(into[k], up[j]) for k, j in enumerate(mine)], axis=0)
        gate_grad = jnp.sum(made * upstream, axis=-1, keepdims=True)
        moe = (made * gate_prob).astype(bf16)
        pair_grad = (upstream * gate_prob).astype(bf16)
        act_grad = dot_nt(pair_grad, wd[...])
        both = jnp.concatenate(
            [act_grad * high * (sig * (1.0 + gate * (1.0 - sig))), act_grad * silu], axis=1
        ).astype(bf16)
        back = dot_nt(both, wgu[...]).astype(bf16)
        upper = gate_grad.astype(bf16).astype(f32)
        wide_lane = lanes_of(halves * cap)
        extra = jnp.where(wide_lane == expert, upper, 0.0)
        extra = jnp.where(wide_lane == expert + LOW, gate_grad - upper, extra).astype(bf16)
        for k, j in enumerate(mine):
            part = slice(k * cap, (k + 1) * cap)
            back_s[j, :, 0:width] = dot(outs_of[k], back[part]).astype(bf16)
            back_s[j, :, width:] = dot(outs_of[k], extra[part]).astype(bf16)
        store(back_s.at[pl.ds(h * halves, halves)], near_out if h == 0 else far_out)
        for k, j in enumerate(mine):
            part = slice(k * cap, (k + 1) * cap)
            moe_s[j] = dot(outs_of[k], moe[part]).astype(bf16)
        store(moe_s.at[pl.ds(h * halves, halves)], (mnear_out if h == 0 else mfar_out).at[dz])
        own = pl.ds(h * halves * cap, halves * cap)
        for value, buf, out in ((x, x_s, x_out), (pair_grad, pg_s, pg_out), (act, act_s, act_out), (both, both_s, both_out)):
            buf[own, :] = value
            store(buf.at[own], out.at[dz, own])
    for copy in stores:
        copy.wait()


def experts(meta, pays, upstream, wgu, wd, cap, zs, dz, carried):
    place = len(pays)
    rows, wide = pays[0].shape
    width = wide - LANES
    units = wd.shape[0]
    first = carried is None
    anyspace = pl.BlockSpec(memory_space=pl.ANY)
    args = list(pays) + [upstream, wgu, wd]
    aliases = {}
    if not first:
        aliases = {1 + len(args) + k: 2 + k for k in range(6)}
        args += list(carried)
    half = jax.ShapeDtypeStruct((place // 2, rows, wide), bf16)
    slots = place * cap
    return pl.pallas_call(
        functools.partial(expert_kernel, place, cap, zs, dz, first),
        out_shape=(
            half,
            half,
            jax.ShapeDtypeStruct((zs, place // 2, rows, width), bf16),
            jax.ShapeDtypeStruct((zs, place // 2, rows, width), bf16),
            jax.ShapeDtypeStruct((zs, slots, width), bf16),
            jax.ShapeDtypeStruct((zs, slots, width), bf16),
            jax.ShapeDtypeStruct((zs, slots, units), bf16),
            jax.ShapeDtypeStruct((zs, slots, 2 * units), bf16),
        ),
        in_specs=[pl.BlockSpec(memory_space=pltpu.SMEM)] + [anyspace] * len(args),
        out_specs=(anyspace,) * 8,
        scratch_shapes=[
            pltpu.VMEM((place, rows, wide), bf16),
            pltpu.VMEM((place, rows, width), bf16),
            pltpu.VMEM(wgu.shape, bf16),
            pltpu.VMEM(wd.shape, bf16),
            pltpu.VMEM((place, rows, wide), bf16),
            pltpu.VMEM((place, rows, width), bf16),
            pltpu.VMEM((slots, width), bf16),
            pltpu.VMEM((slots, width), bf16),
            pltpu.VMEM((slots, units), bf16),
            pltpu.VMEM((slots, 2 * units), bf16),
            pltpu.SemaphoreType.DMA((2 * place + 2,)),
            pltpu.SemaphoreType.DMA((12,)),
        ],
        input_output_aliases=aliases,
        compiler_params=pltpu.CompilerParams(vmem_limit_bytes=VMEM_LIMIT),
        cost_estimate=pl.CostEstimate(
            flops=16 * slots * width * units, bytes_accessed=12 * slots * width, transcendentals=0
        ),
        name="experts",
    )(meta, *args)


def turn_kernel(nparts, seqs, meta, *refs):
    parts = refs[:nparts]
    (
        res_ref,
        up_ref,
        gate_ref,
        code_ref,
        wr_ref,
        gain_ref,
        wo_ref,
        resgrad_ref,
        branch_ref,
        out_ref,
        logit_ref,
        gaingrad_ref,
    ) = refs[nparts:]
    rows, width = res_ref.shape
    span = rows // seqs
    total = parts[0][...].astype(f32)
    for part in parts[1:]:
        total = total + part[...].astype(f32)
    extra = total[:, width:]
    gate_grad = jnp.where(code_ref[...] > 0, extra + pltpu.roll(extra, LANES - LOW, 1), 0.0)
    gates = gate_ref[...]
    logit_grad = gates * (gate_grad - jnp.sum(gates * gate_grad, axis=-1, keepdims=True))
    logit_ref[...] = logit_grad
    normed_grad = total[:, 0:width] + lax.dot_general(
        logit_grad,
        wr_ref[...].astype(f32),
        (((1,), (1,)), ((), ())),
        preferred_element_type=f32,
        precision=lax.Precision.HIGHEST,
    )
    res = res_ref[...]
    scale = lax.rsqrt(jnp.mean(res * res, axis=-1, keepdims=True) + eps)
    gaingrad_ref[...] = jnp.sum(normed_grad * (res * scale), axis=0, keepdims=True)
    scaled = normed_grad * gain_ref[...]
    row = meta[seqs] + lax.broadcasted_iota(jnp.int32, (span, 1), 0)
    valid = jnp.concatenate([(row < meta[s]).astype(f32) for s in range(seqs)], axis=0)
    upstream = jnp.where(valid > 0, up_ref[...].astype(f32), 0.0)
    centre = jnp.mean(scaled * res, axis=-1, keepdims=True)
    res_grad = upstream + scaled * scale - res * (scale * scale * scale * centre)
    resgrad_ref[...] = res_grad
    branch = res_grad.astype(bf16)
    branch_ref[...] = branch
    mixed = dot_nt(branch, wo_ref[...]).astype(bf16).astype(f32)
    half = span // 2
    low = lanes_of(half) < HD
    for s in range(seqs):
        at = slice(s * half, (s + 1) * half)
        for j in range(out_ref.shape[0] // 2):
            cols = slice(j * LANES, (j + 1) * LANES)
            upper = mixed[s * span : s * span + half, cols]
            lower = mixed[s * span + half : (s + 1) * span, cols]
            out_ref[2 * j, at] = jnp.where(low, upper, pltpu.roll(lower, HD, 1)).astype(bf16)
            out_ref[2 * j + 1, at] = jnp.where(low, pltpu.roll(upper, HD, 1), lower).astype(bf16)


def turn(meta, seqs, parts, res, up, gates, code, wr, gain, wo):
    rows, width = res.shape
    heads = wo.shape[0] // HD
    vmem = pl.BlockSpec(memory_space=pltpu.VMEM)
    return pl.pallas_call(
        functools.partial(turn_kernel, len(parts), seqs),
        out_shape=(
            jax.ShapeDtypeStruct((rows, width), f32),
            jax.ShapeDtypeStruct((rows, width), bf16),
            jax.ShapeDtypeStruct((heads, rows // 2, LANES), bf16),
            jax.ShapeDtypeStruct((rows, LANES), f32),
            jax.ShapeDtypeStruct((1, width), f32),
        ),
        in_specs=[pl.BlockSpec(memory_space=pltpu.SMEM)] + [vmem] * (len(parts) + 7),
        out_specs=(vmem,) * 5,
        compiler_params=pltpu.CompilerParams(vmem_limit_bytes=VMEM_LIMIT),
        cost_estimate=pl.CostEstimate(
            flops=4 * rows * width * width, bytes_accessed=4 * width * width, transcendentals=0
        ),
        name="turn_back",
    )(meta, *parts, res, up, gates, code, wr, gain, wo)


def back_kernel(
    replicas,
    meta,
    grad_ref,
    qk_ref,
    v_ref,
    qkt_ref,
    stat_ref,
    cos_ref,
    sin_ref,
    out_ref,
    do_ref,
    dk_ref,
    dv_ref,
    dqt_ref,
):
    zs, place, rows, _ = out_ref.shape
    total = qk_ref.shape[1]
    span = total // (zs * place)
    seqs = rows // span
    s = pl.program_id(0)
    length = meta[s]
    half = span // 2
    for e in range(total // span):
        chunk = grad_ref[e].astype(f32)
        do_ref[e * span : e * span + half, :] = chunk
        do_ref[e * span + half : (e + 1) * span, :] = pltpu.roll(chunk, HD, 1)
    dk_ref[...] = jnp.zeros_like(dk_ref)
    dv_ref[...] = jnp.zeros_like(dv_ref)
    key_row = lax.broadcasted_iota(jnp.int32, (SLAB, SLAB), 0)
    query_col = lax.broadcasted_iota(jnp.int32, (SLAB, SLAB), 1)
    for i, lo in enumerate(range(0, total, SLAB)):
        hi = lo + SLAB
        mine = lo < length
        if replicas > 1:
            mine = mine & (meta[seqs] == i % replicas)

        @pl.when(mine)
        def _():
            qt = qkt_ref[0, 0:HD, lo:hi]
            qk = qk_ref[0, lo:hi, :]
            grad = do_ref[lo:hi, :]
            grad_low = grad.astype(bf16)
            grad_t = grad.T[0:HD]
            delta = jnp.sum(grad_t * stat_ref[0, 0:HD, lo:hi], axis=0, keepdims=True)
            grad_t = grad_t.astype(bf16)
            log_total = stat_ref[0, HD : HD + 1, lo:hi]

            def piece(start, stop, masked):
                scores = dot(qk_ref[0, start:stop, HD:LANES], qt)
                probs = jnp.exp(scores - log_total)
                if masked:
                    probs = jnp.where(key_row <= query_col, probs, 0.0)
                prob_grad = dot(v_ref[0, start:stop, 0:HD], grad_t)
                score_grad = (probs * (prob_grad - delta)).astype(bf16)
                dv_ref[start:stop, :] += dot(probs.astype(bf16), grad_low)
                dk_ref[start:stop, :] += dot(score_grad, qk)
                return dot(qkt_ref[0, :, start:stop], score_grad)

            moved = piece(lo, hi, True)
            if lo:
                moved = moved + piece(0, lo, False)
            dqt_ref[:, lo:hi] = moved

        @pl.when(jnp.logical_not(mine))
        def _():
            dqt_ref[:, lo:hi] = jnp.zeros((LANES, SLAB), f32)

    low = lanes_of(SLAB) < HD
    for lo in range(0, total, SLAB):
        at = slice(lo, lo + SLAB)
        both = jnp.where(low, dk_ref[at, :], dqt_ref[:, at].T * HD ** (-0.5))
        both = pltpu.roll(both, HD, 1)
        dk_ref[at, :] = both * cos_ref[at, :] - half_swap(both) * sin_ref[at, :]
        dv_ref[at, :] = jnp.where(low, dv_ref[at, :], 0.0)
    dest = pl.ds(pl.multiple_of(s * span, 32), span)
    for d in range(zs):
        for j in range(place):
            at = pl.multiple_of((meta[seqs + 1 + d] * place + meta[seqs + 1 + zs + j]) * span, 32)
            out_ref[d, j, dest, 0:LANES] = dk_ref[pl.ds(at, span), :].astype(bf16)
            out_ref[d, j, dest, LANES:PACK] = dv_ref[pl.ds(at, span), :].astype(bf16)


def back(meta, grads, qk, v, qkt, stat, cos, sin, shape, seqs, replicas):
    total = qk.shape[1]
    span = total // grads.shape[0]
    return pl.pallas_call(
        functools.partial(back_kernel, replicas),
        grid=(seqs,),
        out_shape=jax.ShapeDtypeStruct(shape, bf16),
        in_specs=[
            pl.BlockSpec(memory_space=pltpu.SMEM),
            pl.BlockSpec((total // span, span // 2, LANES), lambda s: (0, s, 0)),
            pl.BlockSpec((1, total, LANES), lambda s: (s, 0, 0)),
            pl.BlockSpec((1, total, LANES), lambda s: (s, 0, 0)),
            pl.BlockSpec((1, LANES, total), lambda s: (s, 0, 0)),
            pl.BlockSpec((1, HD + 8, total), lambda s: (s, 0, 0)),
            pl.BlockSpec((total, LANES), lambda s: (0, 0)),
            pl.BlockSpec((total, LANES), lambda s: (0, 0)),
        ],
        out_specs=pl.BlockSpec(shape, lambda s: (0, 0, 0, 0)),
        scratch_shapes=[
            pltpu.VMEM((total, LANES), f32),
            pltpu.VMEM((total, LANES), f32),
            pltpu.VMEM((total, LANES), f32),
            pltpu.VMEM((LANES, total), f32),
        ],
        compiler_params=pltpu.CompilerParams(vmem_limit_bytes=VMEM_LIMIT),
        cost_estimate=pl.CostEstimate(
            flops=10 * seqs * total * total * LANES,
            bytes_accessed=6 * seqs * total * PACK,
            transcendentals=seqs * total * total // 2,
        ),
        name="attend_backward",
    )(meta, grads, qk, v, qkt, stat, cos, sin)


def expert_grads_kernel(x_ref, both_ref, act_ref, pg_ref, *refs):
    outs, acc_ref = refs[:-1], refs[-1]
    width = x_ref.shape[2]

    @pl.when(pl.program_id(0) == 0)
    def _():
        acc_ref[...] = jnp.zeros_like(acc_ref)

    acc_ref[0:width, :] += dot_tn(x_ref[0], both_ref[0])
    acc_ref[width:, :] += dot_tn(act_ref[0], pg_ref[0])

    @pl.when(pl.program_id(0) == pl.num_programs(0) - 1)
    def _():
        for k, out_ref in enumerate(outs):
            rows = out_ref.shape[0]
            out_ref[...] = acc_ref[k * rows : (k + 1) * rows, :].astype(bf16)


def expert_grads(x, both, act, pg):
    zs, slots, width = x.shape
    units = act.shape[2]
    pieces = 4
    piece = (width + units) // pieces

    def block(a):
        return pl.BlockSpec((1,) + a.shape[1:], lambda i: (i, 0, 0))

    return pl.pallas_call(
        expert_grads_kernel,
        grid=(zs,),
        out_shape=(jax.ShapeDtypeStruct((piece, width), bf16),) * pieces,
        in_specs=[block(a) for a in (x, both, act, pg)],
        out_specs=(pl.BlockSpec((piece, width), lambda i: (0, 0)),) * pieces,
        scratch_shapes=[pltpu.VMEM((width + units, width), f32)],
        compiler_params=pltpu.CompilerParams(vmem_limit_bytes=VMEM_LIMIT),
        cost_estimate=pl.CostEstimate(
            flops=6 * zs * slots * width * units, bytes_accessed=8 * zs * slots * width, transcendentals=0
        ),
        name="expert_grads",
    )(x, both, act, pg)


def late_kernel(column, mixed_ref, branch_ref, pay_ref, logit_ref, gain_ref, out_ref):
    width = mixed_ref.shape[1]
    out_ref[:, 0:width] = dot_tn(mixed_ref[...], branch_ref[...]).astype(bf16)
    logit = logit_ref[...]
    high = logit.astype(bf16)
    low = (logit - high.astype(f32)).astype(bf16)
    normed = pay_ref[:, 0:width]
    side = dot_tn(normed, high) + dot_tn(normed, low)
    gain = jnp.broadcast_to(gain_ref[...], (LANES, width)).T
    out_ref[:, width:] = jnp.where(lanes_of(width) == column, gain, side).astype(bf16)


def late_grads(column, mixed, branch, pay, logit, gain):
    rows, width = mixed.shape
    vmem = pl.BlockSpec(memory_space=pltpu.VMEM)
    return pl.pallas_call(
        functools.partial(late_kernel, column),
        out_shape=jax.ShapeDtypeStruct((width, width + LANES), bf16),
        in_specs=[vmem] * 5,
        out_specs=vmem,
        compiler_params=pltpu.CompilerParams(vmem_limit_bytes=VMEM_LIMIT),
        cost_estimate=pl.CostEstimate(
            flops=2 * rows * width * width, bytes_accessed=4 * width * width, transcendentals=0
        ),
        name="late_grads",
    )(mixed, branch, pay, logit, gain)


def head_grads_kernel(dqkv_ref, normed_ref, out_ref, acc_ref):
    _, place, rows, pack = dqkv_ref.shape

    @pl.when(pl.program_id(0) == 0)
    def _():
        acc_ref[...] = jnp.zeros_like(acc_ref)

    for j in range(place):
        acc_ref[...] += dot_tn(dqkv_ref[0, j], normed_ref[0, j])

    @pl.when(pl.program_id(0) == pl.num_programs(0) - 1)
    def _():
        out_ref[...] = acc_ref[...].T.astype(bf16)


def head_grads(dqkv, normed):
    zs, place, rows, width = normed.shape
    return pl.pallas_call(
        head_grads_kernel,
        grid=(zs,),
        out_shape=jax.ShapeDtypeStruct((width, PACK), bf16),
        in_specs=[
            pl.BlockSpec((1, place, rows, PACK), lambda i: (i, 0, 0, 0)),
            pl.BlockSpec((1, place, rows, width), lambda i: (i, 0, 0, 0)),
        ],
        out_specs=pl.BlockSpec((width, PACK), lambda i: (0, 0)),
        scratch_shapes=[pltpu.VMEM((PACK, width), f32)],
        compiler_params=pltpu.CompilerParams(vmem_limit_bytes=VMEM_LIMIT),
        cost_estimate=pl.CostEstimate(
            flops=2 * zs * place * rows * width * PACK,
            bytes_accessed=2 * zs * place * rows * width,
            transcendentals=0,
        ),
        name="head_grads",
    )(dqkv, normed)


def finish_kernel(nparts, *refs):
    hid_ref, gain_ref, resgrad_ref = refs[0:3]
    parts = refs[3 : 3 + nparts]
    out_ref = refs[-1]
    total = parts[0][...].astype(f32)
    for part in parts[1:]:
        total = total + part[...].astype(f32)
    x = hid_ref[...].astype(f32)
    scale = lax.rsqrt(jnp.mean(x * x, axis=-1, keepdims=True) + eps)
    scaled = total * gain_ref[...]
    centre = jnp.mean(scaled * x, axis=-1, keepdims=True)
    out_ref[...] = resgrad_ref[...] + scaled * scale - x * (scale * scale * scale * centre)


def finish(hidden, gain, resgrad, parts):
    vmem = pl.BlockSpec(memory_space=pltpu.VMEM)
    return pl.pallas_call(
        functools.partial(finish_kernel, len(parts)),
        out_shape=jax.ShapeDtypeStruct(hidden.shape, f32),
        in_specs=[vmem] * (3 + len(parts)),
        out_specs=vmem,
        compiler_params=pltpu.CompilerParams(vmem_limit_bytes=VMEM_LIMIT),
        name="input_grad",
    )(hidden, gain, resgrad, *parts)


def body(
    hidden,
    lengths,
    expert_ids,
    pair_keep,
    attn_gain,
    query_weight_matrix,
    key_weight_matrix,
    value_weight_matrix,
    attention_output_weight,
    moe_gain,
    router_weight_matrix,
    w_gate_up,
    w_down,
    out_grad,
):
    seqs, span, width = hidden.shape
    rows = seqs * span
    top_k = expert_ids.shape[2]
    ep = lax.axis_size("ep")
    dp = lax.axis_size("dp")
    zs, ys, _ = ep_shape(ep)
    place = 2 * ys
    me = lax.axis_index("ep").astype(jnp.int32)
    expert_count = w_gate_up.shape[0] * ep
    capacity = max(2, rows * top_k // expert_count)
    cap = -(-capacity // 16) * 16
    heads = query_weight_matrix.shape[1] // HD
    kv_heads = key_weight_matrix.shape[1] // HD
    replicas = ep // heads
    total = span * ep
    own_rows = query_weight_matrix.shape[0]
    hidden = hidden.reshape(rows, width)
    out_grad = out_grad.reshape(rows, width)

    def per_head(weight, count):
        split = weight.reshape(own_rows, count, HD).transpose(1, 0, 2)
        return jnp.repeat(split, heads // count, axis=0)

    small = jnp.concatenate(
        [router_weight_matrix, attn_gain[:, None], moe_gain[:, None]], axis=1
    )
    small = jnp.pad(small, ((0, 0), (0, PACK - 3 * HD - small.shape[1])))
    packed = jnp.concatenate(
        [
            per_head(query_weight_matrix, heads),
            per_head(key_weight_matrix, kv_heads),
            per_head(value_weight_matrix, kv_heads),
            jnp.broadcast_to(small[None], (heads,) + small.shape),
        ],
        axis=2,
    )
    packed = jnp.repeat(packed, replicas, axis=0)
    packed = jnp.broadcast_to(packed[None], (dp,) + packed.shape).reshape(
        dp * ep, own_rows, PACK
    )
    packed = lax.all_to_all(packed, ("dp", "ep"), split_axis=0, concat_axis=0, tiled=True)
    head_w = packed.reshape(dp * ep * own_rows, PACK)
    at = 3 * HD
    wr = jnp.pad(head_w[:, at : at + expert_count], ((0, 0), (0, LANES - expert_count)))
    gains = head_w[:, at + expert_count : at + expert_count + 2].astype(f32)
    gain_one = gains[:, 0].reshape(1, width)
    gain_two = gains[:, 1].reshape(1, width)
    head_w = jnp.where(jnp.arange(PACK)[None, :] < at, head_w, jnp.zeros((), bf16))

    positions = me * span + jnp.arange(span, dtype=jnp.int32)
    is_valid = positions[None, :] < lengths[:, None]
    expert_range = jnp.arange(LANES, dtype=jnp.int32)
    hit = expert_ids[..., None] == expert_range
    chosen = jnp.any(hit, axis=2).reshape(rows, LANES).astype(f32)
    live = jnp.any(hit & (pair_keep[..., None] > 0), axis=2) & is_valid[..., None]
    live = live.reshape(rows, LANES).astype(bf16)
    earlier = jnp.arange(rows)[:, None] > jnp.arange(rows)[None, :]
    slot = jnp.dot(earlier.astype(bf16), live, preferred_element_type=f32)
    code = jnp.where((slot < capacity) & (live > 0), slot + 1.0, 0.0)

    rates = theta_base ** (-2.0 * jnp.arange(HD // 2, dtype=f32) / HD)
    angle = jnp.arange(total, dtype=jnp.int32).astype(f32)[:, None] * rates[None, :]
    cos = jnp.tile(jnp.cos(angle), (1, 4))
    sin = jnp.sin(angle)
    sin = jnp.concatenate([-sin, sin, -sin, sin], axis=1)
    core = me % 2
    col = (me // 2) % ys
    plane = me // place
    planes = (plane + jnp.arange(zs, dtype=jnp.int32)) % zs
    rows_at = (col + jnp.arange(ys, dtype=jnp.int32)) % ys
    places = jnp.concatenate([rows_at * 2 + core, rows_at * 2 + 1 - core])
    replica = me % replicas if replicas > 1 else jnp.zeros((), jnp.int32)
    attend_meta = jnp.concatenate([lengths, replica[None], planes, places]).astype(jnp.int32)
    expert_meta = jnp.concatenate([jnp.stack([me, plane]), places]).astype(jnp.int32)
    project_meta = expert_meta[1:]
    turn_meta = jnp.concatenate([lengths, (me * span)[None]]).astype(jnp.int32)

    order = list(range(zs))

    def move(x, sender=False, **offset):
        return lax.ppermute(x, "ep", (send_to if sender else fetch_from)(ep, **offset))

    def steps(t):
        n = len(order)
        return t < n - 1, t < n, 1 <= t <= n, 2 <= t < n + 2

    columns, near, far, carried, x = [hidden], {}, {}, None, hidden
    wo_part = [attention_output_weight]
    for t in range(len(order) + 2):
        on_z, on_y, on_core, on_work = steps(t)
        z_new = [move(columns[t], dz=1)] if on_z else []
        y_new = [move(columns[t], dy=k) for k in range(1, ys)] if on_y else []
        c_new = [move(block, dc=1) for block in near[t - 1]] if on_core else []
        if on_work:
            d = order[t - 2]
            carried = project(
                project_meta, near[t - 2] + far[t - 2], head_w, gain_one, cos, sin, zs, d, carried
            )
        block = wo_part[0]
        wo_new = []
        if t == zs - 1:
            wo_new = [move(block, dz=k) for k in range(1, zs)]
        elif t == zs:
            wo_new = [move(block, dy=k) for k in range(1, ys)]
        x, columns, near, far, z_new, y_new, c_new, carried, wo_part, wo_new = phase_tree(
            x, columns, near, far, z_new, y_new, c_new, carried, wo_part, wo_new
        )
        if wo_new:
            wo_part = [jnp.stack(wo_part + wo_new)]
        columns = columns + z_new
        if on_y:
            near[t] = [columns[t]] + y_new
        if on_core:
            far[t - 1] = c_new
        if t == len(order) - 1:
            upstream = lax.all_gather(phase(out_grad, columns[-1])[0], "ep", axis=0)
    wo_new = [
        lax.ppermute(wo_part[0], "dp", [((i + k) % dp, i) for i in range(dp)]) for k in range(1, dp)
    ]
    normed_all, qkv = carried
    made, qk, v, qkt, stat = attend(attend_meta, qkv, seqs, replicas)
    made, wo_new, wo_part = phase_tree(made, wo_new, wo_part)
    recv = lax.all_to_all(made, "ep", split_axis=0, concat_axis=0, tiled=True)
    wo_part = jnp.stack(wo_part + wo_new)
    wo_part = [jnp.stack([wo_part, move(wo_part, dc=1)])]
    line = jnp.arange(dp * ep, dtype=jnp.int32)
    away = (line % 2 - core) % 2
    away = away * dp + (line // ep - lax.axis_index("dp")) % dp
    away = away * ys + ((line // 2) % ys - col) % ys
    away = away * zs + ((line // place) % zs - plane) % zs
    wo = wo_part[0].reshape(dp * ep, own_rows, width)
    wo = jnp.take(wo, away, axis=0, mode="clip").reshape(heads * HD, width)
    if replicas > 1:
        recv = recv.reshape((heads, replicas) + recv.shape[1:]).sum(axis=1).astype(bf16)
    res, pay, mixed, gates = middle(seqs, recv, hidden, wo, gain_two, wr, chosen, code)

    count = zs
    columns, near, far, chips, totals = [pay], {}, {}, {}, {}
    outs, carried, extra, passed = {}, None, {}, None
    rings = [[(i, (i + d) % dp) for i in range(dp)] for d in range(1, dp)]
    cuts = ((1,), tuple(range(2, zs)), (0,))

    def hop(value):
        return lax.ppermute(value, "ep", fetch_from(ep, dz=1))

    def swap(piece):
        return [lax.ppermute(piece, "dp", ring) for ring in rings]

    for t in range(count + 5):
        on_z, on_y, on_core, on_work = steps(t)
        z_new = [move(columns[t], dz=1)] if on_z else []
        y_new = [move(columns[t], dy=k) for k in range(1, ys)] if on_y else []
        c_new = [move(block, dc=1) for block in near[t - 1]] if on_core else []
        rc, ry, rz = t - 3, t - 4, t - 5
        rc_new = [move(outs[rc][1], True, dc=1)] if 0 <= rc < count else []
        ry_new = [move(chips[ry][d], True, dy=d) for d in range(1, ys)] if 0 <= ry < count else []
        rz_new = []
        if 1 <= rz < count:
            rz_new = [hop(totals[rz] if rz == 1 else add_low(totals[rz], passed))]
        new = {}
        if on_work:
            d = order[t - 2]
            out = experts(
                expert_meta,
                near[t - 2] + far[t - 2],
                upstream,
                w_gate_up[0],
                w_down[0],
                cap,
                zs,
                d,
                carried,
            )
            outs[t - 2], carried = out[:2], out[2:]
        if t == count + 2:
            new["got"] = move(carried[1], True, dc=1)
            new["grads"] = list(expert_grads(carried[2], carried[5], carried[4], carried[3]))
        if t == count + 3:
            new["chip"] = [
                [
                    add_low(
                        jnp.stack([carried[0][k, d] for k in cut]),
                        jnp.stack([extra["got"][k, d] for k in cut]),
                    )
                    for cut in cuts
                    if cut
                ]
                for d in range(ys)
            ]
        if t >= count + 3:
            new["swap%d" % (t - count - 3)] = swap(extra["grads"][t - count - 3])
        if t == count + 4:
            new["first"] = [move(extra["chip"][d][0], True, dy=d) for d in range(1, ys)]
        state = (pay, columns, near, far, outs, chips, totals, carried, extra)
        state = phase_tree(state, z_new, y_new, c_new, rc_new, ry_new, rz_new, new)
        state, z_new, y_new, c_new, rc_new, ry_new, rz_new, new = state
        pay, columns, near, far, outs, chips, totals, carried, extra = state
        columns = columns + z_new
        if on_y:
            near[t] = [columns[t]] + y_new
        if on_core:
            far[t - 1] = c_new
        if rc_new:
            chips[rc] = [add_low(outs[rc][0][d], rc_new[0][d]) for d in range(ys)]
        if 0 <= ry < count:
            totals[ry] = add_low(chips[ry][0], *ry_new)
        if rz_new:
            passed = rz_new[0]
        extra.update(new)
    parts = [totals[0]] + ([passed] if zs > 1 else [])
    moe_chip = extra["chip"]
    grads_low = extra["grads"]

    res_grad, branch, grads, logit_grad, gain_two_grad = turn(
        turn_meta, seqs, parts, res, out_grad, gates, code, wr, gain_two, wo
    )
    if replicas > 1:
        grads = jnp.repeat(grads, replicas, axis=0)
    grads = lax.all_to_all(grads, "ep", split_axis=0, concat_axis=0, tiled=True)
    late = late_grads(expert_count, mixed, branch, pay, logit_grad, gain_two_grad)
    late = late.reshape(dp, zs * ys, 2, own_rows, late.shape[1])

    def stage_parts(value, axis, here_at, size):
        return [
            lax.dynamic_index_in_dim(value, (here_at + d) % size, axis, keepdims=False)
            for d in range(size)
        ]

    late_parts = stage_parts(late, 2, core, 2)
    moe = [add_low(moe_chip[0][0], *extra["first"])]
    moe_new = [move(moe_chip[d][1], True, dy=d) for d in range(1, ys)]
    passed = hop(moe[0][0])
    grads_moved = [extra["swap0"], extra["swap1"], swap(grads_low[2])]
    grads, moe, moe_new, passed, moe_chip, late_parts, grads_low, grads_moved = phase_tree(
        grads, moe, moe_new, passed, moe_chip, late_parts, grads_low, grads_moved
    )
    moe.append(add_low(moe_chip[0][1], *moe_new))

    grads_moved.append(swap(grads_low[3]))
    dqkv = back(attend_meta, grads, qk, v, qkt, stat, cos, sin, qkv.shape, seqs, replicas)
    moe_new = [move(moe_chip[d][2], True, dy=d) for d in range(1, ys)]
    passed = hop(add_low(moe[1][0], passed))
    late_got = [move(late_parts[1], True, dc=1)]
    dqkv, moe, moe_new, passed, moe_chip, late_parts, late_got, grads_moved = phase_tree(
        dqkv, moe, moe_new, passed, moe_chip, late_parts, late_got, grads_moved
    )
    moe.append(add_low(moe_chip[0][2], *moe_new))
    late = add_low(late_parts[0], *late_got)

    def groups_of(picked, first):
        rows_in = jnp.stack([dqkv[d, first : first + ys] for d in picked])
        out = dot_nt(rows_in.reshape(-1, PACK), head_w).astype(bf16)
        return out.reshape(len(picked), ys, rows, width)

    halves = ((1, 2), (3, 0)) if zs == 4 else (tuple(range(1, zs)), (0,))
    turn_order = [d for half in halves for d in half]
    near = [groups_of(halves[0], 0)]
    far = [groups_of(halves[0], ys)]
    near, far, dqkv, late = phase_tree(near, far, dqkv, late)

    got = [move(far[0], True, dc=1)]
    near.append(groups_of(halves[1], 0))
    far.append(groups_of(halves[1], ys))
    near, far, got, dqkv, late = phase_tree(near, far, got, dqkv, late)

    def chips_of(k):
        return {
            d: [add_low(near[k][at, y], got[k][at, y]) for y in range(ys)]
            for at, d in enumerate(halves[k])
        }

    chips = chips_of(0)
    totals, received = {}, None
    for k, d in enumerate(turn_order):
        moved = [move(chips[d][y], True, dy=y) for y in range(1, ys)]
        if k == 0:
            got.append(move(far[1], True, dc=1))
            moe_hop = hop(add_low(moe[1][1], passed)) if zs == 4 else passed
            late_parts = stage_parts(late, 0, lax.axis_index("dp"), dp)
            late_got = [lax.ppermute(part, "dp", ring) for part, ring in zip(late_parts[1:], rings)]
            head_grad = head_grads(dqkv, normed_all).reshape(dp * ep, own_rows, PACK)
            near, got, chips, moved, moe_hop, late_parts, late_got, head_grad = phase_tree(
                near, got, chips, moved, moe_hop, late_parts, late_got, head_grad
            )
            late = add_low(late_parts[0], *late_got)
            plane_groups = [[c + 2 * k for k in range(zs * ys)] for c in range(2)]
            late = lax.all_to_all(
                late, "ep", split_axis=0, concat_axis=0, tiled=True, axis_index_groups=plane_groups
            )
            chips.update(chips_of(1))
        else:
            last = totals[turn_order[k - 1]]
            received = hop(last if k == 1 else add_low(last, received))
            chips, moved, received, totals = phase_tree(chips, moved, received, totals)
        totals[d] = add_low(chips[d][0], *moved)
    parts = [totals[0], received]
    head_grad = lax.all_to_all(head_grad, ("dp", "ep"), split_axis=0, concat_axis=0, tiled=True)
    late, head_grad = phase_tree((late, head_grad), totals[0], received)[0]
    late = late.astype(f32).sum(axis=0)
    mparts = [moe[-1][0], moe_hop]
    sums = []
    for own, moved in zip(grads_low, grads_moved):
        piece = own.astype(f32)
        for other in moved:
            piece = piece + other.astype(f32)
        sums.append(piece)
    grads_total = jnp.concatenate(sums)
    gu_total = grads_total[0:width]
    d_total = grads_total[width:]

    head_grad = head_grad.astype(f32).reshape(dp, heads, replicas, own_rows, PACK).sum(axis=(0, 2))

    def rows_of(part, count):
        part = part.reshape(count, heads // count, own_rows, HD).sum(axis=1)
        return part.transpose(1, 0, 2).reshape(own_rows, count * HD)

    query_w_grad = rows_of(head_grad[..., 0:HD], heads)
    key_w_grad = rows_of(head_grad[..., HD : 2 * HD], kv_heads)
    value_w_grad = rows_of(head_grad[..., 2 * HD : 3 * HD], kv_heads)
    gain_one_grad = (
        jnp.sum(query_w_grad * query_weight_matrix.astype(f32), axis=1)
        + jnp.sum(key_w_grad * key_weight_matrix.astype(f32), axis=1)
        + jnp.sum(value_w_grad * value_weight_matrix.astype(f32), axis=1)
    ) / attn_gain.astype(f32)

    moe_own = res
    for part in mparts:
        moe_own = moe_own + part.astype(f32)
    output = jnp.where(
        is_valid[..., None], moe_own.reshape(seqs, span, width), 0.0
    ).astype(bf16)
    small = (output, gain_one_grad, query_w_grad, key_w_grad, value_w_grad, late, gu_total, d_total)
    parts, small = phase_tree(parts, small)
    output, gain_one_grad, query_w_grad, key_w_grad, value_w_grad, late, gu_total, d_total = small
    input_grad = finish(hidden, gain_one, res_grad, parts)
    model = width
    return (
        output,
        input_grad.reshape(seqs, span, width),
        gain_one_grad,
        query_w_grad,
        key_w_grad,
        value_w_grad,
        late[:, 0:model],
        late[:, model + expert_count],
        late[:, model : model + expert_count],
        gu_total[None],
        d_total[None],
    )


def solution(mesh):
    return jax.shard_map(
        body,
        mesh=mesh,
        in_specs=(
            P("dp", "ep", None),
            P("dp"),
            P("dp", "ep", None),
            P("dp", "ep", None),
            P(("dp", "ep")),
            P(("dp", "ep"), None),
            P(("dp", "ep"), None),
            P(("dp", "ep"), None),
            P(("dp", "ep"), None),
            P(("dp", "ep")),
            P(("dp", "ep"), None),
            P("ep", None, None),
            P("ep", None, None),
            P("dp", "ep", None),
        ),
        out_specs=(
            P("dp", "ep", None),
            P("dp", "ep", None),
            P(("dp", "ep")),
            P(("dp", "ep"), None),
            P(("dp", "ep"), None),
            P(("dp", "ep"), None),
            P(("dp", "ep"), None),
            P(("dp", "ep")),
            P(("dp", "ep"), None),
            P("ep", None, None),
            P("ep", None, None),
        ),
        check_vma=False,
    )
```

```python
import functools

import jax
import jax.numpy as jnp
from jax import lax
from jax.experimental import pallas as pl
from jax.experimental.pallas import tpu as pltpu
from jax.sharding import PartitionSpec as P

HD = 64
LANES = 128
SLAB = 256
WIDE = 512
PACK = 256
LOW = 32
eps = 1e-05
theta_base = 10000.0
f32 = jnp.float32
bf16 = jnp.bfloat16
VMEM_LIMIT = 56 * 1024 * 1024


def dot(a, b):
    return lax.dot_general(a, b, (((1,), (0,)), ((), ())), preferred_element_type=f32)


def dot_nt(a, b):
    return lax.dot_general(a, b, (((1,), (1,)), ((), ())), preferred_element_type=f32)


def dot_tn(a, b):
    return lax.dot_general(a, b, (((0,), (0,)), ((), ())), preferred_element_type=f32)


def lanes_of(rows, width=LANES):
    return lax.broadcasted_iota(jnp.int32, (rows, width), 1)


def half_swap(x):
    lane = lanes_of(x.shape[0])
    return jnp.where(lane % HD < HD // 2, pltpu.roll(x, LANES - HD // 2, 1), pltpu.roll(x, HD // 2, 1))


def ep_shape(ep):
    zs = 4 if ep % 8 == 0 else 1
    return zs, ep // (2 * zs), 2


def fetch_from(ep, dz=0, dy=0, dc=0):
    zs, ys, cs = ep_shape(ep)
    pairs = []
    for z in range(zs):
        for y in range(ys):
            for c in range(cs):
                src = (((z + dz) % zs) * ys + (y + dy) % ys) * cs + (c + dc) % cs
                pairs.append((src, (z * ys + y) * cs + c))
    return pairs


def send_to(ep, **offset):
    return [(dst, src) for src, dst in fetch_from(ep, **offset)]


def phase(*values):
    return lax.optimization_barrier(values)


def phase_tree(*values):
    flat, tree = jax.tree.flatten(values)
    return jax.tree.unflatten(tree, phase(*flat))


def add_low(*parts):
    total = parts[0].astype(f32)
    for part in parts[1:]:
        total = total + part.astype(f32)
    return total.astype(bf16)


def project_kernel(place, carry, meta, *refs):
    blocks = refs[:place]
    w_ref, gain_ref, cos_ref, sin_ref = refs[place : place + 4]
    normed_ref, qkv_ref = refs[-2:]
    rows, _ = blocks[0].shape
    span = cos_ref.shape[0] // place
    seqs = rows // span
    lane = lanes_of(rows)
    for j in range(place):
        x = blocks[j][...].astype(f32)
        scale = lax.rsqrt(jnp.mean(x * x, axis=-1, keepdims=True) + eps)
        normed = (x * scale * gain_ref[...]).astype(bf16)
        normed_ref[0, j] = normed
        raw = dot(normed, w_ref[...])
        at = pl.ds(pl.multiple_of(meta[1 + j] * span, 32), span)
        cos = jnp.concatenate([cos_ref[at, :]] * seqs, axis=0)
        sin = jnp.concatenate([sin_ref[at, :]] * seqs, axis=0)
        both = raw[:, 0:LANES]
        both = (both * cos + half_swap(both) * sin).astype(bf16).astype(f32)
        both = jnp.where(lane < HD, both * HD ** (-0.5), both)
        qkv_ref[0, j, :, 0:LANES] = both.astype(bf16)
        qkv_ref[0, j, :, LANES:PACK] = jnp.where(lane < HD, raw[:, LANES:PACK], 0.0).astype(bf16)


def project(meta, blocks, w, gain, cos, sin, zs, dz, carried):
    rows, width = blocks[0].shape
    place = len(blocks)
    span = cos.shape[0] // (zs * place)

    def whole(a):
        return pl.BlockSpec(a.shape, lambda i, m: (0,) * a.ndim)

    table = pl.BlockSpec((place * span, LANES), lambda i, m: (lax.rem(m[0] + dz, zs), 0))
    args = list(blocks) + [w, gain, cos, sin]
    in_specs = [whole(a) for a in blocks] + [whole(w), whole(gain), table, table]
    aliases = {}
    if carried is not None:
        aliases = {1 + len(args): 0, 2 + len(args): 1}
        args += list(carried)
        in_specs += [pl.BlockSpec(memory_space=pl.ANY)] * 2
    return pl.pallas_call(
        functools.partial(project_kernel, place, carried is not None),
        grid_spec=pltpu.PrefetchScalarGridSpec(
            num_scalar_prefetch=1,
            grid=(1,),
            in_specs=in_specs,
            out_specs=(
                pl.BlockSpec((1, place, rows, width), lambda i, m: (dz, 0, 0, 0)),
                pl.BlockSpec((1, place, rows, PACK), lambda i, m: (dz, 0, 0, 0)),
            ),
        ),
        out_shape=(
            jax.ShapeDtypeStruct((zs, place, rows, width), bf16),
            jax.ShapeDtypeStruct((zs, place, rows, PACK), bf16),
        ),
        input_output_aliases=aliases,
        compiler_params=pltpu.CompilerParams(vmem_limit_bytes=VMEM_LIMIT),
        cost_estimate=pl.CostEstimate(
            flops=2 * place * rows * width * PACK,
            bytes_accessed=4 * place * rows * width,
            transcendentals=0,
        ),
        name="project_in",
    )(meta, *args)


def attend_kernel(
    replicas,
    meta,
    qkv_ref,
    out_ref,
    qk_ref,
    v_ref,
    qkt_ref,
    stat_ref,
    vt_ref,
    wide_ref,
):
    zs, place, rows, _ = qkv_ref.shape
    total = qk_ref.shape[1]
    span = total // (zs * place)
    s = pl.program_id(0)
    seqs = rows // span
    source = pl.ds(pl.multiple_of(s * span, 32), span)
    for d in range(zs):
        for j in range(place):
            at = pl.multiple_of((meta[seqs + 1 + d] * place + meta[seqs + 1 + zs + j]) * span, 32)
            qk_ref[0, pl.ds(at, span), :] = qkv_ref[d, j, source, 0:LANES]
            v_ref[0, pl.ds(at, span), :] = qkv_ref[d, j, source, LANES:PACK]
    for lo in range(0, total, SLAB):
        at = slice(lo, lo + SLAB)
        qkt_ref[0, :, at] = qk_ref[0, at, :].astype(f32).T.astype(bf16)
        vt_ref[:, at] = v_ref[0, at, :].astype(f32).T.astype(bf16)

    key_row = lax.broadcasted_iota(jnp.int32, (WIDE, WIDE), 0)
    query_col = lax.broadcasted_iota(jnp.int32, (WIDE, WIDE), 1)

    def one_slab(lo):
        hi = lo + WIDE
        qt = qkt_ref[0, 0:HD, lo:hi]
        diag = dot(qk_ref[0, lo:hi, HD:LANES], qt)
        diag = jnp.where(key_row <= query_col, diag, -jnp.inf)
        top = jnp.max(diag, axis=0, keepdims=True)
        if lo:
            full = dot(qk_ref[0, 0:lo, HD:LANES], qt)
            top = jnp.maximum(top, jnp.max(full, axis=0, keepdims=True))
        p_diag = jnp.exp(diag - top)
        row_total = jnp.sum(p_diag, axis=0, keepdims=True)
        out = dot(vt_ref[:, lo:hi], p_diag.astype(bf16))
        if lo:
            p_full = jnp.exp(full - top)
            row_total = row_total + jnp.sum(p_full, axis=0, keepdims=True)
            out = out + dot(vt_ref[:, 0:lo], p_full.astype(bf16))
        out = out[0:HD] / row_total
        stat_ref[0, 0:HD, lo:hi] = out
        stat_ref[0, HD : HD + 8, lo:hi] = jnp.broadcast_to(top + jnp.log(row_total), (8, WIDE))
        wide_ref[lo:hi, :] = jnp.concatenate([out, out], axis=0).T

    def no_slab(lo):
        stat_ref[0, :, lo : lo + WIDE] = jnp.zeros((HD + 8, WIDE), f32)
        wide_ref[lo : lo + WIDE, :] = jnp.zeros((WIDE, LANES), f32)

    for i, lo in enumerate(range(0, total, WIDE)):
        if replicas > 1:
            mine = meta[seqs] == i % replicas
            pl.when(mine)(functools.partial(one_slab, lo))
            pl.when(jnp.logical_not(mine))(functools.partial(no_slab, lo))
        else:
            one_slab(lo)

    half = span // 2
    for e in range(total // span):
        upper = wide_ref[e * span : e * span + half, :]
        lower = wide_ref[e * span + half : (e + 1) * span, :]
        out_ref[e] = jnp.where(lanes_of(half) < HD, upper, lower).astype(bf16)


def attend(meta, qkv, seqs, replicas):
    zs, place, rows, _ = qkv.shape
    span = rows // seqs
    total = zs * place * span
    return pl.pallas_call(
        functools.partial(attend_kernel, replicas),
        grid=(seqs,),
        out_shape=(
            jax.ShapeDtypeStruct((total // span, seqs * (span // 2), LANES), bf16),
            jax.ShapeDtypeStruct((seqs, total, LANES), bf16),
            jax.ShapeDtypeStruct((seqs, total, LANES), bf16),
            jax.ShapeDtypeStruct((seqs, LANES, total), bf16),
            jax.ShapeDtypeStruct((seqs, HD + 8, total), f32),
        ),
        in_specs=[
            pl.BlockSpec(memory_space=pltpu.SMEM),
            pl.BlockSpec(qkv.shape, lambda s: (0, 0, 0, 0)),
        ],
        out_specs=(
            pl.BlockSpec((total // span, span // 2, LANES), lambda s: (0, s, 0)),
            pl.BlockSpec((1, total, LANES), lambda s: (s, 0, 0)),
            pl.BlockSpec((1, total, LANES), lambda s: (s, 0, 0)),
            pl.BlockSpec((1, LANES, total), lambda s: (s, 0, 0)),
            pl.BlockSpec((1, HD + 8, total), lambda s: (s, 0, 0)),
        ),
        scratch_shapes=[pltpu.VMEM((LANES, total), bf16), pltpu.VMEM((total, LANES), f32)],
        compiler_params=pltpu.CompilerParams(vmem_limit_bytes=VMEM_LIMIT),
        cost_estimate=pl.CostEstimate(
            flops=4 * seqs * total * total * LANES,
            bytes_accessed=4 * seqs * total * PACK,
            transcendentals=seqs * total * total // 2,
        ),
        name="attend_forward",
    )(meta, qkv)


def gates_of(normed, wr_ref, code):
    logits = jnp.where(code != 0, dot(normed, wr_ref[...]), -1e30)
    powers = jnp.exp(logits - jnp.max(logits, axis=-1, keepdims=True))
    return powers / jnp.sum(powers, axis=-1, keepdims=True)


def middle_kernel(
    seqs,
    recv_ref,
    hid_ref,
    wo_ref,
    gain_ref,
    wr_ref,
    code_ref,
    res_ref,
    pay_ref,
    mixed_ref,
    gate_ref,
):
    heads, half_rows, _ = recv_ref.shape
    width = hid_ref.shape[1]
    half = half_rows // seqs
    low = lanes_of(half_rows) < HD
    uppers, lowers = [], []
    for j in range(heads // 2):
        a = recv_ref[2 * j].astype(f32)
        b = recv_ref[2 * j + 1].astype(f32)
        uppers.append(jnp.where(low, a, pltpu.roll(b, HD, 1)).astype(bf16))
        lowers.append(jnp.where(low, pltpu.roll(a, HD, 1), b).astype(bf16))
    upper = jnp.concatenate(uppers, axis=1)
    lower = jnp.concatenate(lowers, axis=1)
    pieces = []
    for s in range(seqs):
        pieces += [upper[s * half : (s + 1) * half], lower[s * half : (s + 1) * half]]
    mixed = jnp.concatenate(pieces, axis=0)
    mixed_ref[...] = mixed
    res = hid_ref[...].astype(f32) + dot(mixed, wo_ref[...])
    res_ref[...] = res
    scale = lax.rsqrt(jnp.mean(res * res, axis=-1, keepdims=True) + eps)
    normed = (res * scale * gain_ref[...]).astype(bf16)
    gate_ref[...] = gates_of(normed, wr_ref, code_ref[...])
    pay_ref[...] = normed


def middle(seqs, recv, hid, wo, gain, wr, code):
    rows, width = hid.shape
    vmem = pl.BlockSpec(memory_space=pltpu.VMEM)
    return pl.pallas_call(
        functools.partial(middle_kernel, seqs),
        out_shape=(
            jax.ShapeDtypeStruct((rows, width), f32),
            jax.ShapeDtypeStruct((rows, width), bf16),
            jax.ShapeDtypeStruct((rows, width), bf16),
            jax.ShapeDtypeStruct((rows, LANES), f32),
        ),
        in_specs=[vmem] * 6,
        out_specs=(vmem,) * 4,
        compiler_params=pltpu.CompilerParams(vmem_limit_bytes=VMEM_LIMIT),
        cost_estimate=pl.CostEstimate(
            flops=4 * rows * width * width, bytes_accessed=4 * width * width, transcendentals=0
        ),
        name="project_out",
    )(recv, hid, wo, gain, wr, code)


def expert_kernel(place, cap, zs, dz, first, meta, *refs):
    pay_in = refs[0:place]
    up_in, wgu_in, wd_in, wr_ref = refs[place : place + 4]
    rest = refs[place + 4 + (0 if first else 6) :]
    near_out, far_out, mnear_out, mfar_out, x_out, pg_out, act_out, both_out = rest[:8]
    pay, up, code, wgu, wd, back_s, moe_s, x_s, pg_s, act_s, both_s, in_sem, out_sem = rest[8:]
    rows, width = pay_in[0].shape
    units = wd.shape[0]
    halves = place // 2
    expert = meta[0]
    plane = lax.rem(meta[1] + dz, zs)
    loads = {}
    order = []
    for j in range(place):
        loads["p", j] = pltpu.make_async_copy(pay_in[j], pay.at[j], in_sem.at[2 * j])
        source = up_in.at[plane * place + meta[2 + j]]
        loads["u", j] = pltpu.make_async_copy(
            source.at[pl.ds(0, rows)], up.at[j], in_sem.at[2 * j + 1]
        )
        loads["c", j] = pltpu.make_async_copy(
            source.at[pl.ds(rows, code.shape[1]), pl.ds(0, code.shape[2])],
            code.at[j],
            in_sem.at[2 * place + 2 + j],
        )
    loads["gu"] = pltpu.make_async_copy(wgu_in, wgu, in_sem.at[2 * place])
    loads["d"] = pltpu.make_async_copy(wd_in, wd, in_sem.at[2 * place + 1])
    order = [("c", j) for j in range(place)]
    order += [("p", j) for j in range(halves)] + ["gu", "d"]
    order += [("u", j) for j in range(halves)]
    order += [("p", j) for j in range(halves, place)] + [("u", j) for j in range(halves, place)]
    for key in order:
        loads[key].start()
    stores = []

    def store(src, dst):
        copy = pltpu.make_async_copy(src, dst, out_sem.at[len(stores)])
        copy.start()
        stores.append(copy)

    def save(h, value, buf, out):
        own = pl.ds(h * halves * cap, halves * cap)
        buf[own, :] = value
        store(buf.at[own], out.at[dz, own])

    lane = lanes_of(rows)
    slot_row = lax.broadcasted_iota(jnp.int32, (cap, rows), 0)
    slot_col = lax.broadcasted_iota(jnp.int32, (rows, cap), 1)
    code_row = lax.broadcasted_iota(jnp.int32, (code.shape[1], rows), 0)
    cap_lane = lanes_of(cap)
    for h in range(2):
        mine = range(h * halves, (h + 1) * halves)
        for j in mine:
            loads["c", j].wait()
            loads["p", j].wait()
        outs_of, xs, gates = [], [], []
        into = []
        for j in mine:
            lines = code[j].astype(f32)
            blank = jnp.zeros((LANES - lines.shape[0], lines.shape[1]), f32)
            codes = jnp.concatenate([lines, blank], axis=0).T[0:rows]
            column = jnp.sum(jnp.where(lane == expert, codes, 0.0), axis=1, keepdims=True)
            line = jnp.sum(
                jnp.where(code_row == expert, lines[:, 0:rows], 0.0), axis=0, keepdims=True
            )
            into.append(jnp.where(line.astype(jnp.int32) == slot_row + 1, 1.0, 0.0).astype(bf16))
            outs_of.append(
                jnp.where(column.astype(jnp.int32) == slot_col + 1, 1.0, 0.0).astype(bf16)
            )
            xs.append(dot(into[-1], pay[j]).astype(bf16))
            gate = gates_of(xs[-1], wr_ref, dot(into[-1], codes.astype(bf16)))
            gates.append(jnp.sum(jnp.where(cap_lane == expert, gate, 0.0), axis=1, keepdims=True))
        x = jnp.concatenate(xs, axis=0)
        gate_prob = jnp.concatenate(gates, axis=0)
        if h == 0:
            loads["gu"].wait()
        save(h, x, x_s, x_out)
        gate_up = dot(x, wgu[...])
        gate = gate_up[:, 0:units]
        high = gate_up[:, units:]
        sig = jax.nn.sigmoid(gate)
        silu = gate * sig
        act = (silu * high).astype(bf16)
        if h == 0:
            loads["d"].wait()
        save(h, act, act_s, act_out)
        made = dot(act, wd[...]).astype(bf16).astype(f32)
        for j in mine:
            loads["u", j].wait()
        upstream = jnp.concatenate([dot(into[k], up[j]) for k, j in enumerate(mine)], axis=0)
        gate_grad = jnp.sum(made * upstream, axis=-1, keepdims=True)
        moe = (made * gate_prob).astype(bf16)
        pair_grad = (upstream * gate_prob).astype(bf16)
        for k, j in enumerate(mine):
            part = slice(k * cap, (k + 1) * cap)
            moe_s[j] = dot(outs_of[k], moe[part]).astype(bf16)
        store(moe_s.at[pl.ds(h * halves, halves)], (mnear_out if h == 0 else mfar_out).at[dz])
        save(h, pair_grad, pg_s, pg_out)
        act_grad = dot_nt(pair_grad, wd[...])
        both = jnp.concatenate(
            [act_grad * high * (sig * (1.0 + gate * (1.0 - sig))), act_grad * silu], axis=1
        ).astype(bf16)
        save(h, both, both_s, both_out)
        back = dot_nt(both, wgu[...]).astype(bf16)
        upper = gate_grad.astype(bf16).astype(f32)
        wide_lane = lanes_of(halves * cap)
        extra = jnp.where(wide_lane == expert, upper, 0.0)
        extra = jnp.where(wide_lane == expert + LOW, gate_grad - upper, extra).astype(bf16)
        for k, j in enumerate(mine):
            part = slice(k * cap, (k + 1) * cap)
            back_s[j, :, 0:width] = dot(outs_of[k], back[part]).astype(bf16)
            back_s[j, :, width:] = dot(outs_of[k], extra[part]).astype(bf16)
        store(back_s.at[pl.ds(h * halves, halves)], near_out if h == 0 else far_out)
    for copy in stores:
        copy.wait()


def experts(meta, pays, upstream, wgu, wd, wr, cap, zs, dz, carried):
    place = len(pays)
    rows, width = pays[0].shape
    wide = width + LANES
    units = wd.shape[0]
    first = carried is None
    anyspace = pl.BlockSpec(memory_space=pl.ANY)
    args = list(pays) + [upstream, wgu, wd, wr]
    code_rows = upstream.shape[1] - rows
    aliases = {}
    if not first:
        aliases = {1 + len(args) + k: 2 + k for k in range(6)}
        args += list(carried)
    half = jax.ShapeDtypeStruct((place // 2, rows, wide), bf16)
    slots = place * cap
    return pl.pallas_call(
        functools.partial(expert_kernel, place, cap, zs, dz, first),
        out_shape=(
            half,
            half,
            jax.ShapeDtypeStruct((zs, place // 2, rows, width), bf16),
            jax.ShapeDtypeStruct((zs, place // 2, rows, width), bf16),
            jax.ShapeDtypeStruct((zs, slots, width), bf16),
            jax.ShapeDtypeStruct((zs, slots, width), bf16),
            jax.ShapeDtypeStruct((zs, slots, units), bf16),
            jax.ShapeDtypeStruct((zs, slots, 2 * units), bf16),
        ),
        in_specs=[pl.BlockSpec(memory_space=pltpu.SMEM)]
        + [anyspace] * (place + 3)
        + [pl.BlockSpec(memory_space=pltpu.VMEM)]
        + [anyspace] * (len(args) - place - 4),
        out_specs=(anyspace,) * 8,
        scratch_shapes=[
            pltpu.VMEM((place, rows, width), bf16),
            pltpu.VMEM((place, rows, width), bf16),
            pltpu.VMEM((place, code_rows, -(-rows // LANES) * LANES), bf16),
            pltpu.VMEM(wgu.shape, bf16),
            pltpu.VMEM(wd.shape, bf16),
            pltpu.VMEM((place, rows, wide), bf16),
            pltpu.VMEM((place, rows, width), bf16),
            pltpu.VMEM((slots, width), bf16),
            pltpu.VMEM((slots, width), bf16),
            pltpu.VMEM((slots, units), bf16),
            pltpu.VMEM((slots, 2 * units), bf16),
            pltpu.SemaphoreType.DMA((3 * place + 2,)),
            pltpu.SemaphoreType.DMA((12,)),
        ],
        input_output_aliases=aliases,
        compiler_params=pltpu.CompilerParams(vmem_limit_bytes=VMEM_LIMIT),
        cost_estimate=pl.CostEstimate(
            flops=16 * slots * width * units, bytes_accessed=12 * slots * width, transcendentals=0
        ),
        name="experts",
    )(meta, *args)


def turn_kernel(nparts, seqs, meta, *refs):
    parts = refs[:nparts]
    (
        res_ref,
        up_ref,
        gate_ref,
        code_ref,
        wr_ref,
        gain_ref,
        wo_ref,
        resgrad_ref,
        branch_ref,
        out_ref,
        logit_ref,
        gaingrad_ref,
    ) = refs[nparts:]
    rows, width = res_ref.shape
    span = rows // seqs
    total = parts[0][...].astype(f32)
    for part in parts[1:]:
        total = total + part[...].astype(f32)
    extra = total[:, width:]
    gate_grad = jnp.where(code_ref[...] > 0, extra + pltpu.roll(extra, LANES - LOW, 1), 0.0)
    gates = gate_ref[...]
    logit_grad = gates * (gate_grad - jnp.sum(gates * gate_grad, axis=-1, keepdims=True))
    logit_ref[...] = logit_grad
    normed_grad = total[:, 0:width] + lax.dot_general(
        logit_grad,
        wr_ref[...].astype(f32),
        (((1,), (1,)), ((), ())),
        preferred_element_type=f32,
        precision=lax.Precision.HIGHEST,
    )
    res = res_ref[...]
    scale = lax.rsqrt(jnp.mean(res * res, axis=-1, keepdims=True) + eps)
    gaingrad_ref[...] = jnp.sum(normed_grad * (res * scale), axis=0, keepdims=True)
    scaled = normed_grad * gain_ref[...]
    row = meta[seqs] + lax.broadcasted_iota(jnp.int32, (span, 1), 0)
    valid = jnp.concatenate([(row < meta[s]).astype(f32) for s in range(seqs)], axis=0)
    upstream = jnp.where(valid > 0, up_ref[...].astype(f32), 0.0)
    centre = jnp.mean(scaled * res, axis=-1, keepdims=True)
    res_grad = upstream + scaled * scale - res * (scale * scale * scale * centre)
    resgrad_ref[...] = res_grad
    branch = res_grad.astype(bf16)
    branch_ref[...] = branch
    mixed = dot_nt(branch, wo_ref[...]).astype(bf16).astype(f32)
    half = span // 2
    low = lanes_of(half) < HD
    for s in range(seqs):
        at = slice(s * half, (s + 1) * half)
        for j in range(out_ref.shape[0] // 2):
            cols = slice(j * LANES, (j + 1) * LANES)
            upper = mixed[s * span : s * span + half, cols]
            lower = mixed[s * span + half : (s + 1) * span, cols]
            out_ref[2 * j, at] = jnp.where(low, upper, pltpu.roll(lower, HD, 1)).astype(bf16)
            out_ref[2 * j + 1, at] = jnp.where(low, pltpu.roll(upper, HD, 1), lower).astype(bf16)


def turn(meta, seqs, parts, res, up, gates, code, wr, gain, wo):
    rows, width = res.shape
    heads = wo.shape[0] // HD
    vmem = pl.BlockSpec(memory_space=pltpu.VMEM)
    return pl.pallas_call(
        functools.partial(turn_kernel, len(parts), seqs),
        out_shape=(
            jax.ShapeDtypeStruct((rows, width), f32),
            jax.ShapeDtypeStruct((rows, width), bf16),
            jax.ShapeDtypeStruct((heads, rows // 2, LANES), bf16),
            jax.ShapeDtypeStruct((rows, LANES), f32),
            jax.ShapeDtypeStruct((1, width), f32),
        ),
        in_specs=[pl.BlockSpec(memory_space=pltpu.SMEM)] + [vmem] * (len(parts) + 7),
        out_specs=(vmem,) * 5,
        compiler_params=pltpu.CompilerParams(vmem_limit_bytes=VMEM_LIMIT),
        cost_estimate=pl.CostEstimate(
            flops=4 * rows * width * width, bytes_accessed=4 * width * width, transcendentals=0
        ),
        name="turn_back",
    )(meta, *parts, res, up, gates, code, wr, gain, wo)


def back_kernel(
    replicas,
    meta,
    grad_ref,
    qk_ref,
    v_ref,
    qkt_ref,
    stat_ref,
    cos_ref,
    sin_ref,
    out_ref,
    do_ref,
    dk_ref,
    dv_ref,
    dqt_ref,
):
    zs, place, rows, _ = out_ref.shape
    total = qk_ref.shape[1]
    span = total // (zs * place)
    seqs = rows // span
    s = pl.program_id(0)
    half = span // 2
    for e in range(total // span):
        chunk = grad_ref[e].astype(f32)
        do_ref[e * span : e * span + half, :] = chunk
        do_ref[e * span + half : (e + 1) * span, :] = pltpu.roll(chunk, HD, 1)
    dk_ref[...] = jnp.zeros_like(dk_ref)
    dv_ref[...] = jnp.zeros_like(dv_ref)
    key_row = lax.broadcasted_iota(jnp.int32, (SLAB, SLAB), 0)
    query_col = lax.broadcasted_iota(jnp.int32, (SLAB, SLAB), 1)
    def one_slab(lo):
        hi = lo + 2 * SLAB
        mid = lo + SLAB
        grad = do_ref[lo:hi, :]
        grad_low = grad.astype(bf16)
        grad_t = grad.T[0:HD]
        delta = jnp.sum(grad_t * stat_ref[0, 0:HD, lo:hi], axis=0, keepdims=True)
        grad_t = grad_t.astype(bf16)
        log_total = stat_ref[0, HD : HD + 1, lo:hi]

        def piece(start, stop, first, last, masked):
            cols = slice(first - lo, last - lo)
            scores = dot(qk_ref[0, start:stop, HD:LANES], qkt_ref[0, 0:HD, first:last])
            probs = jnp.exp(scores - log_total[:, cols])
            if masked:
                probs = jnp.where(key_row <= query_col, probs, 0.0)
            prob_grad = dot(v_ref[0, start:stop, 0:HD], grad_t[:, cols])
            score_grad = (probs * (prob_grad - delta[:, cols])).astype(bf16)
            dv_ref[start:stop, :] += dot(probs.astype(bf16), grad_low[cols])
            dk_ref[start:stop, :] += dot(score_grad, qk_ref[0, first:last, :])
            return dot(qkt_ref[0, :, start:stop], score_grad)

        moved = piece(lo, mid, lo, mid, True)
        moved_next = piece(mid, hi, mid, hi, True) + piece(lo, mid, mid, hi, False)
        if lo:
            full = piece(0, lo, lo, hi, False)
            moved = moved + full[:, 0:SLAB]
            moved_next = moved_next + full[:, SLAB:]
        dqt_ref[:, lo:mid] = moved
        dqt_ref[:, mid:hi] = moved_next

    def no_slab(lo):
        dqt_ref[:, lo : lo + 2 * SLAB] = jnp.zeros((LANES, 2 * SLAB), f32)

    for i, lo in enumerate(range(0, total, 2 * SLAB)):
        if replicas > 1:
            mine = meta[seqs] == i % replicas
            pl.when(mine)(functools.partial(one_slab, lo))
            pl.when(jnp.logical_not(mine))(functools.partial(no_slab, lo))
        else:
            one_slab(lo)

    low = lanes_of(SLAB) < HD
    for lo in range(0, total, SLAB):
        at = slice(lo, lo + SLAB)
        both = jnp.where(low, dk_ref[at, :], dqt_ref[:, at].T * HD ** (-0.5))
        both = pltpu.roll(both, HD, 1)
        dk_ref[at, :] = both * cos_ref[at, :] - half_swap(both) * sin_ref[at, :]
        dv_ref[at, :] = jnp.where(low, dv_ref[at, :], 0.0)
    dest = pl.ds(pl.multiple_of(s * span, 32), span)
    for d in range(zs):
        for j in range(place):
            at = pl.multiple_of((meta[seqs + 1 + d] * place + meta[seqs + 1 + zs + j]) * span, 32)
            out_ref[d, j, dest, 0:LANES] = dk_ref[pl.ds(at, span), :].astype(bf16)
            out_ref[d, j, dest, LANES:PACK] = dv_ref[pl.ds(at, span), :].astype(bf16)


def back(meta, grads, qk, v, qkt, stat, cos, sin, shape, seqs, replicas):
    total = qk.shape[1]
    span = total // grads.shape[0]
    return pl.pallas_call(
        functools.partial(back_kernel, replicas),
        grid=(seqs,),
        out_shape=jax.ShapeDtypeStruct(shape, bf16),
        in_specs=[
            pl.BlockSpec(memory_space=pltpu.SMEM),
            pl.BlockSpec((total // span, span // 2, LANES), lambda s: (0, s, 0)),
            pl.BlockSpec((1, total, LANES), lambda s: (s, 0, 0)),
            pl.BlockSpec((1, total, LANES), lambda s: (s, 0, 0)),
            pl.BlockSpec((1, LANES, total), lambda s: (s, 0, 0)),
            pl.BlockSpec((1, HD + 8, total), lambda s: (s, 0, 0)),
            pl.BlockSpec((total, LANES), lambda s: (0, 0)),
            pl.BlockSpec((total, LANES), lambda s: (0, 0)),
        ],
        out_specs=pl.BlockSpec(shape, lambda s: (0, 0, 0, 0)),
        scratch_shapes=[
            pltpu.VMEM((total, LANES), f32),
            pltpu.VMEM((total, LANES), f32),
            pltpu.VMEM((total, LANES), f32),
            pltpu.VMEM((LANES, total), f32),
        ],
        compiler_params=pltpu.CompilerParams(vmem_limit_bytes=VMEM_LIMIT),
        cost_estimate=pl.CostEstimate(
            flops=10 * seqs * total * total * LANES,
            bytes_accessed=6 * seqs * total * PACK,
            transcendentals=seqs * total * total // 2,
        ),
        name="attend_backward",
    )(meta, grads, qk, v, qkt, stat, cos, sin)


def expert_grads_kernel(x_ref, both_ref, act_ref, pg_ref, *refs):
    outs, acc_ref = refs[:-1], refs[-1]
    width = x_ref.shape[2]

    @pl.when(pl.program_id(0) == 0)
    def _():
        acc_ref[...] = jnp.zeros_like(acc_ref)

    acc_ref[0:width, :] += dot_tn(x_ref[0], both_ref[0])
    acc_ref[width:, :] += dot_tn(act_ref[0], pg_ref[0])

    @pl.when(pl.program_id(0) == pl.num_programs(0) - 1)
    def _():
        for k, out_ref in enumerate(outs):
            rows = out_ref.shape[0]
            out_ref[...] = acc_ref[k * rows : (k + 1) * rows, :].astype(bf16)


def expert_grads(x, both, act, pg):
    zs, slots, width = x.shape
    units = act.shape[2]
    pieces = 4
    piece = (width + units) // pieces

    def block(a):
        return pl.BlockSpec((1,) + a.shape[1:], lambda i: (i, 0, 0))

    return pl.pallas_call(
        expert_grads_kernel,
        grid=(zs,),
        out_shape=(jax.ShapeDtypeStruct((piece, width), bf16),) * pieces,
        in_specs=[block(a) for a in (x, both, act, pg)],
        out_specs=(pl.BlockSpec((piece, width), lambda i: (0, 0)),) * pieces,
        scratch_shapes=[pltpu.VMEM((width + units, width), f32)],
        compiler_params=pltpu.CompilerParams(vmem_limit_bytes=VMEM_LIMIT),
        cost_estimate=pl.CostEstimate(
            flops=6 * zs * slots * width * units, bytes_accessed=8 * zs * slots * width, transcendentals=0
        ),
        name="expert_grads",
    )(x, both, act, pg)


def late_kernel(column, mixed_ref, branch_ref, pay_ref, logit_ref, gain_ref, out_ref):
    width = mixed_ref.shape[1]
    out_ref[:, 0:width] = dot_tn(mixed_ref[...], branch_ref[...]).astype(bf16)
    logit = logit_ref[...]
    high = logit.astype(bf16)
    low = (logit - high.astype(f32)).astype(bf16)
    normed = pay_ref[...]
    side = dot_tn(normed, high) + dot_tn(normed, low)
    gain = jnp.broadcast_to(gain_ref[...], (LANES, width)).T
    out_ref[:, width:] = jnp.where(lanes_of(width) == column, gain, side).astype(bf16)


def late_grads(column, mixed, branch, pay, logit, gain):
    rows, width = mixed.shape
    vmem = pl.BlockSpec(memory_space=pltpu.VMEM)
    return pl.pallas_call(
        functools.partial(late_kernel, column),
        out_shape=jax.ShapeDtypeStruct((width, width + LANES), bf16),
        in_specs=[vmem] * 5,
        out_specs=vmem,
        compiler_params=pltpu.CompilerParams(vmem_limit_bytes=VMEM_LIMIT),
        cost_estimate=pl.CostEstimate(
            flops=2 * rows * width * width, bytes_accessed=4 * width * width, transcendentals=0
        ),
        name="late_grads",
    )(mixed, branch, pay, logit, gain)


def head_grads_kernel(dqkv_ref, normed_ref, out_ref, acc_ref):
    _, place, rows, pack = dqkv_ref.shape

    @pl.when(pl.program_id(0) == 0)
    def _():
        acc_ref[...] = jnp.zeros_like(acc_ref)

    for j in range(place):
        acc_ref[...] += dot_tn(dqkv_ref[0, j], normed_ref[0, j])

    @pl.when(pl.program_id(0) == pl.num_programs(0) - 1)
    def _():
        out_ref[...] = acc_ref[...].T.astype(bf16)


def head_grads(dqkv, normed):
    zs, place, rows, width = normed.shape
    return pl.pallas_call(
        head_grads_kernel,
        grid=(zs,),
        out_shape=jax.ShapeDtypeStruct((width, PACK), bf16),
        in_specs=[
            pl.BlockSpec((1, place, rows, PACK), lambda i: (i, 0, 0, 0)),
            pl.BlockSpec((1, place, rows, width), lambda i: (i, 0, 0, 0)),
        ],
        out_specs=pl.BlockSpec((width, PACK), lambda i: (0, 0)),
        scratch_shapes=[pltpu.VMEM((PACK, width), f32)],
        compiler_params=pltpu.CompilerParams(vmem_limit_bytes=VMEM_LIMIT),
        cost_estimate=pl.CostEstimate(
            flops=2 * zs * place * rows * width * PACK,
            bytes_accessed=2 * zs * place * rows * width,
            transcendentals=0,
        ),
        name="head_grads",
    )(dqkv, normed)


def spread_kernel(dqkv_ref, w_ref, near_ref, far_ref):
    _, place, rows, pack = dqkv_ref.shape
    for ref, first in ((near_ref, 0), (far_ref, place // 2)):
        for j in range(place // 2):
            ref[0, j] = dot_nt(dqkv_ref[0, first + j], w_ref[...]).astype(bf16)


def spread(dqkv, w, picked):
    _, place, rows, pack = dqkv.shape
    width = w.shape[0]
    first, step = picked[0], (picked[1] - picked[0] if len(picked) > 1 else 0)
    half = jax.ShapeDtypeStruct((len(picked), place // 2, rows, width), bf16)
    out = pl.BlockSpec((1, place // 2, rows, width), lambda i: (i, 0, 0, 0))
    return pl.pallas_call(
        spread_kernel,
        grid=(len(picked),),
        out_shape=(half, half),
        in_specs=[
            pl.BlockSpec((1, place, rows, pack), lambda i: (first + i * step, 0, 0, 0)),
            pl.BlockSpec(w.shape, lambda i: (0, 0)),
        ],
        out_specs=(out, out),
        compiler_params=pltpu.CompilerParams(vmem_limit_bytes=VMEM_LIMIT),
        cost_estimate=pl.CostEstimate(
            flops=2 * len(picked) * place * rows * pack * width,
            bytes_accessed=2 * len(picked) * place * rows * width,
            transcendentals=0,
        ),
        name="spread",
    )(dqkv, w)


def finish_kernel(nparts, *refs):
    hid_ref, gain_ref, resgrad_ref = refs[0:3]
    parts = refs[3 : 3 + nparts]
    out_ref = refs[-1]
    total = parts[0][...].astype(f32)
    for part in parts[1:]:
        total = total + part[...].astype(f32)
    x = hid_ref[...].astype(f32)
    scale = lax.rsqrt(jnp.mean(x * x, axis=-1, keepdims=True) + eps)
    scaled = total * gain_ref[...]
    centre = jnp.mean(scaled * x, axis=-1, keepdims=True)
    out_ref[...] = resgrad_ref[...] + scaled * scale - x * (scale * scale * scale * centre)


def finish(hidden, gain, resgrad, parts):
    vmem = pl.BlockSpec(memory_space=pltpu.VMEM)
    return pl.pallas_call(
        functools.partial(finish_kernel, len(parts)),
        out_shape=jax.ShapeDtypeStruct(hidden.shape, f32),
        in_specs=[vmem] * (3 + len(parts)),
        out_specs=vmem,
        compiler_params=pltpu.CompilerParams(vmem_limit_bytes=VMEM_LIMIT),
        name="input_grad",
    )(hidden, gain, resgrad, *parts)


def body(
    hidden,
    lengths,
    expert_ids,
    pair_keep,
    attn_gain,
    query_weight_matrix,
    key_weight_matrix,
    value_weight_matrix,
    attention_output_weight,
    moe_gain,
    router_weight_matrix,
    w_gate_up,
    w_down,
    out_grad,
):
    seqs, span, width = hidden.shape
    rows = seqs * span
    top_k = expert_ids.shape[2]
    ep = lax.axis_size("ep")
    dp = lax.axis_size("dp")
    zs, ys, _ = ep_shape(ep)
    place = 2 * ys
    me = lax.axis_index("ep").astype(jnp.int32)
    expert_count = w_gate_up.shape[0] * ep
    capacity = max(2, rows * top_k // expert_count)
    cap = -(-capacity // 16) * 16
    heads = query_weight_matrix.shape[1] // HD
    kv_heads = key_weight_matrix.shape[1] // HD
    replicas = ep // heads
    total = span * ep
    own_rows = query_weight_matrix.shape[0]
    hidden = hidden.reshape(rows, width)
    out_grad = out_grad.reshape(rows, width)

    def per_head(weight, count):
        split = weight.reshape(own_rows, count, HD).transpose(1, 0, 2)
        return jnp.repeat(split, heads // count, axis=0)

    small = jnp.concatenate(
        [router_weight_matrix, attn_gain[:, None], moe_gain[:, None]], axis=1
    )
    small = jnp.pad(small, ((0, 0), (0, PACK - 3 * HD - small.shape[1])))
    packed = jnp.concatenate(
        [
            per_head(query_weight_matrix, heads),
            per_head(key_weight_matrix, kv_heads),
            per_head(value_weight_matrix, kv_heads),
            jnp.broadcast_to(small[None], (heads,) + small.shape),
        ],
        axis=2,
    )
    packed = jnp.repeat(packed, replicas, axis=0)
    packed = jnp.broadcast_to(packed[None], (dp,) + packed.shape).reshape(
        dp * ep, own_rows, PACK
    )
    packed = lax.all_to_all(packed, ("dp", "ep"), split_axis=0, concat_axis=0, tiled=True)
    head_w = packed.reshape(dp * ep * own_rows, PACK)
    at = 3 * HD
    wr = jnp.pad(head_w[:, at : at + expert_count], ((0, 0), (0, LANES - expert_count)))
    gains = head_w[:, at + expert_count : at + expert_count + 2].astype(f32)
    gain_one = gains[:, 0].reshape(1, width)
    gain_two = gains[:, 1].reshape(1, width)
    head_w = jnp.where(jnp.arange(PACK)[None, :] < at, head_w, jnp.zeros((), bf16))

    positions = me * span + jnp.arange(span, dtype=jnp.int32)
    is_valid = positions[None, :] < lengths[:, None]
    expert_range = jnp.arange(LANES, dtype=jnp.int32)
    hit = expert_ids[..., None] == expert_range
    chosen = jnp.any(hit, axis=2).reshape(rows, LANES).astype(f32)
    live = jnp.any(hit & (pair_keep[..., None] > 0), axis=2) & is_valid[..., None]
    live = live.reshape(rows, LANES).astype(bf16)
    earlier = jnp.arange(rows)[:, None] > jnp.arange(rows)[None, :]
    slot = jnp.dot(earlier.astype(bf16), live, preferred_element_type=f32)
    code = jnp.where((slot < capacity) & (live > 0), slot + 1.0, -chosen)
    code_rows = -(-expert_count // 16) * 16
    lines = jnp.pad(code[:, 0:code_rows].T.astype(bf16), ((0, 0), (0, width - rows)))
    lifted = jnp.concatenate([out_grad, lines])

    rates = theta_base ** (-2.0 * jnp.arange(HD // 2, dtype=f32) / HD)
    angle = jnp.arange(total, dtype=jnp.int32).astype(f32)[:, None] * rates[None, :]
    cos = jnp.tile(jnp.cos(angle), (1, 4))
    sin = jnp.sin(angle)
    sin = jnp.concatenate([-sin, sin, -sin, sin], axis=1)
    core = me % 2
    col = (me // 2) % ys
    plane = me // place
    planes = (plane + jnp.arange(zs, dtype=jnp.int32)) % zs
    rows_at = (col + jnp.arange(ys, dtype=jnp.int32)) % ys
    places = jnp.concatenate([rows_at * 2 + core, rows_at * 2 + 1 - core])
    replica = me % replicas if replicas > 1 else jnp.zeros((), jnp.int32)
    attend_meta = jnp.concatenate([lengths, replica[None], planes, places]).astype(jnp.int32)
    expert_meta = jnp.concatenate([jnp.stack([me, plane]), places]).astype(jnp.int32)
    project_meta = expert_meta[1:]
    turn_meta = jnp.concatenate([lengths, (me * span)[None]]).astype(jnp.int32)

    order = list(range(zs))

    def move(x, sender=False, **offset):
        return lax.ppermute(x, "ep", (send_to if sender else fetch_from)(ep, **offset))

    def steps(t):
        n = len(order)
        return t < n - 1, t < n, 1 <= t <= n, 2 <= t < n + 2

    columns, near, far, carried, x = [hidden], {}, {}, None, hidden
    wo_part = [attention_output_weight]
    for t in range(len(order) + 2):
        on_z, on_y, on_core, on_work = steps(t)
        z_new = [move(columns[t], dz=1)] if on_z else []
        y_new = [move(columns[t], dy=k) for k in range(1, ys)] if on_y else []
        c_new = [move(block, dc=1) for block in near[t - 1]] if on_core else []
        if on_work:
            d = order[t - 2]
            carried = project(
                project_meta, near[t - 2] + far[t - 2], head_w, gain_one, cos, sin, zs, d, carried
            )
        block = wo_part[0]
        wo_new = []
        if t == zs - 1:
            wo_new = [move(block, dz=k) for k in range(1, zs)]
        elif t == zs:
            wo_new = [move(block, dy=k) for k in range(1, ys)]
        x, columns, near, far, z_new, y_new, c_new, carried, wo_part, wo_new = phase_tree(
            x, columns, near, far, z_new, y_new, c_new, carried, wo_part, wo_new
        )
        if wo_new:
            wo_part = [jnp.stack(wo_part + wo_new)]
        columns = columns + z_new
        if on_y:
            near[t] = [columns[t]] + y_new
        if on_core:
            far[t - 1] = c_new
        if t == 2:
            upstream = lax.all_gather(phase(lifted, columns[-1])[0], "ep", axis=0)
    wo_new = [
        lax.ppermute(wo_part[0], "dp", [((i + k) % dp, i) for i in range(dp)]) for k in range(1, dp)
    ]
    normed_all, qkv = carried
    made, qk, v, qkt, stat = attend(attend_meta, qkv, seqs, replicas)
    made, wo_new, wo_part = phase_tree(made, wo_new, wo_part)
    recv = lax.all_to_all(made, "ep", split_axis=0, concat_axis=0, tiled=True)
    wo_part = jnp.stack(wo_part + wo_new)
    wo_part = [jnp.stack([wo_part, move(wo_part, dc=1)])]
    line = jnp.arange(dp * ep, dtype=jnp.int32)
    away = (line % 2 - core) % 2
    away = away * dp + (line // ep - lax.axis_index("dp")) % dp
    away = away * ys + ((line // 2) % ys - col) % ys
    away = away * zs + ((line // place) % zs - plane) % zs
    wo = wo_part[0].reshape(dp * ep, own_rows, width)
    wo = jnp.take(wo, away, axis=0, mode="clip").reshape(heads * HD, width)
    if replicas > 1:
        recv = recv.reshape((heads, replicas) + recv.shape[1:]).sum(axis=1).astype(bf16)
    res, pay, mixed, gates = middle(seqs, recv, hidden, wo, gain_two, wr, code)

    count = zs
    columns, near, far, chips, totals = [pay], {}, {}, {}, {}
    outs, carried, extra, passed = {}, None, {}, None
    rings = [[(i, (i + d) % dp) for i in range(dp)] for d in range(1, dp)]
    cuts = ((1,), tuple(range(2, zs)), (0,))

    def hop(value):
        return lax.ppermute(value, "ep", fetch_from(ep, dz=1))

    def swap(piece):
        return [lax.ppermute(piece, "dp", ring) for ring in rings]

    for t in range(count + 5):
        on_z, on_y, on_core, on_work = steps(t)
        z_new = [move(columns[t], dz=1)] if on_z else []
        y_new = [move(columns[t], dy=k) for k in range(1, ys)] if on_y else []
        c_new = [move(block, dc=1) for block in near[t - 1]] if on_core else []
        rc, ry, rz = t - 3, t - 4, t - 5
        rc_new = [move(outs[rc][1], True, dc=1)] if 0 <= rc < count else []
        ry_new = [move(chips[ry][d], True, dy=d) for d in range(1, ys)] if 0 <= ry < count else []
        rz_new = []
        if 1 <= rz < count:
            rz_new = [hop(totals[rz] if rz == 1 else add_low(totals[rz], passed))]
        new = {}
        if on_work:
            d = order[t - 2]
            out = experts(
                expert_meta,
                near[t - 2] + far[t - 2],
                upstream,
                w_gate_up[0],
                w_down[0],
                wr,
                cap,
                zs,
                d,
                carried,
            )
            outs[t - 2], carried = out[:2], out[2:]
        if t == count + 2:
            new["got"] = move(carried[1], True, dc=1)
            new["grads"] = list(expert_grads(carried[2], carried[5], carried[4], carried[3]))
        if t == count + 3:
            new["chip"] = [
                [
                    add_low(
                        jnp.stack([carried[0][k, d] for k in cut]),
                        jnp.stack([extra["got"][k, d] for k in cut]),
                    )
                    for cut in cuts
                    if cut
                ]
                for d in range(ys)
            ]
        if t == count + 4:
            new["swap"] = swap(extra["grads"][0])
            new["first"] = [move(extra["chip"][d][0], True, dy=d) for d in range(1, ys)]
        state = (pay, columns, near, far, outs, chips, totals, carried, extra)
        state = phase_tree(state, z_new, y_new, c_new, rc_new, ry_new, rz_new, new)
        state, z_new, y_new, c_new, rc_new, ry_new, rz_new, new = state
        pay, columns, near, far, outs, chips, totals, carried, extra = state
        columns = columns + z_new
        if on_y:
            near[t] = [columns[t]] + y_new
        if on_core:
            far[t - 1] = c_new
        if rc_new:
            chips[rc] = [add_low(outs[rc][0][d], rc_new[0][d]) for d in range(ys)]
        if 0 <= ry < count:
            totals[ry] = add_low(chips[ry][0], *ry_new)
        if rz_new:
            passed = rz_new[0]
        extra.update(new)
    parts = [totals[0]] + ([passed] if zs > 1 else [])
    moe_chip = extra["chip"]
    grads_low = extra["grads"]

    res_grad, branch, grads, logit_grad, gain_two_grad = turn(
        turn_meta, seqs, parts, res, out_grad, gates, code, wr, gain_two, wo
    )
    if replicas > 1:
        grads = jnp.repeat(grads, replicas, axis=0)
    grads = lax.all_to_all(grads, "ep", split_axis=0, concat_axis=0, tiled=True)
    late = late_grads(expert_count, mixed, branch, pay, logit_grad, gain_two_grad)
    late = late.reshape(dp, zs * ys, 2, own_rows, late.shape[1])

    def stage_parts(value, axis, here_at, size):
        return [
            lax.dynamic_index_in_dim(value, (here_at + d) % size, axis, keepdims=False)
            for d in range(size)
        ]

    late_parts = stage_parts(late, 2, core, 2)
    moe = [add_low(moe_chip[0][0], *extra["first"])]
    moe_new = [move(moe_chip[d][1], True, dy=d) for d in range(1, ys)]
    grads_moved = [extra["swap"], swap(grads_low[1])]
    state = (grads, moe, moe_new, moe_chip, late_parts, grads_low, grads_moved)
    grads, moe, moe_new, moe_chip, late_parts, grads_low, grads_moved = phase_tree(*state)
    moe.append(add_low(moe_chip[0][1], *moe_new))

    dqkv = back(attend_meta, grads, qk, v, qkt, stat, cos, sin, qkv.shape, seqs, replicas)
    moe_new = [move(moe_chip[d][2], True, dy=d) for d in range(1, ys)]
    passed = hop(moe[0][0])
    late_got = [move(late_parts[1], True, dc=1)]
    swapped = swap(grads_low[2])
    state = (dqkv, moe, moe_new, passed, moe_chip, late_parts, late_got, grads_low, swapped)
    state = phase_tree(*state)
    dqkv, moe, moe_new, passed, moe_chip, late_parts, late_got, grads_low, swapped = state
    moe.append(add_low(moe_chip[0][2], *moe_new))
    grads_moved.append(swapped)
    late = add_low(late_parts[0], *late_got)
    late_parts = stage_parts(late, 0, lax.axis_index("dp"), dp)
    late_got = [lax.ppermute(part, "dp", ring) for part, ring in zip(late_parts[1:], rings)]

    halves = ((1, 2), (3, 0)) if zs == 4 else (tuple(range(1, zs)), (0,))
    turn_order = [d for half in halves for d in half]
    near, far = ([part] for part in spread(dqkv, head_w, halves[0]))
    near, far, dqkv = phase_tree(near, far, dqkv)

    got = [move(far[0], True, dc=1)]
    more = spread(dqkv, head_w, halves[1])
    near.append(more[0])
    far.append(more[1])
    passed = hop(add_low(moe[1][0], passed))
    head_grad = head_grads(dqkv, normed_all).reshape(dp * ep, own_rows, PACK)
    state = (near, far, got, moe, passed, head_grad, late_parts, late_got, grads_low)
    near, far, got, moe, passed, head_grad, late_parts, late_got, grads_low = phase_tree(*state)
    late = add_low(late_parts[0], *late_got)
    plane_groups = [[c + 2 * k for k in range(zs * ys)] for c in range(2)]
    late = lax.all_to_all(
        late, "ep", split_axis=0, concat_axis=0, tiled=True, axis_index_groups=plane_groups
    )

    totals, received = {}, None
    for k, d in enumerate(turn_order):
        half = 0 if d in halves[0] else 1
        at = halves[half].index(d)
        chip = [add_low(near[half][at, y], got[half][at, y]) for y in range(ys)]
        moved = [move(chip[y], True, dy=y) for y in range(1, ys)]
        if k:
            last = totals[turn_order[k - 1]]
            received = hop(last if k == 1 else add_low(last, received))
        if k == 0:
            got.append(move(far[1], True, dc=1))
            passed = hop(add_low(moe[1][1], passed)) if zs == 4 else passed
            swapped = swap(grads_low[3])
            near, got, chip, moved, passed, swapped = phase_tree(
                near, got, chip, moved, passed, swapped
            )
            grads_moved.append(swapped)
        else:
            near, got, chip, moved, received, totals = phase_tree(
                near, got, chip, moved, received, totals
            )
        totals[d] = add_low(chip[0], *moved)
    parts = [totals[0], received]
    head_grad = lax.all_to_all(head_grad, ("dp", "ep"), split_axis=0, concat_axis=0, tiled=True)
    late, head_grad = phase_tree((late, head_grad), totals[0], received)[0]
    late = late.astype(f32).sum(axis=0)
    mparts = [moe[-1][0], passed]
    sums = []
    for own, moved in zip(grads_low, grads_moved):
        piece = own.astype(f32)
        for other in moved:
            piece = piece + other.astype(f32)
        sums.append(piece)
    grads_total = jnp.concatenate(sums)
    gu_total = grads_total[0:width]
    d_total = grads_total[width:]

    head_grad = head_grad.astype(f32).reshape(dp, heads, replicas, own_rows, PACK).sum(axis=(0, 2))

    def rows_of(part, count):
        part = part.reshape(count, heads // count, own_rows, HD).sum(axis=1)
        return part.transpose(1, 0, 2).reshape(own_rows, count * HD)

    query_w_grad = rows_of(head_grad[..., 0:HD], heads)
    key_w_grad = rows_of(head_grad[..., HD : 2 * HD], kv_heads)
    value_w_grad = rows_of(head_grad[..., 2 * HD : 3 * HD], kv_heads)
    gain_one_grad = (
        jnp.sum(query_w_grad * query_weight_matrix.astype(f32), axis=1)
        + jnp.sum(key_w_grad * key_weight_matrix.astype(f32), axis=1)
        + jnp.sum(value_w_grad * value_weight_matrix.astype(f32), axis=1)
    ) / attn_gain.astype(f32)

    moe_own = res
    for part in mparts:
        moe_own = moe_own + part.astype(f32)
    output = jnp.where(
        is_valid[..., None], moe_own.reshape(seqs, span, width), 0.0
    ).astype(bf16)
    small = (output, gain_one_grad, query_w_grad, key_w_grad, value_w_grad, late, gu_total, d_total)
    parts, small = phase_tree(parts, small)
    output, gain_one_grad, query_w_grad, key_w_grad, value_w_grad, late, gu_total, d_total = small
    input_grad = finish(hidden, gain_one, res_grad, parts)
    model = width
    return (
        output,
        input_grad.reshape(seqs, span, width),
        gain_one_grad,
        query_w_grad,
        key_w_grad,
        value_w_grad,
        late[:, 0:model],
        late[:, model + expert_count],
        late[:, model : model + expert_count],
        gu_total[None],
        d_total[None],
    )


def solution(mesh):
    return jax.shard_map(
        body,
        mesh=mesh,
        in_specs=(
            P("dp", "ep", None),
            P("dp"),
            P("dp", "ep", None),
            P("dp", "ep", None),
            P(("dp", "ep")),
            P(("dp", "ep"), None),
            P(("dp", "ep"), None),
            P(("dp", "ep"), None),
            P(("dp", "ep"), None),
            P(("dp", "ep")),
            P(("dp", "ep"), None),
            P("ep", None, None),
            P("ep", None, None),
            P("dp", "ep", None),
        ),
        out_specs=(
            P("dp", "ep", None),
            P("dp", "ep", None),
            P(("dp", "ep")),
            P(("dp", "ep"), None),
            P(("dp", "ep"), None),
            P(("dp", "ep"), None),
            P(("dp", "ep"), None),
            P(("dp", "ep")),
            P(("dp", "ep"), None),
            P("ep", None, None),
            P("ep", None, None),
        ),
        check_vma=False,
    )
```

```python
import functools

import jax
import jax.numpy as jnp
from jax import lax
from jax.experimental import pallas as pl
from jax.experimental.pallas import tpu as pltpu
from jax.sharding import PartitionSpec as P

HD = 64
LANES = 128
SLAB = 256
WIDE = 512
PACK = 256
LOW = 32
eps = 1e-05
theta_base = 10000.0
f32 = jnp.float32
bf16 = jnp.bfloat16
VMEM_LIMIT = 56 * 1024 * 1024


def dot(a, b):
    return lax.dot_general(a, b, (((1,), (0,)), ((), ())), preferred_element_type=f32)


def dot_nt(a, b):
    return lax.dot_general(a, b, (((1,), (1,)), ((), ())), preferred_element_type=f32)


def dot_tn(a, b):
    return lax.dot_general(a, b, (((0,), (0,)), ((), ())), preferred_element_type=f32)


def lanes_of(rows, width=LANES):
    return lax.broadcasted_iota(jnp.int32, (rows, width), 1)


def half_swap(x):
    lane = lanes_of(x.shape[0])
    return jnp.where(lane % HD < HD // 2, pltpu.roll(x, LANES - HD // 2, 1), pltpu.roll(x, HD // 2, 1))


def ep_shape(ep):
    zs = 4 if ep % 8 == 0 else 1
    return zs, ep // (2 * zs), 2


def fetch_from(ep, dz=0, dy=0, dc=0):
    zs, ys, cs = ep_shape(ep)
    pairs = []
    for z in range(zs):
        for y in range(ys):
            for c in range(cs):
                src = (((z + dz) % zs) * ys + (y + dy) % ys) * cs + (c + dc) % cs
                pairs.append((src, (z * ys + y) * cs + c))
    return pairs


def send_to(ep, **offset):
    return [(dst, src) for src, dst in fetch_from(ep, **offset)]


def phase(*values):
    return lax.optimization_barrier(values)


def phase_tree(*values):
    flat, tree = jax.tree.flatten(values)
    return jax.tree.unflatten(tree, phase(*flat))


def add_low(*parts):
    total = parts[0].astype(f32)
    for part in parts[1:]:
        total = total + part.astype(f32)
    return total.astype(bf16)


def project_kernel(place, carry, meta, *refs):
    blocks = refs[:place]
    w_ref, gain_ref, cos_ref, sin_ref = refs[place : place + 4]
    normed_ref, qkv_ref = refs[-2:]
    rows, _ = blocks[0].shape
    span = cos_ref.shape[0] // place
    seqs = rows // span
    lane = lanes_of(rows)
    for j in range(place):
        x = blocks[j][...].astype(f32)
        scale = lax.rsqrt(jnp.mean(x * x, axis=-1, keepdims=True) + eps)
        normed = (x * scale * gain_ref[...]).astype(bf16)
        normed_ref[0, j] = normed
        raw = dot(normed, w_ref[...])
        at = pl.ds(pl.multiple_of(meta[1 + j] * span, 32), span)
        cos = jnp.concatenate([cos_ref[at, :]] * seqs, axis=0)
        sin = jnp.concatenate([sin_ref[at, :]] * seqs, axis=0)
        both = raw[:, 0:LANES]
        both = (both * cos + half_swap(both) * sin).astype(bf16).astype(f32)
        both = jnp.where(lane < HD, both * HD ** (-0.5), both)
        qkv_ref[0, j, :, 0:LANES] = both.astype(bf16)
        qkv_ref[0, j, :, LANES:PACK] = jnp.where(lane < HD, raw[:, LANES:PACK], 0.0).astype(bf16)


def project(meta, blocks, w, gain, cos, sin, zs, dz, carried):
    rows, width = blocks[0].shape
    place = len(blocks)
    span = cos.shape[0] // (zs * place)

    def whole(a):
        return pl.BlockSpec(a.shape, lambda i, m: (0,) * a.ndim)

    table = pl.BlockSpec((place * span, LANES), lambda i, m: (lax.rem(m[0] + dz, zs), 0))
    args = list(blocks) + [w, gain, cos, sin]
    in_specs = [whole(a) for a in blocks] + [whole(w), whole(gain), table, table]
    aliases = {}
    if carried is not None:
        aliases = {1 + len(args): 0, 2 + len(args): 1}
        args += list(carried)
        in_specs += [pl.BlockSpec(memory_space=pl.ANY)] * 2
    return pl.pallas_call(
        functools.partial(project_kernel, place, carried is not None),
        grid_spec=pltpu.PrefetchScalarGridSpec(
            num_scalar_prefetch=1,
            grid=(1,),
            in_specs=in_specs,
            out_specs=(
                pl.BlockSpec((1, place, rows, width), lambda i, m: (dz, 0, 0, 0)),
                pl.BlockSpec((1, place, rows, PACK), lambda i, m: (dz, 0, 0, 0)),
            ),
        ),
        out_shape=(
            jax.ShapeDtypeStruct((zs, place, rows, width), bf16),
            jax.ShapeDtypeStruct((zs, place, rows, PACK), bf16),
        ),
        input_output_aliases=aliases,
        compiler_params=pltpu.CompilerParams(vmem_limit_bytes=VMEM_LIMIT),
        cost_estimate=pl.CostEstimate(
            flops=2 * place * rows * width * PACK,
            bytes_accessed=4 * place * rows * width,
            transcendentals=0,
        ),
        name="project_in",
    )(meta, *args)


def attend_kernel(
    replicas,
    meta,
    qkv_ref,
    out_ref,
    qk_ref,
    v_ref,
    qkt_ref,
    stat_ref,
    vt_ref,
    wide_ref,
):
    zs, place, rows, _ = qkv_ref.shape
    total = qk_ref.shape[1]
    span = total // (zs * place)
    s = pl.program_id(0)
    seqs = rows // span
    source = pl.ds(pl.multiple_of(s * span, 32), span)
    for d in range(zs):
        for j in range(place):
            at = pl.multiple_of((meta[seqs + 1 + d] * place + meta[seqs + 1 + zs + j]) * span, 32)
            qk_ref[0, pl.ds(at, span), :] = qkv_ref[d, j, source, 0:LANES]
            v_ref[0, pl.ds(at, span), :] = qkv_ref[d, j, source, LANES:PACK]
    for lo in range(0, total, SLAB):
        at = slice(lo, lo + SLAB)
        qkt_ref[0, :, at] = qk_ref[0, at, :].astype(f32).T.astype(bf16)
        vt_ref[:, at] = v_ref[0, at, :].astype(f32).T.astype(bf16)

    key_row = lax.broadcasted_iota(jnp.int32, (WIDE, WIDE), 0)
    query_col = lax.broadcasted_iota(jnp.int32, (WIDE, WIDE), 1)

    def one_slab(lo):
        hi = lo + WIDE
        qt = qkt_ref[0, 0:HD, lo:hi]
        diag = dot(qk_ref[0, lo:hi, HD:LANES], qt)
        diag = jnp.where(key_row <= query_col, diag, -jnp.inf)
        top = jnp.max(diag, axis=0, keepdims=True)
        if lo:
            full = dot(qk_ref[0, 0:lo, HD:LANES], qt)
            top = jnp.maximum(top, jnp.max(full, axis=0, keepdims=True))
        p_diag = jnp.exp(diag - top)
        row_total = jnp.sum(p_diag, axis=0, keepdims=True)
        out = dot(vt_ref[:, lo:hi], p_diag.astype(bf16))
        if lo:
            p_full = jnp.exp(full - top)
            row_total = row_total + jnp.sum(p_full, axis=0, keepdims=True)
            out = out + dot(vt_ref[:, 0:lo], p_full.astype(bf16))
        out = out[0:HD] / row_total
        stat_ref[0, 0:HD, lo:hi] = out
        stat_ref[0, HD : HD + 8, lo:hi] = jnp.broadcast_to(top + jnp.log(row_total), (8, WIDE))
        wide_ref[lo:hi, :] = jnp.concatenate([out, out], axis=0).T

    def no_slab(lo):
        stat_ref[0, :, lo : lo + WIDE] = jnp.zeros((HD + 8, WIDE), f32)
        wide_ref[lo : lo + WIDE, :] = jnp.zeros((WIDE, LANES), f32)

    for i, lo in enumerate(range(0, total, WIDE)):
        if replicas > 1:
            mine = meta[seqs] == i % replicas
            pl.when(mine)(functools.partial(one_slab, lo))
            pl.when(jnp.logical_not(mine))(functools.partial(no_slab, lo))
        else:
            one_slab(lo)

    half = span // 2
    for e in range(total // span):
        upper = wide_ref[e * span : e * span + half, :]
        lower = wide_ref[e * span + half : (e + 1) * span, :]
        out_ref[e] = jnp.where(lanes_of(half) < HD, upper, lower).astype(bf16)


def attend(meta, qkv, seqs, replicas):
    zs, place, rows, _ = qkv.shape
    span = rows // seqs
    total = zs * place * span
    return pl.pallas_call(
        functools.partial(attend_kernel, replicas),
        grid=(seqs,),
        out_shape=(
            jax.ShapeDtypeStruct((total // span, seqs * (span // 2), LANES), bf16),
            jax.ShapeDtypeStruct((seqs, total, LANES), bf16),
            jax.ShapeDtypeStruct((seqs, total, LANES), bf16),
            jax.ShapeDtypeStruct((seqs, LANES, total), bf16),
            jax.ShapeDtypeStruct((seqs, HD + 8, total), f32),
        ),
        in_specs=[
            pl.BlockSpec(memory_space=pltpu.SMEM),
            pl.BlockSpec(qkv.shape, lambda s: (0, 0, 0, 0)),
        ],
        out_specs=(
            pl.BlockSpec((total // span, span // 2, LANES), lambda s: (0, s, 0)),
            pl.BlockSpec((1, total, LANES), lambda s: (s, 0, 0)),
            pl.BlockSpec((1, total, LANES), lambda s: (s, 0, 0)),
            pl.BlockSpec((1, LANES, total), lambda s: (s, 0, 0)),
            pl.BlockSpec((1, HD + 8, total), lambda s: (s, 0, 0)),
        ),
        scratch_shapes=[pltpu.VMEM((LANES, total), bf16), pltpu.VMEM((total, LANES), f32)],
        compiler_params=pltpu.CompilerParams(vmem_limit_bytes=VMEM_LIMIT),
        cost_estimate=pl.CostEstimate(
            flops=4 * seqs * total * total * LANES,
            bytes_accessed=4 * seqs * total * PACK,
            transcendentals=seqs * total * total // 2,
        ),
        name="attend_forward",
    )(meta, qkv)


def gates_of(normed, wr_ref, code):
    logits = jnp.where(code != 0, dot(normed, wr_ref[...]), -1e30)
    powers = jnp.exp(logits - jnp.max(logits, axis=-1, keepdims=True))
    return powers / jnp.sum(powers, axis=-1, keepdims=True)


def middle_kernel(
    seqs,
    recv_ref,
    hid_ref,
    wo_ref,
    gain_ref,
    wr_ref,
    code_ref,
    res_ref,
    pay_ref,
    mixed_ref,
    gate_ref,
):
    heads, half_rows, _ = recv_ref.shape
    width = hid_ref.shape[1]
    half = half_rows // seqs
    low = lanes_of(half_rows) < HD
    uppers, lowers = [], []
    for j in range(heads // 2):
        a = recv_ref[2 * j].astype(f32)
        b = recv_ref[2 * j + 1].astype(f32)
        uppers.append(jnp.where(low, a, pltpu.roll(b, HD, 1)).astype(bf16))
        lowers.append(jnp.where(low, pltpu.roll(a, HD, 1), b).astype(bf16))
    upper = jnp.concatenate(uppers, axis=1)
    lower = jnp.concatenate(lowers, axis=1)
    pieces = []
    for s in range(seqs):
        pieces += [upper[s * half : (s + 1) * half], lower[s * half : (s + 1) * half]]
    mixed = jnp.concatenate(pieces, axis=0)
    mixed_ref[...] = mixed
    res = hid_ref[...].astype(f32) + dot(mixed, wo_ref[...])
    res_ref[...] = res
    scale = lax.rsqrt(jnp.mean(res * res, axis=-1, keepdims=True) + eps)
    normed = (res * scale * gain_ref[...]).astype(bf16)
    gate_ref[...] = gates_of(normed, wr_ref, code_ref[...])
    pay_ref[...] = normed


def middle(seqs, recv, hid, wo, gain, wr, code):
    rows, width = hid.shape
    vmem = pl.BlockSpec(memory_space=pltpu.VMEM)
    return pl.pallas_call(
        functools.partial(middle_kernel, seqs),
        out_shape=(
            jax.ShapeDtypeStruct((rows, width), f32),
            jax.ShapeDtypeStruct((rows, width), bf16),
            jax.ShapeDtypeStruct((rows, width), bf16),
            jax.ShapeDtypeStruct((rows, LANES), f32),
        ),
        in_specs=[vmem] * 6,
        out_specs=(vmem,) * 4,
        compiler_params=pltpu.CompilerParams(vmem_limit_bytes=VMEM_LIMIT),
        cost_estimate=pl.CostEstimate(
            flops=4 * rows * width * width, bytes_accessed=4 * width * width, transcendentals=0
        ),
        name="project_out",
    )(recv, hid, wo, gain, wr, code)


def expert_kernel(place, cap, zs, dz, first, meta, *refs):
    pay_in = refs[0:place]
    up_in, wgu_in, wd_in, wr_ref = refs[place : place + 4]
    rest = refs[place + 4 + (0 if first else 6) :]
    near_out, far_out, mnear_out, mfar_out, x_out, pg_out, act_out, both_out = rest[:8]
    pay, up, code, wgu, wd, back_s, moe_s, x_s, pg_s, act_s, both_s, in_sem, out_sem = rest[8:]
    rows, width = pay_in[0].shape
    units = wd.shape[0]
    halves = place // 2
    expert = meta[0]
    plane = lax.rem(meta[1] + dz, zs)
    loads = {}
    order = []
    for j in range(place):
        loads["p", j] = pltpu.make_async_copy(pay_in[j], pay.at[j], in_sem.at[2 * j])
        source = up_in.at[plane * place + meta[2 + j]]
        loads["u", j] = pltpu.make_async_copy(
            source.at[pl.ds(0, rows)], up.at[j], in_sem.at[2 * j + 1]
        )
        loads["c", j] = pltpu.make_async_copy(
            source.at[pl.ds(rows, code.shape[1]), pl.ds(0, code.shape[2])],
            code.at[j],
            in_sem.at[2 * place + 2 + j],
        )
    loads["gu"] = pltpu.make_async_copy(wgu_in, wgu, in_sem.at[2 * place])
    loads["d"] = pltpu.make_async_copy(wd_in, wd, in_sem.at[2 * place + 1])
    order = [("c", j) for j in range(place)]
    order += [("p", j) for j in range(halves)] + ["gu", "d"]
    order += [("u", j) for j in range(halves)]
    order += [("p", j) for j in range(halves, place)] + [("u", j) for j in range(halves, place)]
    for key in order:
        loads[key].start()
    stores = []

    def store(src, dst):
        copy = pltpu.make_async_copy(src, dst, out_sem.at[len(stores)])
        copy.start()
        stores.append(copy)

    def save(h, value, buf, out):
        own = pl.ds(h * halves * cap, halves * cap)
        buf[own, :] = value
        store(buf.at[own], out.at[dz, own])

    lane = lanes_of(rows)
    slot_row = lax.broadcasted_iota(jnp.int32, (cap, rows), 0)
    slot_col = lax.broadcasted_iota(jnp.int32, (rows, cap), 1)
    code_row = lax.broadcasted_iota(jnp.int32, (code.shape[1], rows), 0)
    cap_lane = lanes_of(cap)
    for h in range(2):
        mine = range(h * halves, (h + 1) * halves)
        for j in mine:
            loads["c", j].wait()
            loads["p", j].wait()
        outs_of, xs, gates = [], [], []
        into = []
        for j in mine:
            lines = code[j].astype(f32)
            blank = jnp.zeros((LANES - lines.shape[0], lines.shape[1]), f32)
            codes = jnp.concatenate([lines, blank], axis=0).T[0:rows]
            column = jnp.sum(jnp.where(lane == expert, codes, 0.0), axis=1, keepdims=True)
            line = jnp.sum(
                jnp.where(code_row == expert, lines[:, 0:rows], 0.0), axis=0, keepdims=True
            )
            into.append(jnp.where(line.astype(jnp.int32) == slot_row + 1, 1.0, 0.0).astype(bf16))
            outs_of.append(
                jnp.where(column.astype(jnp.int32) == slot_col + 1, 1.0, 0.0).astype(bf16)
            )
            xs.append(dot(into[-1], pay[j]).astype(bf16))
            gate = gates_of(xs[-1], wr_ref, dot(into[-1], codes.astype(bf16)))
            gates.append(jnp.sum(jnp.where(cap_lane == expert, gate, 0.0), axis=1, keepdims=True))
        x = jnp.concatenate(xs, axis=0)
        gate_prob = jnp.concatenate(gates, axis=0)
        if h == 0:
            loads["gu"].wait()
        save(h, x, x_s, x_out)
        gate_up = dot(x, wgu[...])
        gate = gate_up[:, 0:units]
        high = gate_up[:, units:]
        sig = jax.nn.sigmoid(gate)
        silu = gate * sig
        act = (silu * high).astype(bf16)
        if h == 0:
            loads["d"].wait()
        save(h, act, act_s, act_out)
        made = dot(act, wd[...]).astype(bf16).astype(f32)
        for j in mine:
            loads["u", j].wait()
        upstream = jnp.concatenate([dot(into[k], up[j]) for k, j in enumerate(mine)], axis=0)
        gate_grad = jnp.sum(made * upstream, axis=-1, keepdims=True)
        moe = (made * gate_prob).astype(bf16)
        pair_grad = (upstream * gate_prob).astype(bf16)
        for k, j in enumerate(mine):
            part = slice(k * cap, (k + 1) * cap)
            moe_s[j] = dot(outs_of[k], moe[part]).astype(bf16)
        store(moe_s.at[pl.ds(h * halves, halves)], (mnear_out if h == 0 else mfar_out).at[dz])
        save(h, pair_grad, pg_s, pg_out)
        act_grad = dot_nt(pair_grad, wd[...])
        both = jnp.concatenate(
            [act_grad * high * (sig * (1.0 + gate * (1.0 - sig))), act_grad * silu], axis=1
        ).astype(bf16)
        save(h, both, both_s, both_out)
        back = dot_nt(both, wgu[...]).astype(bf16)
        upper = gate_grad.astype(bf16).astype(f32)
        wide_lane = lanes_of(halves * cap)
        extra = jnp.where(wide_lane == expert, upper, 0.0)
        extra = jnp.where(wide_lane == expert + LOW, gate_grad - upper, extra).astype(bf16)
        for k, j in enumerate(mine):
            part = slice(k * cap, (k + 1) * cap)
            back_s[j, :, 0:width] = dot(outs_of[k], back[part]).astype(bf16)
            back_s[j, :, width:] = dot(outs_of[k], extra[part]).astype(bf16)
        store(back_s.at[pl.ds(h * halves, halves)], near_out if h == 0 else far_out)
    for copy in stores:
        copy.wait()


def experts(meta, pays, upstream, wgu, wd, wr, cap, zs, dz, carried):
    place = len(pays)
    rows, width = pays[0].shape
    wide = width + LANES
    units = wd.shape[0]
    first = carried is None
    anyspace = pl.BlockSpec(memory_space=pl.ANY)
    args = list(pays) + [upstream, wgu, wd, wr]
    code_rows = upstream.shape[1] - rows
    aliases = {}
    if not first:
        aliases = {1 + len(args) + k: 2 + k for k in range(6)}
        args += list(carried)
    half = jax.ShapeDtypeStruct((place // 2, rows, wide), bf16)
    slots = place * cap
    return pl.pallas_call(
        functools.partial(expert_kernel, place, cap, zs, dz, first),
        out_shape=(
            half,
            half,
            jax.ShapeDtypeStruct((zs, place // 2, rows, width), bf16),
            jax.ShapeDtypeStruct((zs, place // 2, rows, width), bf16),
            jax.ShapeDtypeStruct((zs, slots, width), bf16),
            jax.ShapeDtypeStruct((zs, slots, width), bf16),
            jax.ShapeDtypeStruct((zs, slots, units), bf16),
            jax.ShapeDtypeStruct((zs, slots, 2 * units), bf16),
        ),
        in_specs=[pl.BlockSpec(memory_space=pltpu.SMEM)]
        + [anyspace] * (place + 3)
        + [pl.BlockSpec(memory_space=pltpu.VMEM)]
        + [anyspace] * (len(args) - place - 4),
        out_specs=(anyspace,) * 8,
        scratch_shapes=[
            pltpu.VMEM((place, rows, width), bf16),
            pltpu.VMEM((place, rows, width), bf16),
            pltpu.VMEM((place, code_rows, -(-rows // LANES) * LANES), bf16),
            pltpu.VMEM(wgu.shape, bf16),
            pltpu.VMEM(wd.shape, bf16),
            pltpu.VMEM((place, rows, wide), bf16),
            pltpu.VMEM((place, rows, width), bf16),
            pltpu.VMEM((slots, width), bf16),
            pltpu.VMEM((slots, width), bf16),
            pltpu.VMEM((slots, units), bf16),
            pltpu.VMEM((slots, 2 * units), bf16),
            pltpu.SemaphoreType.DMA((3 * place + 2,)),
            pltpu.SemaphoreType.DMA((12,)),
        ],
        input_output_aliases=aliases,
        compiler_params=pltpu.CompilerParams(vmem_limit_bytes=VMEM_LIMIT),
        cost_estimate=pl.CostEstimate(
            flops=16 * slots * width * units, bytes_accessed=12 * slots * width, transcendentals=0
        ),
        name="experts",
    )(meta, *args)


def turn_kernel(nparts, seqs, meta, *refs):
    parts = refs[:nparts]
    (
        res_ref,
        up_ref,
        gate_ref,
        code_ref,
        wr_ref,
        gain_ref,
        wo_ref,
        resgrad_ref,
        branch_ref,
        out_ref,
        logit_ref,
        gaingrad_ref,
    ) = refs[nparts:]
    rows, width = res_ref.shape
    span = rows // seqs
    total = parts[0][...].astype(f32)
    for part in parts[1:]:
        total = total + part[...].astype(f32)
    extra = total[:, width:]
    gate_grad = jnp.where(code_ref[...] > 0, extra + pltpu.roll(extra, LANES - LOW, 1), 0.0)
    gates = gate_ref[...]
    logit_grad = gates * (gate_grad - jnp.sum(gates * gate_grad, axis=-1, keepdims=True))
    logit_ref[...] = logit_grad
    normed_grad = total[:, 0:width] + lax.dot_general(
        logit_grad,
        wr_ref[...].astype(f32),
        (((1,), (1,)), ((), ())),
        preferred_element_type=f32,
        precision=lax.Precision.HIGHEST,
    )
    res = res_ref[...]
    scale = lax.rsqrt(jnp.mean(res * res, axis=-1, keepdims=True) + eps)
    gaingrad_ref[...] = jnp.sum(normed_grad * (res * scale), axis=0, keepdims=True)
    scaled = normed_grad * gain_ref[...]
    row = meta[seqs] + lax.broadcasted_iota(jnp.int32, (span, 1), 0)
    valid = jnp.concatenate([(row < meta[s]).astype(f32) for s in range(seqs)], axis=0)
    upstream = jnp.where(valid > 0, up_ref[...].astype(f32), 0.0)
    centre = jnp.mean(scaled * res, axis=-1, keepdims=True)
    res_grad = upstream + scaled * scale - res * (scale * scale * scale * centre)
    resgrad_ref[...] = res_grad
    branch = res_grad.astype(bf16)
    branch_ref[...] = branch
    mixed = dot_nt(branch, wo_ref[...]).astype(bf16).astype(f32)
    half = span // 2
    low = lanes_of(half) < HD
    for s in range(seqs):
        at = slice(s * half, (s + 1) * half)
        for j in range(out_ref.shape[0] // 2):
            cols = slice(j * LANES, (j + 1) * LANES)
            upper = mixed[s * span : s * span + half, cols]
            lower = mixed[s * span + half : (s + 1) * span, cols]
            out_ref[2 * j, at] = jnp.where(low, upper, pltpu.roll(lower, HD, 1)).astype(bf16)
            out_ref[2 * j + 1, at] = jnp.where(low, pltpu.roll(upper, HD, 1), lower).astype(bf16)


def turn(meta, seqs, parts, res, up, gates, code, wr, gain, wo):
    rows, width = res.shape
    heads = wo.shape[0] // HD
    vmem = pl.BlockSpec(memory_space=pltpu.VMEM)
    return pl.pallas_call(
        functools.partial(turn_kernel, len(parts), seqs),
        out_shape=(
            jax.ShapeDtypeStruct((rows, width), f32),
            jax.ShapeDtypeStruct((rows, width), bf16),
            jax.ShapeDtypeStruct((heads, rows // 2, LANES), bf16),
            jax.ShapeDtypeStruct((rows, LANES), f32),
            jax.ShapeDtypeStruct((1, width), f32),
        ),
        in_specs=[pl.BlockSpec(memory_space=pltpu.SMEM)] + [vmem] * (len(parts) + 7),
        out_specs=(vmem,) * 5,
        compiler_params=pltpu.CompilerParams(vmem_limit_bytes=VMEM_LIMIT),
        cost_estimate=pl.CostEstimate(
            flops=4 * rows * width * width, bytes_accessed=4 * width * width, transcendentals=0
        ),
        name="turn_back",
    )(meta, *parts, res, up, gates, code, wr, gain, wo)


def back_kernel(
    replicas,
    meta,
    grad_ref,
    qk_ref,
    v_ref,
    qkt_ref,
    stat_ref,
    cos_ref,
    sin_ref,
    out_ref,
    do_ref,
    dk_ref,
    dv_ref,
    dqt_ref,
):
    zs, place, rows, _ = out_ref.shape
    total = qk_ref.shape[1]
    span = total // (zs * place)
    seqs = rows // span
    s = pl.program_id(0)
    half = span // 2
    for e in range(total // span):
        chunk = grad_ref[e].astype(f32)
        do_ref[e * span : e * span + half, :] = chunk
        do_ref[e * span + half : (e + 1) * span, :] = pltpu.roll(chunk, HD, 1)
    dk_ref[...] = jnp.zeros_like(dk_ref)
    dv_ref[...] = jnp.zeros_like(dv_ref)
    key_row = lax.broadcasted_iota(jnp.int32, (SLAB, SLAB), 0)
    query_col = lax.broadcasted_iota(jnp.int32, (SLAB, SLAB), 1)
    def one_slab(lo):
        hi = lo + 2 * SLAB
        mid = lo + SLAB
        grad = do_ref[lo:hi, :]
        grad_low = grad.astype(bf16)
        grad_t = grad.T[0:HD]
        delta = jnp.sum(grad_t * stat_ref[0, 0:HD, lo:hi], axis=0, keepdims=True)
        grad_t = grad_t.astype(bf16)
        log_total = stat_ref[0, HD : HD + 1, lo:hi]

        def piece(start, stop, first, last, masked):
            cols = slice(first - lo, last - lo)
            scores = dot(qk_ref[0, start:stop, HD:LANES], qkt_ref[0, 0:HD, first:last])
            probs = jnp.exp(scores - log_total[:, cols])
            if masked:
                probs = jnp.where(key_row <= query_col, probs, 0.0)
            prob_grad = dot(v_ref[0, start:stop, 0:HD], grad_t[:, cols])
            score_grad = (probs * (prob_grad - delta[:, cols])).astype(bf16)
            dv_ref[start:stop, :] += dot(probs.astype(bf16), grad_low[cols])
            dk_ref[start:stop, :] += dot(score_grad, qk_ref[0, first:last, :])
            return dot(qkt_ref[0, :, start:stop], score_grad)

        moved = piece(lo, mid, lo, mid, True)
        moved_next = piece(mid, hi, mid, hi, True) + piece(lo, mid, mid, hi, False)
        if lo:
            full = piece(0, lo, lo, hi, False)
            moved = moved + full[:, 0:SLAB]
            moved_next = moved_next + full[:, SLAB:]
        dqt_ref[:, lo:mid] = moved
        dqt_ref[:, mid:hi] = moved_next

    def no_slab(lo):
        dqt_ref[:, lo : lo + 2 * SLAB] = jnp.zeros((LANES, 2 * SLAB), f32)

    for i, lo in enumerate(range(0, total, 2 * SLAB)):
        if replicas > 1:
            mine = meta[seqs] == i % replicas
            pl.when(mine)(functools.partial(one_slab, lo))
            pl.when(jnp.logical_not(mine))(functools.partial(no_slab, lo))
        else:
            one_slab(lo)

    low = lanes_of(SLAB) < HD
    for lo in range(0, total, SLAB):
        at = slice(lo, lo + SLAB)
        both = jnp.where(low, dk_ref[at, :], dqt_ref[:, at].T * HD ** (-0.5))
        both = pltpu.roll(both, HD, 1)
        dk_ref[at, :] = both * cos_ref[at, :] - half_swap(both) * sin_ref[at, :]
        dv_ref[at, :] = jnp.where(low, dv_ref[at, :], 0.0)
    dest = pl.ds(pl.multiple_of(s * span, 32), span)
    for d in range(zs):
        for j in range(place):
            at = pl.multiple_of((meta[seqs + 1 + d] * place + meta[seqs + 1 + zs + j]) * span, 32)
            out_ref[d, j, dest, 0:LANES] = dk_ref[pl.ds(at, span), :].astype(bf16)
            out_ref[d, j, dest, LANES:PACK] = dv_ref[pl.ds(at, span), :].astype(bf16)


def back(meta, grads, qk, v, qkt, stat, cos, sin, shape, seqs, replicas):
    total = qk.shape[1]
    span = total // grads.shape[0]
    return pl.pallas_call(
        functools.partial(back_kernel, replicas),
        grid=(seqs,),
        out_shape=jax.ShapeDtypeStruct(shape, bf16),
        in_specs=[
            pl.BlockSpec(memory_space=pltpu.SMEM),
            pl.BlockSpec((total // span, span // 2, LANES), lambda s: (0, s, 0)),
            pl.BlockSpec((1, total, LANES), lambda s: (s, 0, 0)),
            pl.BlockSpec((1, total, LANES), lambda s: (s, 0, 0)),
            pl.BlockSpec((1, LANES, total), lambda s: (s, 0, 0)),
            pl.BlockSpec((1, HD + 8, total), lambda s: (s, 0, 0)),
            pl.BlockSpec((total, LANES), lambda s: (0, 0)),
            pl.BlockSpec((total, LANES), lambda s: (0, 0)),
        ],
        out_specs=pl.BlockSpec(shape, lambda s: (0, 0, 0, 0)),
        scratch_shapes=[
            pltpu.VMEM((total, LANES), f32),
            pltpu.VMEM((total, LANES), f32),
            pltpu.VMEM((total, LANES), f32),
            pltpu.VMEM((LANES, total), f32),
        ],
        compiler_params=pltpu.CompilerParams(vmem_limit_bytes=VMEM_LIMIT),
        cost_estimate=pl.CostEstimate(
            flops=10 * seqs * total * total * LANES,
            bytes_accessed=6 * seqs * total * PACK,
            transcendentals=seqs * total * total // 2,
        ),
        name="attend_backward",
    )(meta, grads, qk, v, qkt, stat, cos, sin)


def expert_grads_kernel(x_ref, both_ref, act_ref, pg_ref, *refs):
    outs, acc_ref = refs[:-1], refs[-1]
    width = x_ref.shape[2]

    @pl.when(pl.program_id(0) == 0)
    def _():
        acc_ref[...] = jnp.zeros_like(acc_ref)

    acc_ref[0:width, :] += dot_tn(x_ref[0], both_ref[0])
    acc_ref[width:, :] += dot_tn(act_ref[0], pg_ref[0])

    @pl.when(pl.program_id(0) == pl.num_programs(0) - 1)
    def _():
        for k, out_ref in enumerate(outs):
            rows = out_ref.shape[0]
            out_ref[...] = acc_ref[k * rows : (k + 1) * rows, :].astype(bf16)


def expert_grads(x, both, act, pg):
    zs, slots, width = x.shape
    units = act.shape[2]
    pieces = 4
    piece = (width + units) // pieces

    def block(a):
        return pl.BlockSpec((1,) + a.shape[1:], lambda i: (i, 0, 0))

    return pl.pallas_call(
        expert_grads_kernel,
        grid=(zs,),
        out_shape=(jax.ShapeDtypeStruct((piece, width), bf16),) * pieces,
        in_specs=[block(a) for a in (x, both, act, pg)],
        out_specs=(pl.BlockSpec((piece, width), lambda i: (0, 0)),) * pieces,
        scratch_shapes=[pltpu.VMEM((width + units, width), f32)],
        compiler_params=pltpu.CompilerParams(vmem_limit_bytes=VMEM_LIMIT),
        cost_estimate=pl.CostEstimate(
            flops=6 * zs * slots * width * units, bytes_accessed=8 * zs * slots * width, transcendentals=0
        ),
        name="expert_grads",
    )(x, both, act, pg)


def late_kernel(column, mixed_ref, branch_ref, pay_ref, logit_ref, gain_ref, out_ref):
    width = mixed_ref.shape[1]
    out_ref[:, 0:width] = dot_tn(mixed_ref[...], branch_ref[...]).astype(bf16)
    logit = logit_ref[...]
    high = logit.astype(bf16)
    low = (logit - high.astype(f32)).astype(bf16)
    normed = pay_ref[...]
    side = dot_tn(normed, high) + dot_tn(normed, low)
    gain = jnp.broadcast_to(gain_ref[...], (LANES, width)).T
    out_ref[:, width:] = jnp.where(lanes_of(width) == column, gain, side).astype(bf16)


def late_grads(column, mixed, branch, pay, logit, gain):
    rows, width = mixed.shape
    vmem = pl.BlockSpec(memory_space=pltpu.VMEM)
    return pl.pallas_call(
        functools.partial(late_kernel, column),
        out_shape=jax.ShapeDtypeStruct((width, width + LANES), bf16),
        in_specs=[vmem] * 5,
        out_specs=vmem,
        compiler_params=pltpu.CompilerParams(vmem_limit_bytes=VMEM_LIMIT),
        cost_estimate=pl.CostEstimate(
            flops=2 * rows * width * width, bytes_accessed=4 * width * width, transcendentals=0
        ),
        name="late_grads",
    )(mixed, branch, pay, logit, gain)


def head_grads_kernel(dqkv_ref, normed_ref, out_ref, acc_ref):
    _, place, rows, pack = dqkv_ref.shape

    @pl.when(pl.program_id(0) == 0)
    def _():
        acc_ref[...] = jnp.zeros_like(acc_ref)

    left = dqkv_ref[0].reshape(place * rows, pack)
    acc_ref[...] += dot_tn(left, normed_ref[0].reshape(place * rows, normed_ref.shape[3]))

    @pl.when(pl.program_id(0) == pl.num_programs(0) - 1)
    def _():
        out_ref[...] = acc_ref[...].T.astype(bf16)


def head_grads(dqkv, normed):
    zs, place, rows, width = normed.shape
    return pl.pallas_call(
        head_grads_kernel,
        grid=(zs,),
        out_shape=jax.ShapeDtypeStruct((width, PACK), bf16),
        in_specs=[
            pl.BlockSpec((1, place, rows, PACK), lambda i: (i, 0, 0, 0)),
            pl.BlockSpec((1, place, rows, width), lambda i: (i, 0, 0, 0)),
        ],
        out_specs=pl.BlockSpec((width, PACK), lambda i: (0, 0)),
        scratch_shapes=[pltpu.VMEM((PACK, width), f32)],
        compiler_params=pltpu.CompilerParams(vmem_limit_bytes=VMEM_LIMIT),
        cost_estimate=pl.CostEstimate(
            flops=2 * zs * place * rows * width * PACK,
            bytes_accessed=2 * zs * place * rows * width,
            transcendentals=0,
        ),
        name="head_grads",
    )(dqkv, normed)


def spread_kernel(dqkv_ref, w_ref, near_ref, far_ref):
    _, place, rows, pack = dqkv_ref.shape
    for ref, first in ((near_ref, 0), (far_ref, place // 2)):
        for j in range(place // 2):
            ref[0, j] = dot_nt(dqkv_ref[0, first + j], w_ref[...]).astype(bf16)


def spread(dqkv, w, picked):
    _, place, rows, pack = dqkv.shape
    width = w.shape[0]
    first, step = picked[0], (picked[1] - picked[0] if len(picked) > 1 else 0)
    half = jax.ShapeDtypeStruct((len(picked), place // 2, rows, width), bf16)
    out = pl.BlockSpec((1, place // 2, rows, width), lambda i: (i, 0, 0, 0))
    return pl.pallas_call(
        spread_kernel,
        grid=(len(picked),),
        out_shape=(half, half),
        in_specs=[
            pl.BlockSpec((1, place, rows, pack), lambda i: (first + i * step, 0, 0, 0)),
            pl.BlockSpec(w.shape, lambda i: (0, 0)),
        ],
        out_specs=(out, out),
        compiler_params=pltpu.CompilerParams(vmem_limit_bytes=VMEM_LIMIT),
        cost_estimate=pl.CostEstimate(
            flops=2 * len(picked) * place * rows * pack * width,
            bytes_accessed=2 * len(picked) * place * rows * width,
            transcendentals=0,
        ),
        name="spread",
    )(dqkv, w)


def finish_kernel(nparts, *refs):
    hid_ref, gain_ref, resgrad_ref = refs[0:3]
    parts = refs[3 : 3 + nparts]
    out_ref = refs[-1]
    total = parts[0][...].astype(f32)
    for part in parts[1:]:
        total = total + part[...].astype(f32)
    x = hid_ref[...].astype(f32)
    scale = lax.rsqrt(jnp.mean(x * x, axis=-1, keepdims=True) + eps)
    scaled = total * gain_ref[...]
    centre = jnp.mean(scaled * x, axis=-1, keepdims=True)
    out_ref[...] = resgrad_ref[...] + scaled * scale - x * (scale * scale * scale * centre)


def finish(hidden, gain, resgrad, parts):
    vmem = pl.BlockSpec(memory_space=pltpu.VMEM)
    return pl.pallas_call(
        functools.partial(finish_kernel, len(parts)),
        out_shape=jax.ShapeDtypeStruct(hidden.shape, f32),
        in_specs=[vmem] * (3 + len(parts)),
        out_specs=vmem,
        compiler_params=pltpu.CompilerParams(vmem_limit_bytes=VMEM_LIMIT),
        name="input_grad",
    )(hidden, gain, resgrad, *parts)


def body(
    hidden,
    lengths,
    expert_ids,
    pair_keep,
    attn_gain,
    query_weight_matrix,
    key_weight_matrix,
    value_weight_matrix,
    attention_output_weight,
    moe_gain,
    router_weight_matrix,
    w_gate_up,
    w_down,
    out_grad,
):
    seqs, span, width = hidden.shape
    rows = seqs * span
    top_k = expert_ids.shape[2]
    ep = lax.axis_size("ep")
    dp = lax.axis_size("dp")
    zs, ys, _ = ep_shape(ep)
    place = 2 * ys
    me = lax.axis_index("ep").astype(jnp.int32)
    expert_count = w_gate_up.shape[0] * ep
    capacity = max(2, rows * top_k // expert_count)
    cap = -(-capacity // 16) * 16
    heads = query_weight_matrix.shape[1] // HD
    kv_heads = key_weight_matrix.shape[1] // HD
    replicas = ep // heads
    total = span * ep
    own_rows = query_weight_matrix.shape[0]
    hidden = hidden.reshape(rows, width)
    out_grad = out_grad.reshape(rows, width)

    def per_head(weight, count):
        split = weight.reshape(own_rows, count, HD).transpose(1, 0, 2)
        return jnp.repeat(split, heads // count, axis=0)

    small = jnp.concatenate(
        [router_weight_matrix, attn_gain[:, None], moe_gain[:, None]], axis=1
    )
    small = jnp.pad(small, ((0, 0), (0, PACK - 3 * HD - small.shape[1])))
    packed = jnp.concatenate(
        [
            per_head(query_weight_matrix, heads),
            per_head(key_weight_matrix, kv_heads),
            per_head(value_weight_matrix, kv_heads),
            jnp.broadcast_to(small[None], (heads,) + small.shape),
        ],
        axis=2,
    )
    packed = jnp.repeat(packed, replicas, axis=0)
    packed = jnp.broadcast_to(packed[None], (dp,) + packed.shape).reshape(
        dp * ep, own_rows, PACK
    )
    packed = lax.all_to_all(packed, ("dp", "ep"), split_axis=0, concat_axis=0, tiled=True)
    head_w = packed.reshape(dp * ep * own_rows, PACK)
    at = 3 * HD
    wr = jnp.pad(head_w[:, at : at + expert_count], ((0, 0), (0, LANES - expert_count)))
    gains = head_w[:, at + expert_count : at + expert_count + 2].astype(f32)
    gain_one = gains[:, 0].reshape(1, width)
    gain_two = gains[:, 1].reshape(1, width)
    head_w = jnp.where(jnp.arange(PACK)[None, :] < at, head_w, jnp.zeros((), bf16))

    positions = me * span + jnp.arange(span, dtype=jnp.int32)
    is_valid = positions[None, :] < lengths[:, None]
    expert_range = jnp.arange(LANES, dtype=jnp.int32)
    hit = expert_ids[..., None] == expert_range
    chosen = jnp.any(hit, axis=2).reshape(rows, LANES).astype(f32)
    live = jnp.any(hit & (pair_keep[..., None] > 0), axis=2) & is_valid[..., None]
    live = live.reshape(rows, LANES).astype(bf16)
    earlier = jnp.arange(rows)[:, None] > jnp.arange(rows)[None, :]
    slot = jnp.dot(earlier.astype(bf16), live, preferred_element_type=f32)
    code = jnp.where((slot < capacity) & (live > 0), slot + 1.0, -chosen)
    code_rows = -(-expert_count // 16) * 16
    lines = jnp.pad(code[:, 0:code_rows].T.astype(bf16), ((0, 0), (0, width - rows)))
    lifted = jnp.concatenate([out_grad, lines])

    rates = theta_base ** (-2.0 * jnp.arange(HD // 2, dtype=f32) / HD)
    angle = jnp.arange(total, dtype=jnp.int32).astype(f32)[:, None] * rates[None, :]
    cos = jnp.tile(jnp.cos(angle), (1, 4))
    sin = jnp.sin(angle)
    sin = jnp.concatenate([-sin, sin, -sin, sin], axis=1)
    core = me % 2
    col = (me // 2) % ys
    plane = me // place
    planes = (plane + jnp.arange(zs, dtype=jnp.int32)) % zs
    rows_at = (col + jnp.arange(ys, dtype=jnp.int32)) % ys
    places = jnp.concatenate([rows_at * 2 + core, rows_at * 2 + 1 - core])
    replica = me % replicas if replicas > 1 else jnp.zeros((), jnp.int32)
    attend_meta = jnp.concatenate([lengths, replica[None], planes, places]).astype(jnp.int32)
    expert_meta = jnp.concatenate([jnp.stack([me, plane]), places]).astype(jnp.int32)
    project_meta = expert_meta[1:]
    turn_meta = jnp.concatenate([lengths, (me * span)[None]]).astype(jnp.int32)

    order = list(range(zs))

    def move(x, sender=False, **offset):
        return lax.ppermute(x, "ep", (send_to if sender else fetch_from)(ep, **offset))

    def steps(t):
        n = len(order)
        return t < n - 1, t < n, 1 <= t <= n, 2 <= t < n + 2

    columns, near, far, carried, x = [hidden], {}, {}, None, hidden
    wo_part = [attention_output_weight]
    for t in range(len(order) + 2):
        on_z, on_y, on_core, on_work = steps(t)
        z_new = [move(columns[t], dz=1)] if on_z else []
        y_new = [move(columns[t], dy=k) for k in range(1, ys)] if on_y else []
        c_new = [move(block, dc=1) for block in near[t - 1]] if on_core else []
        if on_work:
            d = order[t - 2]
            carried = project(
                project_meta, near[t - 2] + far[t - 2], head_w, gain_one, cos, sin, zs, d, carried
            )
        block = wo_part[0]
        wo_new = []
        if t == zs - 1:
            wo_new = [move(block, dz=k) for k in range(1, zs)]
        elif t == zs:
            wo_new = [move(block, dy=k) for k in range(1, ys)]
        x, columns, near, far, z_new, y_new, c_new, carried, wo_part, wo_new = phase_tree(
            x, columns, near, far, z_new, y_new, c_new, carried, wo_part, wo_new
        )
        if wo_new:
            wo_part = [jnp.stack(wo_part + wo_new)]
        columns = columns + z_new
        if on_y:
            near[t] = [columns[t]] + y_new
        if on_core:
            far[t - 1] = c_new
        if t == 2:
            upstream = lax.all_gather(phase(lifted, columns[-1])[0], "ep", axis=0)
    wo_new = [
        lax.ppermute(wo_part[0], "dp", [((i + k) % dp, i) for i in range(dp)]) for k in range(1, dp)
    ]
    normed_all, qkv = carried
    made, qk, v, qkt, stat = attend(attend_meta, qkv, seqs, replicas)
    made, wo_new, wo_part = phase_tree(made, wo_new, wo_part)
    recv = lax.all_to_all(made, "ep", split_axis=0, concat_axis=0, tiled=True)
    wo_part = jnp.stack(wo_part + wo_new)
    wo_part = [jnp.stack([wo_part, move(wo_part, dc=1)])]
    line = jnp.arange(dp * ep, dtype=jnp.int32)
    away = (line % 2 - core) % 2
    away = away * dp + (line // ep - lax.axis_index("dp")) % dp
    away = away * ys + ((line // 2) % ys - col) % ys
    away = away * zs + ((line // place) % zs - plane) % zs
    wo = wo_part[0].reshape(dp * ep, own_rows, width)
    wo = jnp.take(wo, away, axis=0, mode="clip").reshape(heads * HD, width)
    if replicas > 1:
        recv = recv.reshape((heads, replicas) + recv.shape[1:]).sum(axis=1).astype(bf16)
    res, pay, mixed, gates = middle(seqs, recv, hidden, wo, gain_two, wr, code)

    count = zs
    columns, near, far, chips, totals = [pay], {}, {}, {}, {}
    outs, carried, extra, passed = {}, None, {}, None
    rings = [[(i, (i + d) % dp) for i in range(dp)] for d in range(1, dp)]
    cuts = ((1,), tuple(range(2, zs)), (0,))

    def hop(value):
        return lax.ppermute(value, "ep", fetch_from(ep, dz=1))

    def swap(piece):
        return [lax.ppermute(piece, "dp", ring) for ring in rings]

    for t in range(count + 5):
        on_z, on_y, on_core, on_work = steps(t)
        z_new = [move(columns[t], dz=1)] if on_z else []
        y_new = [move(columns[t], dy=k) for k in range(1, ys)] if on_y else []
        c_new = [move(block, dc=1) for block in near[t - 1]] if on_core else []
        rc, ry, rz = t - 3, t - 4, t - 5
        rc_new = [move(outs[rc][1], True, dc=1)] if 0 <= rc < count else []
        ry_new = [move(chips[ry][d], True, dy=d) for d in range(1, ys)] if 0 <= ry < count else []
        rz_new = []
        if 1 <= rz < count:
            rz_new = [hop(totals[rz] if rz == 1 else add_low(totals[rz], passed))]
        new = {}
        if on_work:
            d = order[t - 2]
            out = experts(
                expert_meta,
                near[t - 2] + far[t - 2],
                upstream,
                w_gate_up[0],
                w_down[0],
                wr,
                cap,
                zs,
                d,
                carried,
            )
            outs[t - 2], carried = out[:2], out[2:]
        if t == count + 2:
            new["got"] = move(carried[1], True, dc=1)
            new["grads"] = list(expert_grads(carried[2], carried[5], carried[4], carried[3]))
        if t == count + 3:
            new["chip"] = [
                [
                    add_low(
                        jnp.stack([carried[0][k, d] for k in cut]),
                        jnp.stack([extra["got"][k, d] for k in cut]),
                    )
                    for cut in cuts
                    if cut
                ]
                for d in range(ys)
            ]
        if t == count + 4:
            new["swap"] = swap(extra["grads"][0])
            new["first"] = [move(extra["chip"][d][0], True, dy=d) for d in range(1, ys)]
        state = (pay, columns, near, far, outs, chips, totals, carried, extra)
        state = phase_tree(state, z_new, y_new, c_new, rc_new, ry_new, rz_new, new)
        state, z_new, y_new, c_new, rc_new, ry_new, rz_new, new = state
        pay, columns, near, far, outs, chips, totals, carried, extra = state
        columns = columns + z_new
        if on_y:
            near[t] = [columns[t]] + y_new
        if on_core:
            far[t - 1] = c_new
        if rc_new:
            chips[rc] = [add_low(outs[rc][0][d], rc_new[0][d]) for d in range(ys)]
        if 0 <= ry < count:
            totals[ry] = add_low(chips[ry][0], *ry_new)
        if rz_new:
            passed = rz_new[0]
        extra.update(new)
    parts = [totals[0]] + ([passed] if zs > 1 else [])
    moe_chip = extra["chip"]
    grads_low = extra["grads"]

    res_grad, branch, grads, logit_grad, gain_two_grad = turn(
        turn_meta, seqs, parts, res, out_grad, gates, code, wr, gain_two, wo
    )
    if replicas > 1:
        grads = jnp.repeat(grads, replicas, axis=0)
    grads = lax.all_to_all(grads, "ep", split_axis=0, concat_axis=0, tiled=True)
    late = late_grads(expert_count, mixed, branch, pay, logit_grad, gain_two_grad)
    late = late.reshape(dp, zs * ys, 2, own_rows, late.shape[1])

    def stage_parts(value, axis, here_at, size):
        return [
            lax.dynamic_index_in_dim(value, (here_at + d) % size, axis, keepdims=False)
            for d in range(size)
        ]

    late_parts = stage_parts(late, 2, core, 2)
    moe = [add_low(moe_chip[0][0], *extra["first"])]
    moe_new = [move(moe_chip[d][1], True, dy=d) for d in range(1, ys)]
    grads_moved = [extra["swap"], swap(grads_low[1])]
    state = (grads, moe, moe_new, moe_chip, late_parts, grads_low, grads_moved)
    grads, moe, moe_new, moe_chip, late_parts, grads_low, grads_moved = phase_tree(*state)
    moe.append(add_low(moe_chip[0][1], *moe_new))

    dqkv = back(attend_meta, grads, qk, v, qkt, stat, cos, sin, qkv.shape, seqs, replicas)
    moe_new = [move(moe_chip[d][2], True, dy=d) for d in range(1, ys)]
    passed = hop(moe[0][0])
    late_got = [move(late_parts[1], True, dc=1)]
    swapped = swap(grads_low[2])
    state = (dqkv, moe, moe_new, passed, moe_chip, late_parts, late_got, grads_low, swapped)
    state = phase_tree(*state)
    dqkv, moe, moe_new, passed, moe_chip, late_parts, late_got, grads_low, swapped = state
    moe.append(add_low(moe_chip[0][2], *moe_new))
    grads_moved.append(swapped)
    late = add_low(late_parts[0], *late_got)
    late_parts = stage_parts(late, 0, lax.axis_index("dp"), dp)
    late_got = [lax.ppermute(part, "dp", ring) for part, ring in zip(late_parts[1:], rings)]

    halves = ((1, 2), (3, 0)) if zs == 4 else (tuple(range(1, zs)), (0,))
    turn_order = [d for half in halves for d in half]
    near, far = ([part] for part in spread(dqkv, head_w, halves[0]))
    near, far, dqkv = phase_tree(near, far, dqkv)

    got = [move(far[0], True, dc=1)]
    more = spread(dqkv, head_w, halves[1])
    near.append(more[0])
    far.append(more[1])
    passed = hop(add_low(moe[1][0], passed))
    head_grad = head_grads(dqkv, normed_all).reshape(dp * ep, own_rows, PACK)
    state = (near, far, got, moe, passed, head_grad, late_parts, late_got, grads_low)
    near, far, got, moe, passed, head_grad, late_parts, late_got, grads_low = phase_tree(*state)
    late = add_low(late_parts[0], *late_got)
    plane_groups = [[c + 2 * k for k in range(zs * ys)] for c in range(2)]
    late = lax.all_to_all(
        late, "ep", split_axis=0, concat_axis=0, tiled=True, axis_index_groups=plane_groups
    )

    head_grad = lax.all_to_all(head_grad, ("dp", "ep"), split_axis=0, concat_axis=0, tiled=True)
    totals, received = {}, None

    def chip_of(d):
        half = 0 if d in halves[0] else 1
        at = halves[half].index(d)
        return [add_low(near[half][at, y], got[half][at, y]) for y in range(ys)]

    chip = chip_of(turn_order[0])
    for k, d in enumerate(turn_order):
        ahead = chip_of(turn_order[k + 1]) if k + 1 < len(turn_order) else []
        moved = [move(chip[y], True, dy=y) for y in range(1, ys)]
        if k:
            last = totals[turn_order[k - 1]]
            received = hop(last if k == 1 else add_low(last, received))
        if k == 0:
            got.append(move(far[1], True, dc=1))
            passed = hop(add_low(moe[1][1], passed)) if zs == 4 else passed
            swapped = swap(grads_low[3])
            near, got, chip, ahead, moved, passed, swapped = phase_tree(
                near, got, chip, ahead, moved, passed, swapped
            )
            grads_moved.append(swapped)
        elif k == 2:
            near, got, chip, ahead, moved, received, totals, head_grad = phase_tree(
                near, got, chip, ahead, moved, received, totals, head_grad
            )
        else:
            near, got, chip, ahead, moved, received, totals = phase_tree(
                near, got, chip, ahead, moved, received, totals
            )
        totals[d] = add_low(chip[0], *moved)
        chip = ahead
    parts = [totals[0], received]
    late = phase(late, totals[0], received)[0]
    late = late.astype(f32).sum(axis=0)
    mparts = [moe[-1][0], passed]
    sums = []
    for own, moved in zip(grads_low, grads_moved):
        piece = own.astype(f32)
        for other in moved:
            piece = piece + other.astype(f32)
        sums.append(piece)
    grads_total = jnp.concatenate(sums)
    gu_total = grads_total[0:width]
    d_total = grads_total[width:]

    head_grad = head_grad.astype(f32).reshape(dp, heads, replicas, own_rows, PACK).sum(axis=(0, 2))

    def rows_of(part, count):
        part = part.reshape(count, heads // count, own_rows, HD).sum(axis=1)
        return part.transpose(1, 0, 2).reshape(own_rows, count * HD)

    query_w_grad = rows_of(head_grad[..., 0:HD], heads)
    key_w_grad = rows_of(head_grad[..., HD : 2 * HD], kv_heads)
    value_w_grad = rows_of(head_grad[..., 2 * HD : 3 * HD], kv_heads)
    gain_one_grad = (
        jnp.sum(query_w_grad * query_weight_matrix.astype(f32), axis=1)
        + jnp.sum(key_w_grad * key_weight_matrix.astype(f32), axis=1)
        + jnp.sum(value_w_grad * value_weight_matrix.astype(f32), axis=1)
    ) / attn_gain.astype(f32)

    moe_own = res
    for part in mparts:
        moe_own = moe_own + part.astype(f32)
    output = jnp.where(
        is_valid[..., None], moe_own.reshape(seqs, span, width), 0.0
    ).astype(bf16)
    input_grad = finish(hidden, gain_one, res_grad, parts)
    model = width
    return (
        output,
        input_grad.reshape(seqs, span, width),
        gain_one_grad,
        query_w_grad,
        key_w_grad,
        value_w_grad,
        late[:, 0:model],
        late[:, model + expert_count],
        late[:, model : model + expert_count],
        gu_total[None],
        d_total[None],
    )


def solution(mesh):
    return jax.shard_map(
        body,
        mesh=mesh,
        in_specs=(
            P("dp", "ep", None),
            P("dp"),
            P("dp", "ep", None),
            P("dp", "ep", None),
            P(("dp", "ep")),
            P(("dp", "ep"), None),
            P(("dp", "ep"), None),
            P(("dp", "ep"), None),
            P(("dp", "ep"), None),
            P(("dp", "ep")),
            P(("dp", "ep"), None),
            P("ep", None, None),
            P("ep", None, None),
            P("dp", "ep", None),
        ),
        out_specs=(
            P("dp", "ep", None),
            P("dp", "ep", None),
            P(("dp", "ep")),
            P(("dp", "ep"), None),
            P(("dp", "ep"), None),
            P(("dp", "ep"), None),
            P(("dp", "ep"), None),
            P(("dp", "ep")),
            P(("dp", "ep"), None),
            P("ep", None, None),
            P("ep", None, None),
        ),
        check_vma=False,
    )
```

```python
import functools

import jax
import jax.numpy as jnp
from jax import lax
from jax.experimental import pallas as pl
from jax.experimental.pallas import tpu as pltpu
from jax.sharding import PartitionSpec as P

HD = 64
LANES = 128
SLAB = 256
WIDE = 512
PACK = 256
eps = 1e-05
theta_base = 10000.0
f32 = jnp.float32
bf16 = jnp.bfloat16
VMEM_LIMIT = 56 * 1024 * 1024


def dot(a, b):
    return lax.dot_general(a, b, (((1,), (0,)), ((), ())), preferred_element_type=f32)


def dot_nt(a, b):
    return lax.dot_general(a, b, (((1,), (1,)), ((), ())), preferred_element_type=f32)


def dot_tn(a, b):
    return lax.dot_general(a, b, (((0,), (0,)), ((), ())), preferred_element_type=f32)


def lanes_of(rows, width=LANES):
    return lax.broadcasted_iota(jnp.int32, (rows, width), 1)


def half_swap(x):
    lane = lanes_of(x.shape[0])
    return jnp.where(lane % HD < HD // 2, pltpu.roll(x, LANES - HD // 2, 1), pltpu.roll(x, HD // 2, 1))


def ep_shape(ep):
    zs = 4 if ep % 8 == 0 else 1
    return zs, ep // (2 * zs), 2


def fetch_from(ep, dz=0, dy=0, dc=0):
    zs, ys, cs = ep_shape(ep)
    pairs = []
    for z in range(zs):
        for y in range(ys):
            for c in range(cs):
                src = (((z + dz) % zs) * ys + (y + dy) % ys) * cs + (c + dc) % cs
                pairs.append((src, (z * ys + y) * cs + c))
    return pairs


def send_to(ep, **offset):
    return [(dst, src) for src, dst in fetch_from(ep, **offset)]


def phase(*values):
    return lax.optimization_barrier(values)


def phase_tree(*values):
    flat, tree = jax.tree.flatten(values)
    return jax.tree.unflatten(tree, phase(*flat))


def add_low(*parts):
    total = parts[0].astype(f32)
    for part in parts[1:]:
        total = total + part.astype(f32)
    return total.astype(bf16)


def project_kernel(place, carry, meta, *refs):
    blocks = refs[:place]
    w_ref, gain_ref, cos_ref, sin_ref = refs[place : place + 4]
    normed_ref, qkv_ref = refs[-2:]
    rows, _ = blocks[0].shape
    span = cos_ref.shape[0] // place
    seqs = rows // span
    lane = lanes_of(rows)
    for j in range(place):
        x = blocks[j][...].astype(f32)
        scale = lax.rsqrt(jnp.mean(x * x, axis=-1, keepdims=True) + eps)
        normed = (x * scale * gain_ref[...]).astype(bf16)
        normed_ref[0, j] = normed
        raw = dot(normed, w_ref[...])
        at = pl.ds(pl.multiple_of(meta[1 + j] * span, 32), span)
        cos = jnp.concatenate([cos_ref[at, :]] * seqs, axis=0)
        sin = jnp.concatenate([sin_ref[at, :]] * seqs, axis=0)
        both = raw[:, 0:LANES]
        both = (both * cos + half_swap(both) * sin).astype(bf16).astype(f32)
        both = jnp.where(lane < HD, both * HD ** (-0.5), both)
        qkv_ref[0, j, :, 0:LANES] = both.astype(bf16)
        qkv_ref[0, j, :, LANES:PACK] = jnp.where(lane < HD, raw[:, LANES:PACK], 0.0).astype(bf16)


def project(meta, blocks, w, gain, cos, sin, zs, dz, carried):
    rows, width = blocks[0].shape
    place = len(blocks)
    span = cos.shape[0] // (zs * place)

    def whole(a):
        return pl.BlockSpec(a.shape, lambda i, m: (0,) * a.ndim)

    table = pl.BlockSpec((place * span, LANES), lambda i, m: (lax.rem(m[0] + dz, zs), 0))
    args = list(blocks) + [w, gain, cos, sin]
    in_specs = [whole(a) for a in blocks] + [whole(w), whole(gain), table, table]
    aliases = {}
    if carried is not None:
        aliases = {1 + len(args): 0, 2 + len(args): 1}
        args += list(carried)
        in_specs += [pl.BlockSpec(memory_space=pl.ANY)] * 2
    return pl.pallas_call(
        functools.partial(project_kernel, place, carried is not None),
        grid_spec=pltpu.PrefetchScalarGridSpec(
            num_scalar_prefetch=1,
            grid=(1,),
            in_specs=in_specs,
            out_specs=(
                pl.BlockSpec((1, place, rows, width), lambda i, m: (dz, 0, 0, 0)),
                pl.BlockSpec((1, place, rows, PACK), lambda i, m: (dz, 0, 0, 0)),
            ),
        ),
        out_shape=(
            jax.ShapeDtypeStruct((zs, place, rows, width), bf16),
            jax.ShapeDtypeStruct((zs, place, rows, PACK), bf16),
        ),
        input_output_aliases=aliases,
        compiler_params=pltpu.CompilerParams(vmem_limit_bytes=VMEM_LIMIT),
        cost_estimate=pl.CostEstimate(
            flops=2 * place * rows * width * PACK,
            bytes_accessed=4 * place * rows * width,
            transcendentals=0,
        ),
        name="project_in",
    )(meta, *args)


def attend_kernel(
    replicas,
    meta,
    qkv_ref,
    out_ref,
    qk_ref,
    v_ref,
    qkt_ref,
    stat_ref,
    vt_ref,
    wide_ref,
):
    zs, place, rows, _ = qkv_ref.shape
    total = qk_ref.shape[1]
    span = total // (zs * place)
    s = pl.program_id(0)
    seqs = rows // span
    source = pl.ds(pl.multiple_of(s * span, 32), span)
    for d in range(zs):
        for j in range(place):
            at = pl.multiple_of((meta[seqs + 1 + d] * place + meta[seqs + 1 + zs + j]) * span, 32)
            qk_ref[0, pl.ds(at, span), :] = qkv_ref[d, j, source, 0:LANES]
            v_ref[0, pl.ds(at, span), :] = qkv_ref[d, j, source, LANES:PACK]
    for lo in range(0, total, SLAB):
        at = slice(lo, lo + SLAB)
        qkt_ref[0, :, at] = qk_ref[0, at, :].astype(f32).T.astype(bf16)
        vt_ref[:, at] = v_ref[0, at, :].astype(f32).T.astype(bf16)

    key_row = lax.broadcasted_iota(jnp.int32, (WIDE, WIDE), 0)
    query_col = lax.broadcasted_iota(jnp.int32, (WIDE, WIDE), 1)

    def one_slab(lo):
        hi = lo + WIDE
        qt = qkt_ref[0, 0:HD, lo:hi]
        diag = dot(qk_ref[0, lo:hi, HD:LANES], qt)
        diag = jnp.where(key_row <= query_col, diag, -jnp.inf)
        top = jnp.max(diag, axis=0, keepdims=True)
        if lo:
            full = dot(qk_ref[0, 0:lo, HD:LANES], qt)
            top = jnp.maximum(top, jnp.max(full, axis=0, keepdims=True))
        p_diag = jnp.exp(diag - top)
        row_total = jnp.sum(p_diag, axis=0, keepdims=True)
        out = dot(vt_ref[:, lo:hi], p_diag.astype(bf16))
        if lo:
            p_full = jnp.exp(full - top)
            row_total = row_total + jnp.sum(p_full, axis=0, keepdims=True)
            out = out + dot(vt_ref[:, 0:lo], p_full.astype(bf16))
        out = out[0:HD] / row_total
        stat_ref[0, 0:HD, lo:hi] = out
        stat_ref[0, HD : HD + 8, lo:hi] = jnp.broadcast_to(top + jnp.log(row_total), (8, WIDE))
        wide_ref[lo:hi, :] = jnp.concatenate([out, out], axis=0).T

    def no_slab(lo):
        stat_ref[0, :, lo : lo + WIDE] = jnp.zeros((HD + 8, WIDE), f32)
        wide_ref[lo : lo + WIDE, :] = jnp.zeros((WIDE, LANES), f32)

    for i, lo in enumerate(range(0, total, WIDE)):
        if replicas > 1:
            mine = meta[seqs] == i % replicas
            pl.when(mine)(functools.partial(one_slab, lo))
            pl.when(jnp.logical_not(mine))(functools.partial(no_slab, lo))
        else:
            one_slab(lo)

    half = span // 2
    for e in range(total // span):
        upper = wide_ref[e * span : e * span + half, :]
        lower = wide_ref[e * span + half : (e + 1) * span, :]
        out_ref[e] = jnp.where(lanes_of(half) < HD, upper, lower).astype(bf16)


def attend(meta, qkv, seqs, replicas):
    zs, place, rows, _ = qkv.shape
    span = rows // seqs
    total = zs * place * span
    return pl.pallas_call(
        functools.partial(attend_kernel, replicas),
        grid=(seqs,),
        out_shape=(
            jax.ShapeDtypeStruct((total // span, seqs * (span // 2), LANES), bf16),
            jax.ShapeDtypeStruct((seqs, total, LANES), bf16),
            jax.ShapeDtypeStruct((seqs, total, LANES), bf16),
            jax.ShapeDtypeStruct((seqs, LANES, total), bf16),
            jax.ShapeDtypeStruct((seqs, HD + 8, total), f32),
        ),
        in_specs=[
            pl.BlockSpec(memory_space=pltpu.SMEM),
            pl.BlockSpec(qkv.shape, lambda s: (0, 0, 0, 0)),
        ],
        out_specs=(
            pl.BlockSpec((total // span, span // 2, LANES), lambda s: (0, s, 0)),
            pl.BlockSpec((1, total, LANES), lambda s: (s, 0, 0)),
            pl.BlockSpec((1, total, LANES), lambda s: (s, 0, 0)),
            pl.BlockSpec((1, LANES, total), lambda s: (s, 0, 0)),
            pl.BlockSpec((1, HD + 8, total), lambda s: (s, 0, 0)),
        ),
        scratch_shapes=[pltpu.VMEM((LANES, total), bf16), pltpu.VMEM((total, LANES), f32)],
        compiler_params=pltpu.CompilerParams(vmem_limit_bytes=VMEM_LIMIT),
        cost_estimate=pl.CostEstimate(
            flops=4 * seqs * total * total * LANES,
            bytes_accessed=4 * seqs * total * PACK,
            transcendentals=seqs * total * total // 2,
        ),
        name="attend_forward",
    )(meta, qkv)


def gates_of(normed, wr_ref, code):
    logits = jnp.where(code != 0, dot(normed, wr_ref[...]), -1e30)
    powers = jnp.exp(logits - jnp.max(logits, axis=-1, keepdims=True))
    return powers / jnp.sum(powers, axis=-1, keepdims=True)


def middle_kernel(
    seqs,
    recv_ref,
    hid_ref,
    wo_ref,
    gain_ref,
    wr_ref,
    code_ref,
    res_ref,
    pay_ref,
    mixed_ref,
    gate_ref,
):
    heads, half_rows, _ = recv_ref.shape
    width = hid_ref.shape[1]
    half = half_rows // seqs
    low = lanes_of(half_rows) < HD
    uppers, lowers = [], []
    for j in range(heads // 2):
        a = recv_ref[2 * j].astype(f32)
        b = recv_ref[2 * j + 1].astype(f32)
        uppers.append(jnp.where(low, a, pltpu.roll(b, HD, 1)).astype(bf16))
        lowers.append(jnp.where(low, pltpu.roll(a, HD, 1), b).astype(bf16))
    upper = jnp.concatenate(uppers, axis=1)
    lower = jnp.concatenate(lowers, axis=1)
    pieces = []
    for s in range(seqs):
        pieces += [upper[s * half : (s + 1) * half], lower[s * half : (s + 1) * half]]
    mixed = jnp.concatenate(pieces, axis=0)
    mixed_ref[...] = mixed
    res = hid_ref[...].astype(f32) + dot(mixed, wo_ref[...])
    res_ref[...] = res
    scale = lax.rsqrt(jnp.mean(res * res, axis=-1, keepdims=True) + eps)
    normed = (res * scale * gain_ref[...]).astype(bf16)
    gate_ref[...] = gates_of(normed, wr_ref, code_ref[...])
    pay_ref[...] = normed


def middle(seqs, recv, hid, wo, gain, wr, code):
    rows, width = hid.shape
    vmem = pl.BlockSpec(memory_space=pltpu.VMEM)
    return pl.pallas_call(
        functools.partial(middle_kernel, seqs),
        out_shape=(
            jax.ShapeDtypeStruct((rows, width), f32),
            jax.ShapeDtypeStruct((rows, width), bf16),
            jax.ShapeDtypeStruct((rows, width), bf16),
            jax.ShapeDtypeStruct((rows, LANES), f32),
        ),
        in_specs=[vmem] * 6,
        out_specs=(vmem,) * 4,
        compiler_params=pltpu.CompilerParams(vmem_limit_bytes=VMEM_LIMIT),
        cost_estimate=pl.CostEstimate(
            flops=4 * rows * width * width, bytes_accessed=4 * width * width, transcendentals=0
        ),
        name="project_out",
    )(recv, hid, wo, gain, wr, code)


def expert_kernel(place, cap, zs, dz, first, meta, *refs):
    pay_in = refs[0:place]
    up_in, wgu_in, wd_in, wr_ref = refs[place : place + 4]
    rest = refs[place + 4 + (0 if first else 6) :]
    near_out, far_out, mnear_out, mfar_out, x_out, pg_out, act_out, both_out = rest[:8]
    pay, up, code, wgu, wd, back_s, moe_s, x_s, pg_s, act_s, both_s, in_sem, out_sem = rest[8:]
    rows, width = pay_in[0].shape
    units = wd.shape[0]
    halves = place // 2
    expert = meta[0]
    plane = lax.rem(meta[1] + dz, zs)
    loads = {}
    order = []
    for j in range(place):
        loads["p", j] = pltpu.make_async_copy(pay_in[j], pay.at[j], in_sem.at[2 * j])
        source = up_in.at[plane * place + meta[2 + j]]
        loads["u", j] = pltpu.make_async_copy(
            source.at[pl.ds(0, rows)], up.at[j], in_sem.at[2 * j + 1]
        )
        loads["c", j] = pltpu.make_async_copy(
            source.at[pl.ds(rows, code.shape[1]), pl.ds(0, code.shape[2])],
            code.at[j],
            in_sem.at[2 * place + 2 + j],
        )
    loads["gu"] = pltpu.make_async_copy(wgu_in, wgu, in_sem.at[2 * place])
    loads["d"] = pltpu.make_async_copy(wd_in, wd, in_sem.at[2 * place + 1])
    order = [("c", j) for j in range(place)]
    order += [("p", j) for j in range(halves)] + ["gu", "d"]
    order += [("u", j) for j in range(halves)]
    order += [("p", j) for j in range(halves, place)] + [("u", j) for j in range(halves, place)]
    for key in order:
        loads[key].start()
    stores = []

    def store(src, dst):
        copy = pltpu.make_async_copy(src, dst, out_sem.at[len(stores)])
        copy.start()
        stores.append(copy)

    def save(h, value, buf, out):
        own = pl.ds(h * halves * cap, halves * cap)
        buf[own, :] = value
        store(buf.at[own], out.at[dz, own])

    lane = lanes_of(rows)
    slot_row = lax.broadcasted_iota(jnp.int32, (cap, rows), 0)
    slot_col = lax.broadcasted_iota(jnp.int32, (rows, cap), 1)
    code_row = lax.broadcasted_iota(jnp.int32, (code.shape[1], rows), 0)
    cap_lane = lanes_of(cap)
    line_row = lax.broadcasted_iota(jnp.int32, code.shape[1:], 0)
    slot_wide = lax.broadcasted_iota(jnp.int32, (cap, code.shape[2]), 0)
    for h in range(2):
        mine = range(h * halves, (h + 1) * halves)
        for j in mine:
            loads["c", j].wait()
            loads["p", j].wait()
        outs_of, xs, gates = [], [], []
        into, into_wide = [], []
        for j in mine:
            lines = code[j].astype(f32)
            blank = jnp.zeros((LANES - lines.shape[0], lines.shape[1]), f32)
            codes = jnp.concatenate([lines, blank], axis=0).T[0:rows]
            column = jnp.sum(jnp.where(lane == expert, codes, 0.0), axis=1, keepdims=True)
            line = jnp.sum(
                jnp.where(code_row == expert, lines[:, 0:rows], 0.0), axis=0, keepdims=True
            )
            into.append(jnp.where(line.astype(jnp.int32) == slot_row + 1, 1.0, 0.0).astype(bf16))
            line = jnp.sum(jnp.where(line_row == expert, lines, 0.0), axis=0, keepdims=True)
            into_wide.append(
                jnp.where(line.astype(jnp.int32) == slot_wide + 1, 1.0, 0.0).astype(bf16)
            )
            outs_of.append(
                jnp.where(column.astype(jnp.int32) == slot_col + 1, 1.0, 0.0).astype(bf16)
            )
            xs.append(dot(into[-1], pay[j]).astype(bf16))
            gate = gates_of(xs[-1], wr_ref, dot(into[-1], codes.astype(bf16)))
            gates.append(jnp.sum(jnp.where(cap_lane == expert, gate, 0.0), axis=1, keepdims=True))
        x = jnp.concatenate(xs, axis=0)
        gate_prob = jnp.concatenate(gates, axis=0)
        if h == 0:
            loads["gu"].wait()
        save(h, x, x_s, x_out)
        gate_up = dot(x, wgu[...])
        gate = gate_up[:, 0:units]
        high = gate_up[:, units:]
        sig = jax.nn.sigmoid(gate)
        silu = gate * sig
        act = (silu * high).astype(bf16)
        if h == 0:
            loads["d"].wait()
        save(h, act, act_s, act_out)
        made = dot(act, wd[...]).astype(bf16).astype(f32)
        for j in mine:
            loads["u", j].wait()
        upstream = jnp.concatenate([dot(into[k], up[j]) for k, j in enumerate(mine)], axis=0)
        gate_grad = jnp.sum(made * upstream, axis=-1, keepdims=True)
        moe = (made * gate_prob).astype(bf16)
        pair_grad = (upstream * gate_prob).astype(bf16)
        for k, j in enumerate(mine):
            part = slice(k * cap, (k + 1) * cap)
            moe_s[j] = dot(outs_of[k], moe[part]).astype(bf16)
        store(moe_s.at[pl.ds(h * halves, halves)], (mnear_out if h == 0 else mfar_out).at[dz])
        save(h, pair_grad, pg_s, pg_out)
        act_grad = dot_nt(pair_grad, wd[...])
        both = jnp.concatenate(
            [act_grad * high * (sig * (1.0 + gate * (1.0 - sig))), act_grad * silu], axis=1
        ).astype(bf16)
        save(h, both, both_s, both_out)
        back = dot_nt(both, wgu[...]).astype(bf16)
        upper = gate_grad.astype(bf16).astype(f32)
        pair_lane = lanes_of(halves * cap)
        pair = jnp.where(pair_lane == 0, upper, gate_grad - upper)
        for k, j in enumerate(mine):
            part = slice(k * cap, (k + 1) * cap)
            back_s[j, 0:rows, :] = dot(outs_of[k], back[part]).astype(bf16)
            found = dot(pair[part].T[0:16].astype(bf16), into_wide[k])
            back_s[j, rows:, :] = jnp.zeros((code.shape[1], width), bf16)
            for row, at in ((0, 0), (1, width // 2)):
                value = jnp.where(line_row == expert, found[row : row + 1], 0.0)
                back_s[j, rows:, at : at + code.shape[2]] = value.astype(bf16)
        store(back_s.at[pl.ds(h * halves, halves)], near_out if h == 0 else far_out)
    for copy in stores:
        copy.wait()


def experts(meta, pays, upstream, wgu, wd, wr, cap, zs, dz, carried):
    place = len(pays)
    rows, width = pays[0].shape
    units = wd.shape[0]
    first = carried is None
    anyspace = pl.BlockSpec(memory_space=pl.ANY)
    args = list(pays) + [upstream, wgu, wd, wr]
    code_rows = upstream.shape[1] - rows
    aliases = {}
    if not first:
        aliases = {1 + len(args) + k: 2 + k for k in range(6)}
        args += list(carried)
    half = jax.ShapeDtypeStruct((place // 2, rows + code_rows, width), bf16)
    slots = place * cap
    return pl.pallas_call(
        functools.partial(expert_kernel, place, cap, zs, dz, first),
        out_shape=(
            half,
            half,
            jax.ShapeDtypeStruct((zs, place // 2, rows, width), bf16),
            jax.ShapeDtypeStruct((zs, place // 2, rows, width), bf16),
            jax.ShapeDtypeStruct((zs, slots, width), bf16),
            jax.ShapeDtypeStruct((zs, slots, width), bf16),
            jax.ShapeDtypeStruct((zs, slots, units), bf16),
            jax.ShapeDtypeStruct((zs, slots, 2 * units), bf16),
        ),
        in_specs=[pl.BlockSpec(memory_space=pltpu.SMEM)]
        + [anyspace] * (place + 3)
        + [pl.BlockSpec(memory_space=pltpu.VMEM)]
        + [anyspace] * (len(args) - place - 4),
        out_specs=(anyspace,) * 8,
        scratch_shapes=[
            pltpu.VMEM((place, rows, width), bf16),
            pltpu.VMEM((place, rows, width), bf16),
            pltpu.VMEM((place, code_rows, -(-rows // LANES) * LANES), bf16),
            pltpu.VMEM(wgu.shape, bf16),
            pltpu.VMEM(wd.shape, bf16),
            pltpu.VMEM((place, rows + code_rows, width), bf16),
            pltpu.VMEM((place, rows, width), bf16),
            pltpu.VMEM((slots, width), bf16),
            pltpu.VMEM((slots, width), bf16),
            pltpu.VMEM((slots, units), bf16),
            pltpu.VMEM((slots, 2 * units), bf16),
            pltpu.SemaphoreType.DMA((3 * place + 2,)),
            pltpu.SemaphoreType.DMA((12,)),
        ],
        input_output_aliases=aliases,
        compiler_params=pltpu.CompilerParams(vmem_limit_bytes=VMEM_LIMIT),
        cost_estimate=pl.CostEstimate(
            flops=16 * slots * width * units, bytes_accessed=12 * slots * width, transcendentals=0
        ),
        name="experts",
    )(meta, *args)


def turn_kernel(nparts, seqs, meta, *refs):
    parts = refs[:nparts]
    (
        res_ref,
        up_ref,
        gate_ref,
        code_ref,
        wr_ref,
        gain_ref,
        wo_ref,
        resgrad_ref,
        branch_ref,
        out_ref,
        logit_ref,
        gaingrad_ref,
    ) = refs[nparts:]
    rows, width = res_ref.shape
    span = rows // seqs
    total = parts[0][...].astype(f32)
    for part in parts[1:]:
        total = total + part[...].astype(f32)
    held = -(-rows // LANES) * LANES
    lines = total[rows:, 0:held] + total[rows:, width // 2 : width // 2 + held]
    blank = jnp.zeros((LANES - lines.shape[0], held), f32)
    gate_grad = jnp.concatenate([lines, blank], axis=0).T[0:rows]
    gate_grad = jnp.where(code_ref[...] > 0, gate_grad, 0.0)
    gates = gate_ref[...]
    logit_grad = gates * (gate_grad - jnp.sum(gates * gate_grad, axis=-1, keepdims=True))
    logit_ref[...] = logit_grad
    normed_grad = total[0:rows] + lax.dot_general(
        logit_grad,
        wr_ref[...].astype(f32),
        (((1,), (1,)), ((), ())),
        preferred_element_type=f32,
        precision=lax.Precision.HIGHEST,
    )
    res = res_ref[...]
    scale = lax.rsqrt(jnp.mean(res * res, axis=-1, keepdims=True) + eps)
    gaingrad_ref[...] = jnp.sum(normed_grad * (res * scale), axis=0, keepdims=True)
    scaled = normed_grad * gain_ref[...]
    row = meta[seqs] + lax.broadcasted_iota(jnp.int32, (span, 1), 0)
    valid = jnp.concatenate([(row < meta[s]).astype(f32) for s in range(seqs)], axis=0)
    upstream = jnp.where(valid > 0, up_ref[...].astype(f32), 0.0)
    centre = jnp.mean(scaled * res, axis=-1, keepdims=True)
    res_grad = upstream + scaled * scale - res * (scale * scale * scale * centre)
    resgrad_ref[...] = res_grad
    branch = res_grad.astype(bf16)
    branch_ref[...] = branch
    mixed = dot_nt(branch, wo_ref[...]).astype(bf16).astype(f32)
    half = span // 2
    low = lanes_of(half) < HD
    for s in range(seqs):
        at = slice(s * half, (s + 1) * half)
        for j in range(out_ref.shape[0] // 2):
            cols = slice(j * LANES, (j + 1) * LANES)
            upper = mixed[s * span : s * span + half, cols]
            lower = mixed[s * span + half : (s + 1) * span, cols]
            out_ref[2 * j, at] = jnp.where(low, upper, pltpu.roll(lower, HD, 1)).astype(bf16)
            out_ref[2 * j + 1, at] = jnp.where(low, pltpu.roll(upper, HD, 1), lower).astype(bf16)


def turn(meta, seqs, parts, res, up, gates, code, wr, gain, wo):
    rows, width = res.shape
    heads = wo.shape[0] // HD
    vmem = pl.BlockSpec(memory_space=pltpu.VMEM)
    return pl.pallas_call(
        functools.partial(turn_kernel, len(parts), seqs),
        out_shape=(
            jax.ShapeDtypeStruct((rows, width), f32),
            jax.ShapeDtypeStruct((rows, width), bf16),
            jax.ShapeDtypeStruct((heads, rows // 2, LANES), bf16),
            jax.ShapeDtypeStruct((rows, LANES), f32),
            jax.ShapeDtypeStruct((1, width), f32),
        ),
        in_specs=[pl.BlockSpec(memory_space=pltpu.SMEM)] + [vmem] * (len(parts) + 7),
        out_specs=(vmem,) * 5,
        compiler_params=pltpu.CompilerParams(vmem_limit_bytes=VMEM_LIMIT),
        cost_estimate=pl.CostEstimate(
            flops=4 * rows * width * width, bytes_accessed=4 * width * width, transcendentals=0
        ),
        name="turn_back",
    )(meta, *parts, res, up, gates, code, wr, gain, wo)


def back_kernel(
    replicas,
    meta,
    grad_ref,
    qk_ref,
    v_ref,
    qkt_ref,
    stat_ref,
    cos_ref,
    sin_ref,
    out_ref,
    do_ref,
    dk_ref,
    dv_ref,
    dqt_ref,
):
    zs, place, rows, _ = out_ref.shape
    total = qk_ref.shape[1]
    span = total // (zs * place)
    seqs = rows // span
    s = pl.program_id(0)
    half = span // 2
    for e in range(total // span):
        chunk = grad_ref[e].astype(f32)
        do_ref[e * span : e * span + half, :] = chunk
        do_ref[e * span + half : (e + 1) * span, :] = pltpu.roll(chunk, HD, 1)
    dk_ref[...] = jnp.zeros_like(dk_ref)
    dv_ref[...] = jnp.zeros_like(dv_ref)
    key_row = lax.broadcasted_iota(jnp.int32, (SLAB, SLAB), 0)
    query_col = lax.broadcasted_iota(jnp.int32, (SLAB, SLAB), 1)
    def one_slab(lo):
        hi = lo + 2 * SLAB
        mid = lo + SLAB
        grad = do_ref[lo:hi, :]
        grad_low = grad.astype(bf16)
        grad_t = grad.T[0:HD]
        delta = jnp.sum(grad_t * stat_ref[0, 0:HD, lo:hi], axis=0, keepdims=True)
        grad_t = grad_t.astype(bf16)
        log_total = stat_ref[0, HD : HD + 1, lo:hi]

        def piece(start, stop, first, last, masked):
            cols = slice(first - lo, last - lo)
            scores = dot(qk_ref[0, start:stop, HD:LANES], qkt_ref[0, 0:HD, first:last])
            probs = jnp.exp(scores - log_total[:, cols])
            if masked:
                probs = jnp.where(key_row <= query_col, probs, 0.0)
            prob_grad = dot(v_ref[0, start:stop, 0:HD], grad_t[:, cols])
            score_grad = (probs * (prob_grad - delta[:, cols])).astype(bf16)
            dv_ref[start:stop, :] += dot(probs.astype(bf16), grad_low[cols])
            dk_ref[start:stop, :] += dot(score_grad, qk_ref[0, first:last, :])
            return dot(qkt_ref[0, :, start:stop], score_grad)

        moved = piece(lo, mid, lo, mid, True)
        moved_next = piece(mid, hi, mid, hi, True) + piece(lo, mid, mid, hi, False)
        if lo:
            full = piece(0, lo, lo, hi, False)
            moved = moved + full[:, 0:SLAB]
            moved_next = moved_next + full[:, SLAB:]
        dqt_ref[:, lo:mid] = moved
        dqt_ref[:, mid:hi] = moved_next

    def no_slab(lo):
        dqt_ref[:, lo : lo + 2 * SLAB] = jnp.zeros((LANES, 2 * SLAB), f32)

    for i, lo in enumerate(range(0, total, 2 * SLAB)):
        if replicas > 1:
            mine = meta[seqs] == i % replicas
            pl.when(mine)(functools.partial(one_slab, lo))
            pl.when(jnp.logical_not(mine))(functools.partial(no_slab, lo))
        else:
            one_slab(lo)

    low = lanes_of(SLAB) < HD
    for lo in range(0, total, SLAB):
        at = slice(lo, lo + SLAB)
        both = jnp.where(low, dk_ref[at, :], dqt_ref[:, at].T * HD ** (-0.5))
        both = pltpu.roll(both, HD, 1)
        dk_ref[at, :] = both * cos_ref[at, :] - half_swap(both) * sin_ref[at, :]
        dv_ref[at, :] = jnp.where(low, dv_ref[at, :], 0.0)
    dest = pl.ds(pl.multiple_of(s * span, 32), span)
    for d in range(zs):
        for j in range(place):
            at = pl.multiple_of((meta[seqs + 1 + d] * place + meta[seqs + 1 + zs + j]) * span, 32)
            out_ref[d, j, dest, 0:LANES] = dk_ref[pl.ds(at, span), :].astype(bf16)
            out_ref[d, j, dest, LANES:PACK] = dv_ref[pl.ds(at, span), :].astype(bf16)


def back(meta, grads, qk, v, qkt, stat, cos, sin, shape, seqs, replicas):
    total = qk.shape[1]
    span = total // grads.shape[0]
    return pl.pallas_call(
        functools.partial(back_kernel, replicas),
        grid=(seqs,),
        out_shape=jax.ShapeDtypeStruct(shape, bf16),
        in_specs=[
            pl.BlockSpec(memory_space=pltpu.SMEM),
            pl.BlockSpec((total // span, span // 2, LANES), lambda s: (0, s, 0)),
            pl.BlockSpec((1, total, LANES), lambda s: (s, 0, 0)),
            pl.BlockSpec((1, total, LANES), lambda s: (s, 0, 0)),
            pl.BlockSpec((1, LANES, total), lambda s: (s, 0, 0)),
            pl.BlockSpec((1, HD + 8, total), lambda s: (s, 0, 0)),
            pl.BlockSpec((total, LANES), lambda s: (0, 0)),
            pl.BlockSpec((total, LANES), lambda s: (0, 0)),
        ],
        out_specs=pl.BlockSpec(shape, lambda s: (0, 0, 0, 0)),
        scratch_shapes=[
            pltpu.VMEM((total, LANES), f32),
            pltpu.VMEM((total, LANES), f32),
            pltpu.VMEM((total, LANES), f32),
            pltpu.VMEM((LANES, total), f32),
        ],
        compiler_params=pltpu.CompilerParams(vmem_limit_bytes=VMEM_LIMIT),
        cost_estimate=pl.CostEstimate(
            flops=10 * seqs * total * total * LANES,
            bytes_accessed=6 * seqs * total * PACK,
            transcendentals=seqs * total * total // 2,
        ),
        name="attend_backward",
    )(meta, grads, qk, v, qkt, stat, cos, sin)


def expert_grads_kernel(x_ref, both_ref, act_ref, pg_ref, *refs):
    outs, acc_ref = refs[:-1], refs[-1]
    width = x_ref.shape[2]

    @pl.when(pl.program_id(0) == 0)
    def _():
        acc_ref[...] = jnp.zeros_like(acc_ref)

    acc_ref[0:width, :] += dot_tn(x_ref[0], both_ref[0])
    acc_ref[width:, :] += dot_tn(act_ref[0], pg_ref[0])

    @pl.when(pl.program_id(0) == pl.num_programs(0) - 1)
    def _():
        for k, out_ref in enumerate(outs):
            rows = out_ref.shape[0]
            out_ref[...] = acc_ref[k * rows : (k + 1) * rows, :].astype(bf16)


def expert_grads(x, both, act, pg):
    zs, slots, width = x.shape
    units = act.shape[2]
    pieces = 4
    piece = (width + units) // pieces

    def block(a):
        return pl.BlockSpec((1,) + a.shape[1:], lambda i: (i, 0, 0))

    return pl.pallas_call(
        expert_grads_kernel,
        grid=(zs,),
        out_shape=(jax.ShapeDtypeStruct((piece, width), bf16),) * pieces,
        in_specs=[block(a) for a in (x, both, act, pg)],
        out_specs=(pl.BlockSpec((piece, width), lambda i: (0, 0)),) * pieces,
        scratch_shapes=[pltpu.VMEM((width + units, width), f32)],
        compiler_params=pltpu.CompilerParams(vmem_limit_bytes=VMEM_LIMIT),
        cost_estimate=pl.CostEstimate(
            flops=6 * zs * slots * width * units, bytes_accessed=8 * zs * slots * width, transcendentals=0
        ),
        name="expert_grads",
    )(x, both, act, pg)


def late_kernel(column, mixed_ref, branch_ref, pay_ref, logit_ref, gain_ref, out_ref):
    width = mixed_ref.shape[1]
    out_ref[:, 0:width] = dot_tn(mixed_ref[...], branch_ref[...]).astype(bf16)
    logit = logit_ref[...]
    high = logit.astype(bf16)
    low = (logit - high.astype(f32)).astype(bf16)
    normed = pay_ref[...]
    side = dot_tn(normed, high) + dot_tn(normed, low)
    gain = jnp.broadcast_to(gain_ref[...], (LANES, width)).T
    out_ref[:, width:] = jnp.where(lanes_of(width) == column, gain, side).astype(bf16)


def late_grads(column, mixed, branch, pay, logit, gain):
    rows, width = mixed.shape
    vmem = pl.BlockSpec(memory_space=pltpu.VMEM)
    return pl.pallas_call(
        functools.partial(late_kernel, column),
        out_shape=jax.ShapeDtypeStruct((width, width + LANES), bf16),
        in_specs=[vmem] * 5,
        out_specs=vmem,
        compiler_params=pltpu.CompilerParams(vmem_limit_bytes=VMEM_LIMIT),
        cost_estimate=pl.CostEstimate(
            flops=2 * rows * width * width, bytes_accessed=4 * width * width, transcendentals=0
        ),
        name="late_grads",
    )(mixed, branch, pay, logit, gain)


def head_grads_kernel(dqkv_ref, normed_ref, out_ref, acc_ref):
    _, place, rows, pack = dqkv_ref.shape

    @pl.when(pl.program_id(0) == 0)
    def _():
        acc_ref[...] = jnp.zeros_like(acc_ref)

    left = dqkv_ref[0].reshape(place * rows, pack)
    acc_ref[...] += dot_tn(left, normed_ref[0].reshape(place * rows, normed_ref.shape[3]))

    @pl.when(pl.program_id(0) == pl.num_programs(0) - 1)
    def _():
        out_ref[...] = acc_ref[...].T.astype(bf16)


def head_grads(dqkv, normed):
    zs, place, rows, width = normed.shape
    return pl.pallas_call(
        head_grads_kernel,
        grid=(zs,),
        out_shape=jax.ShapeDtypeStruct((width, PACK), bf16),
        in_specs=[
            pl.BlockSpec((1, place, rows, PACK), lambda i: (i, 0, 0, 0)),
            pl.BlockSpec((1, place, rows, width), lambda i: (i, 0, 0, 0)),
        ],
        out_specs=pl.BlockSpec((width, PACK), lambda i: (0, 0)),
        scratch_shapes=[pltpu.VMEM((PACK, width), f32)],
        compiler_params=pltpu.CompilerParams(vmem_limit_bytes=VMEM_LIMIT),
        cost_estimate=pl.CostEstimate(
            flops=2 * zs * place * rows * width * PACK,
            bytes_accessed=2 * zs * place * rows * width,
            transcendentals=0,
        ),
        name="head_grads",
    )(dqkv, normed)


def spread_kernel(dqkv_ref, w_ref, near_ref, far_ref):
    _, place, rows, pack = dqkv_ref.shape
    for ref, first in ((near_ref, 0), (far_ref, place // 2)):
        for j in range(place // 2):
            ref[0, j] = dot_nt(dqkv_ref[0, first + j], w_ref[...]).astype(bf16)


def spread(dqkv, w, picked):
    _, place, rows, pack = dqkv.shape
    width = w.shape[0]
    first, step = picked[0], (picked[1] - picked[0] if len(picked) > 1 else 0)
    half = jax.ShapeDtypeStruct((len(picked), place // 2, rows, width), bf16)
    out = pl.BlockSpec((1, place // 2, rows, width), lambda i: (i, 0, 0, 0))
    return pl.pallas_call(
        spread_kernel,
        grid=(len(picked),),
        out_shape=(half, half),
        in_specs=[
            pl.BlockSpec((1, place, rows, pack), lambda i: (first + i * step, 0, 0, 0)),
            pl.BlockSpec(w.shape, lambda i: (0, 0)),
        ],
        out_specs=(out, out),
        compiler_params=pltpu.CompilerParams(vmem_limit_bytes=VMEM_LIMIT),
        cost_estimate=pl.CostEstimate(
            flops=2 * len(picked) * place * rows * pack * width,
            bytes_accessed=2 * len(picked) * place * rows * width,
            transcendentals=0,
        ),
        name="spread",
    )(dqkv, w)


def finish_kernel(nparts, *refs):
    hid_ref, gain_ref, resgrad_ref = refs[0:3]
    parts = refs[3 : 3 + nparts]
    out_ref = refs[-1]
    total = parts[0][...].astype(f32)
    for part in parts[1:]:
        total = total + part[...].astype(f32)
    x = hid_ref[...].astype(f32)
    scale = lax.rsqrt(jnp.mean(x * x, axis=-1, keepdims=True) + eps)
    scaled = total * gain_ref[...]
    centre = jnp.mean(scaled * x, axis=-1, keepdims=True)
    out_ref[...] = resgrad_ref[...] + scaled * scale - x * (scale * scale * scale * centre)


def finish(hidden, gain, resgrad, parts):
    vmem = pl.BlockSpec(memory_space=pltpu.VMEM)
    return pl.pallas_call(
        functools.partial(finish_kernel, len(parts)),
        out_shape=jax.ShapeDtypeStruct(hidden.shape, f32),
        in_specs=[vmem] * (3 + len(parts)),
        out_specs=vmem,
        compiler_params=pltpu.CompilerParams(vmem_limit_bytes=VMEM_LIMIT),
        name="input_grad",
    )(hidden, gain, resgrad, *parts)


def body(
    hidden,
    lengths,
    expert_ids,
    pair_keep,
    attn_gain,
    query_weight_matrix,
    key_weight_matrix,
    value_weight_matrix,
    attention_output_weight,
    moe_gain,
    router_weight_matrix,
    w_gate_up,
    w_down,
    out_grad,
):
    seqs, span, width = hidden.shape
    rows = seqs * span
    top_k = expert_ids.shape[2]
    ep = lax.axis_size("ep")
    dp = lax.axis_size("dp")
    zs, ys, _ = ep_shape(ep)
    place = 2 * ys
    me = lax.axis_index("ep").astype(jnp.int32)
    expert_count = w_gate_up.shape[0] * ep
    capacity = max(2, rows * top_k // expert_count)
    cap = -(-capacity // 16) * 16
    heads = query_weight_matrix.shape[1] // HD
    kv_heads = key_weight_matrix.shape[1] // HD
    replicas = ep // heads
    total = span * ep
    own_rows = query_weight_matrix.shape[0]
    hidden = hidden.reshape(rows, width)
    out_grad = out_grad.reshape(rows, width)

    def per_head(weight, count):
        split = weight.reshape(own_rows, count, HD).transpose(1, 0, 2)
        return jnp.repeat(split, heads // count, axis=0)

    small = jnp.concatenate(
        [router_weight_matrix, attn_gain[:, None], moe_gain[:, None]], axis=1
    )
    small = jnp.pad(small, ((0, 0), (0, PACK - 3 * HD - small.shape[1])))
    packed = jnp.concatenate(
        [
            per_head(query_weight_matrix, heads),
            per_head(key_weight_matrix, kv_heads),
            per_head(value_weight_matrix, kv_heads),
            jnp.broadcast_to(small[None], (heads,) + small.shape),
        ],
        axis=2,
    )
    packed = jnp.repeat(packed, replicas, axis=0)
    packed = jnp.broadcast_to(packed[None], (dp,) + packed.shape).reshape(
        dp * ep, own_rows, PACK
    )
    packed = lax.all_to_all(packed, ("dp", "ep"), split_axis=0, concat_axis=0, tiled=True)
    head_w = packed.reshape(dp * ep * own_rows, PACK)
    at = 3 * HD
    wr = jnp.pad(head_w[:, at : at + expert_count], ((0, 0), (0, LANES - expert_count)))
    gains = head_w[:, at + expert_count : at + expert_count + 2].astype(f32)
    gain_one = gains[:, 0].reshape(1, width)
    gain_two = gains[:, 1].reshape(1, width)
    head_w = jnp.where(jnp.arange(PACK)[None, :] < at, head_w, jnp.zeros((), bf16))

    positions = me * span + jnp.arange(span, dtype=jnp.int32)
    is_valid = positions[None, :] < lengths[:, None]
    expert_range = jnp.arange(LANES, dtype=jnp.int32)
    hit = expert_ids[..., None] == expert_range
    chosen = jnp.any(hit, axis=2).reshape(rows, LANES).astype(f32)
    live = jnp.any(hit & (pair_keep[..., None] > 0), axis=2) & is_valid[..., None]
    live = live.reshape(rows, LANES).astype(bf16)
    earlier = jnp.arange(rows)[:, None] > jnp.arange(rows)[None, :]
    slot = jnp.dot(earlier.astype(bf16), live, preferred_element_type=f32)
    code = jnp.where((slot < capacity) & (live > 0), slot + 1.0, -chosen)
    code_rows = -(-expert_count // 16) * 16
    lines = jnp.pad(code[:, 0:code_rows].T.astype(bf16), ((0, 0), (0, width - rows)))
    lifted = jnp.concatenate([out_grad, lines])

    rates = theta_base ** (-2.0 * jnp.arange(HD // 2, dtype=f32) / HD)
    angle = jnp.arange(total, dtype=jnp.int32).astype(f32)[:, None] * rates[None, :]
    cos = jnp.tile(jnp.cos(angle), (1, 4))
    sin = jnp.sin(angle)
    sin = jnp.concatenate([-sin, sin, -sin, sin], axis=1)
    core = me % 2
    col = (me // 2) % ys
    plane = me // place
    planes = (plane + jnp.arange(zs, dtype=jnp.int32)) % zs
    rows_at = (col + jnp.arange(ys, dtype=jnp.int32)) % ys
    places = jnp.concatenate([rows_at * 2 + core, rows_at * 2 + 1 - core])
    replica = me % replicas if replicas > 1 else jnp.zeros((), jnp.int32)
    attend_meta = jnp.concatenate([lengths, replica[None], planes, places]).astype(jnp.int32)
    expert_meta = jnp.concatenate([jnp.stack([me, plane]), places]).astype(jnp.int32)
    project_meta = expert_meta[1:]
    turn_meta = jnp.concatenate([lengths, (me * span)[None]]).astype(jnp.int32)

    order = list(range(zs))

    def move(x, sender=False, **offset):
        return lax.ppermute(x, "ep", (send_to if sender else fetch_from)(ep, **offset))

    def steps(t):
        n = len(order)
        return t < n - 1, t < n, 1 <= t <= n, 2 <= t < n + 2

    columns, near, far, carried, x = [hidden], {}, {}, None, hidden
    wo_part = [attention_output_weight]
    for t in range(len(order) + 2):
        on_z, on_y, on_core, on_work = steps(t)
        z_new = [move(columns[t], dz=1)] if on_z else []
        y_new = [move(columns[t], dy=k) for k in range(1, ys)] if on_y else []
        c_new = [move(block, dc=1) for block in near[t - 1]] if on_core else []
        if on_work:
            d = order[t - 2]
            carried = project(
                project_meta, near[t - 2] + far[t - 2], head_w, gain_one, cos, sin, zs, d, carried
            )
        block = wo_part[0]
        wo_new = []
        if t == zs - 1:
            wo_new = [move(block, dz=k) for k in range(1, zs)]
        elif t == zs:
            wo_new = [move(block, dy=k) for k in range(1, ys)]
        x, columns, near, far, z_new, y_new, c_new, carried, wo_part, wo_new = phase_tree(
            x, columns, near, far, z_new, y_new, c_new, carried, wo_part, wo_new
        )
        if wo_new:
            wo_part = [jnp.stack(wo_part + wo_new)]
        columns = columns + z_new
        if on_y:
            near[t] = [columns[t]] + y_new
        if on_core:
            far[t - 1] = c_new
        if t == 2:
            upstream = lax.all_gather(phase(lifted, columns[-1])[0], "ep", axis=0)
    wo_new = [
        lax.ppermute(wo_part[0], "dp", [((i + k) % dp, i) for i in range(dp)]) for k in range(1, dp)
    ]
    normed_all, qkv = carried
    made, qk, v, qkt, stat = attend(attend_meta, qkv, seqs, replicas)
    made, wo_new, wo_part = phase_tree(made, wo_new, wo_part)
    recv = lax.all_to_all(made, "ep", split_axis=0, concat_axis=0, tiled=True)
    wo_part = jnp.stack(wo_part + wo_new)
    wo_part = [jnp.stack([wo_part, move(wo_part, dc=1)])]
    line = jnp.arange(dp * ep, dtype=jnp.int32)
    away = (line % 2 - core) % 2
    away = away * dp + (line // ep - lax.axis_index("dp")) % dp
    away = away * ys + ((line // 2) % ys - col) % ys
    away = away * zs + ((line // place) % zs - plane) % zs
    wo = wo_part[0].reshape(dp * ep, own_rows, width)
    wo = jnp.take(wo, away, axis=0, mode="clip").reshape(heads * HD, width)
    if replicas > 1:
        recv = recv.reshape((heads, replicas) + recv.shape[1:]).sum(axis=1).astype(bf16)
    res, pay, mixed, gates = middle(seqs, recv, hidden, wo, gain_two, wr, code)

    count = zs
    columns, near, far, chips, totals = [pay], {}, {}, {}, {}
    outs, carried, extra, passed = {}, None, {}, None
    rings = [[(i, (i + d) % dp) for i in range(dp)] for d in range(1, dp)]
    cuts = ((1,), tuple(range(2, zs)), (0,))

    def hop(value):
        return lax.ppermute(value, "ep", fetch_from(ep, dz=1))

    def swap(piece):
        return [lax.ppermute(piece, "dp", ring) for ring in rings]

    for t in range(count + 5):
        on_z, on_y, on_core, on_work = steps(t)
        z_new = [move(columns[t], dz=1)] if on_z else []
        y_new = [move(columns[t], dy=k) for k in range(1, ys)] if on_y else []
        c_new = [move(block, dc=1) for block in near[t - 1]] if on_core else []
        rc, ry, rz = t - 3, t - 4, t - 5
        rc_new = [move(outs[rc][1], True, dc=1)] if 0 <= rc < count else []
        ry_new = [move(chips[ry][d], True, dy=d) for d in range(1, ys)] if 0 <= ry < count else []
        rz_new = []
        if 1 <= rz < count:
            rz_new = [hop(totals[rz] if rz == 1 else add_low(totals[rz], passed))]
        new = {}
        if on_work:
            d = order[t - 2]
            out = experts(
                expert_meta,
                near[t - 2] + far[t - 2],
                upstream,
                w_gate_up[0],
                w_down[0],
                wr,
                cap,
                zs,
                d,
                carried,
            )
            outs[t - 2], carried = out[:2], out[2:]
        if t == count + 2:
            new["got"] = move(carried[1], True, dc=1)
            new["grads"] = list(expert_grads(carried[2], carried[5], carried[4], carried[3]))
        if t == count + 3:
            new["chip"] = [
                [
                    add_low(
                        jnp.stack([carried[0][k, d] for k in cut]),
                        jnp.stack([extra["got"][k, d] for k in cut]),
                    )
                    for cut in cuts
                    if cut
                ]
                for d in range(ys)
            ]
        if t == count + 4:
            new["swap"] = swap(extra["grads"][0])
            new["first"] = [move(extra["chip"][d][0], True, dy=d) for d in range(1, ys)]
        state = (pay, columns, near, far, outs, chips, totals, carried, extra)
        state = phase_tree(state, z_new, y_new, c_new, rc_new, ry_new, rz_new, new)
        state, z_new, y_new, c_new, rc_new, ry_new, rz_new, new = state
        pay, columns, near, far, outs, chips, totals, carried, extra = state
        columns = columns + z_new
        if on_y:
            near[t] = [columns[t]] + y_new
        if on_core:
            far[t - 1] = c_new
        if rc_new:
            chips[rc] = [add_low(outs[rc][0][d], rc_new[0][d]) for d in range(ys)]
        if 0 <= ry < count:
            totals[ry] = add_low(chips[ry][0], *ry_new)
        if rz_new:
            passed = rz_new[0]
        extra.update(new)
    parts = [totals[0]] + ([passed] if zs > 1 else [])
    moe_chip = extra["chip"]
    grads_low = extra["grads"]

    res_grad, branch, grads, logit_grad, gain_two_grad = turn(
        turn_meta, seqs, parts, res, out_grad, gates, code, wr, gain_two, wo
    )
    if replicas > 1:
        grads = jnp.repeat(grads, replicas, axis=0)
    grads = lax.all_to_all(grads, "ep", split_axis=0, concat_axis=0, tiled=True)
    late = late_grads(expert_count, mixed, branch, pay, logit_grad, gain_two_grad)
    late = late.reshape(dp, zs * ys, 2, own_rows, late.shape[1])

    def stage_parts(value, axis, here_at, size):
        return [
            lax.dynamic_index_in_dim(value, (here_at + d) % size, axis, keepdims=False)
            for d in range(size)
        ]

    late_parts = stage_parts(late, 2, core, 2)
    moe = [add_low(moe_chip[0][0], *extra["first"])]
    moe_new = [move(moe_chip[d][1], True, dy=d) for d in range(1, ys)]
    grads_moved = [extra["swap"], swap(grads_low[1])]
    state = (grads, moe, moe_new, moe_chip, late_parts, grads_low, grads_moved)
    grads, moe, moe_new, moe_chip, late_parts, grads_low, grads_moved = phase_tree(*state)
    moe.append(add_low(moe_chip[0][1], *moe_new))

    dqkv = back(attend_meta, grads, qk, v, qkt, stat, cos, sin, qkv.shape, seqs, replicas)
    moe_new = [move(moe_chip[d][2], True, dy=d) for d in range(1, ys)]
    passed = hop(moe[0][0])
    late_got = [move(late_parts[1], True, dc=1)]
    swapped = swap(grads_low[2])
    state = (dqkv, moe, moe_new, passed, moe_chip, late_parts, late_got, grads_low, swapped)
    state = phase_tree(*state)
    dqkv, moe, moe_new, passed, moe_chip, late_parts, late_got, grads_low, swapped = state
    moe.append(add_low(moe_chip[0][2], *moe_new))
    grads_moved.append(swapped)
    late = add_low(late_parts[0], *late_got)
    late_parts = stage_parts(late, 0, lax.axis_index("dp"), dp)
    late_got = [lax.ppermute(part, "dp", ring) for part, ring in zip(late_parts[1:], rings)]

    halves = ((1, 2), (3, 0)) if zs == 4 else (tuple(range(1, zs)), (0,))
    turn_order = [d for half in halves for d in half]
    near, far = ([part] for part in spread(dqkv, head_w, halves[0]))
    near, far, dqkv = phase_tree(near, far, dqkv)

    got = [move(far[0], True, dc=1)]
    more = spread(dqkv, head_w, halves[1])
    near.append(more[0])
    far.append(more[1])
    passed = hop(add_low(moe[1][0], passed))
    head_grad = head_grads(dqkv, normed_all).reshape(dp * ep, own_rows, PACK)
    state = (near, far, got, moe, passed, head_grad, late_parts, late_got, grads_low)
    near, far, got, moe, passed, head_grad, late_parts, late_got, grads_low = phase_tree(*state)
    late = add_low(late_parts[0], *late_got)
    plane_groups = [[c + 2 * k for k in range(zs * ys)] for c in range(2)]
    late = lax.all_to_all(
        late, "ep", split_axis=0, concat_axis=0, tiled=True, axis_index_groups=plane_groups
    )

    head_grad = lax.all_to_all(head_grad, ("dp", "ep"), split_axis=0, concat_axis=0, tiled=True)
    totals, received = {}, None

    def chip_of(d):
        half = 0 if d in halves[0] else 1
        at = halves[half].index(d)
        return [add_low(near[half][at, y], got[half][at, y]) for y in range(ys)]

    chip = chip_of(turn_order[0])
    for k, d in enumerate(turn_order):
        ahead = chip_of(turn_order[k + 1]) if k + 1 < len(turn_order) else []
        moved = [move(chip[y], True, dy=y) for y in range(1, ys)]
        if k:
            last = totals[turn_order[k - 1]]
            received = hop(last if k == 1 else add_low(last, received))
        if k == 0:
            got.append(move(far[1], True, dc=1))
            passed = hop(add_low(moe[1][1], passed)) if zs == 4 else passed
            swapped = swap(grads_low[3])
            near, got, chip, ahead, moved, passed, swapped = phase_tree(
                near, got, chip, ahead, moved, passed, swapped
            )
            grads_moved.append(swapped)
        elif k == 2:
            near, got, chip, ahead, moved, received, totals, head_grad = phase_tree(
                near, got, chip, ahead, moved, received, totals, head_grad
            )
        else:
            near, got, chip, ahead, moved, received, totals = phase_tree(
                near, got, chip, ahead, moved, received, totals
            )
        totals[d] = add_low(chip[0], *moved)
        chip = ahead
    parts = [totals[0], received]
    late = phase(late, totals[0], received)[0]
    late = late.astype(f32).sum(axis=0)
    mparts = [moe[-1][0], passed]
    sums = []
    for own, moved in zip(grads_low, grads_moved):
        piece = own.astype(f32)
        for other in moved:
            piece = piece + other.astype(f32)
        sums.append(piece)
    grads_total = jnp.concatenate(sums)
    gu_total = grads_total[0:width]
    d_total = grads_total[width:]

    head_grad = head_grad.astype(f32).reshape(dp, heads, replicas, own_rows, PACK).sum(axis=(0, 2))

    def rows_of(part, count):
        part = part.reshape(count, heads // count, own_rows, HD).sum(axis=1)
        return part.transpose(1, 0, 2).reshape(own_rows, count * HD)

    query_w_grad = rows_of(head_grad[..., 0:HD], heads)
    key_w_grad = rows_of(head_grad[..., HD : 2 * HD], kv_heads)
    value_w_grad = rows_of(head_grad[..., 2 * HD : 3 * HD], kv_heads)
    gain_one_grad = (
        jnp.sum(query_w_grad * query_weight_matrix.astype(f32), axis=1)
        + jnp.sum(key_w_grad * key_weight_matrix.astype(f32), axis=1)
        + jnp.sum(value_w_grad * value_weight_matrix.astype(f32), axis=1)
    ) / attn_gain.astype(f32)

    moe_own = res
    for part in mparts:
        moe_own = moe_own + part.astype(f32)
    output = jnp.where(
        is_valid[..., None], moe_own.reshape(seqs, span, width), 0.0
    ).astype(bf16)
    input_grad = finish(hidden, gain_one, res_grad, parts)
    model = width
    return (
        output,
        input_grad.reshape(seqs, span, width),
        gain_one_grad,
        query_w_grad,
        key_w_grad,
        value_w_grad,
        late[:, 0:model],
        late[:, model + expert_count],
        late[:, model : model + expert_count],
        gu_total[None],
        d_total[None],
    )


def solution(mesh):
    return jax.shard_map(
        body,
        mesh=mesh,
        in_specs=(
            P("dp", "ep", None),
            P("dp"),
            P("dp", "ep", None),
            P("dp", "ep", None),
            P(("dp", "ep")),
            P(("dp", "ep"), None),
            P(("dp", "ep"), None),
            P(("dp", "ep"), None),
            P(("dp", "ep"), None),
            P(("dp", "ep")),
            P(("dp", "ep"), None),
            P("ep", None, None),
            P("ep", None, None),
            P("dp", "ep", None),
        ),
        out_specs=(
            P("dp", "ep", None),
            P("dp", "ep", None),
            P(("dp", "ep")),
            P(("dp", "ep"), None),
            P(("dp", "ep"), None),
            P(("dp", "ep"), None),
            P(("dp", "ep"), None),
            P(("dp", "ep")),
            P(("dp", "ep"), None),
            P("ep", None, None),
            P("ep", None, None),
        ),
        check_vma=False,
    )
```

```python
import functools

import jax
import jax.numpy as jnp
from jax import lax
from jax.experimental import pallas as pl
from jax.experimental.pallas import tpu as pltpu
from jax.sharding import PartitionSpec as P

HD = 64
LANES = 128
SLAB = 256
WIDE = 512
PACK = 256
eps = 1e-05
theta_base = 10000.0
f32 = jnp.float32
bf16 = jnp.bfloat16
VMEM_LIMIT = 56 * 1024 * 1024


def dot(a, b):
    return lax.dot_general(a, b, (((1,), (0,)), ((), ())), preferred_element_type=f32)


def dot_nt(a, b):
    return lax.dot_general(a, b, (((1,), (1,)), ((), ())), preferred_element_type=f32)


def dot_tn(a, b):
    return lax.dot_general(a, b, (((0,), (0,)), ((), ())), preferred_element_type=f32)


def lanes_of(rows, width=LANES):
    return lax.broadcasted_iota(jnp.int32, (rows, width), 1)


def half_swap(x):
    lane = lanes_of(x.shape[0])
    return jnp.where(lane % HD < HD // 2, pltpu.roll(x, LANES - HD // 2, 1), pltpu.roll(x, HD // 2, 1))


def ep_shape(ep):
    zs = 4 if ep % 8 == 0 else 1
    return zs, ep // (2 * zs), 2


def fetch_from(ep, dz=0, dy=0, dc=0):
    zs, ys, cs = ep_shape(ep)
    pairs = []
    for z in range(zs):
        for y in range(ys):
            for c in range(cs):
                src = (((z + dz) % zs) * ys + (y + dy) % ys) * cs + (c + dc) % cs
                pairs.append((src, (z * ys + y) * cs + c))
    return pairs


def send_to(ep, **offset):
    return [(dst, src) for src, dst in fetch_from(ep, **offset)]


def phase(*values):
    return lax.optimization_barrier(values)


def phase_tree(*values):
    flat, tree = jax.tree.flatten(values)
    return jax.tree.unflatten(tree, phase(*flat))


def add_low(*parts):
    total = parts[0].astype(f32)
    for part in parts[1:]:
        total = total + part.astype(f32)
    return total.astype(bf16)


def project_kernel(place, carry, meta, *refs):
    blocks = refs[:place]
    w_ref, gain_ref, cos_ref, sin_ref = refs[place : place + 4]
    normed_ref, qkv_ref = refs[-2:]
    rows, _ = blocks[0].shape
    span = cos_ref.shape[0] // place
    seqs = rows // span
    lane = lanes_of(rows)
    for j in range(place):
        x = blocks[j][...].astype(f32)
        scale = lax.rsqrt(jnp.mean(x * x, axis=-1, keepdims=True) + eps)
        normed = (x * scale * gain_ref[...]).astype(bf16)
        normed_ref[0, j] = normed
        raw = dot(normed, w_ref[...])
        at = pl.ds(pl.multiple_of(meta[1 + j] * span, 32), span)
        cos = jnp.concatenate([cos_ref[at, :]] * seqs, axis=0)
        sin = jnp.concatenate([sin_ref[at, :]] * seqs, axis=0)
        both = raw[:, 0:LANES]
        both = (both * cos + half_swap(both) * sin).astype(bf16).astype(f32)
        both = jnp.where(lane < HD, both * HD ** (-0.5), both)
        qkv_ref[0, j, :, 0:LANES] = both.astype(bf16)
        qkv_ref[0, j, :, LANES:PACK] = jnp.where(lane < HD, raw[:, LANES:PACK], 0.0).astype(bf16)


def project(meta, blocks, w, gain, cos, sin, zs, dz, carried):
    rows, width = blocks[0].shape
    place = len(blocks)
    span = cos.shape[0] // (zs * place)

    def whole(a):
        return pl.BlockSpec(a.shape, lambda i, m: (0,) * a.ndim)

    table = pl.BlockSpec((place * span, LANES), lambda i, m: (lax.rem(m[0] + dz, zs), 0))
    args = list(blocks) + [w, gain, cos, sin]
    in_specs = [whole(a) for a in blocks] + [whole(w), whole(gain), table, table]
    aliases = {}
    if carried is not None:
        aliases = {1 + len(args): 0, 2 + len(args): 1}
        args += list(carried)
        in_specs += [pl.BlockSpec(memory_space=pl.ANY)] * 2
    return pl.pallas_call(
        functools.partial(project_kernel, place, carried is not None),
        grid_spec=pltpu.PrefetchScalarGridSpec(
            num_scalar_prefetch=1,
            grid=(1,),
            in_specs=in_specs,
            out_specs=(
                pl.BlockSpec((1, place, rows, width), lambda i, m: (dz, 0, 0, 0)),
                pl.BlockSpec((1, place, rows, PACK), lambda i, m: (dz, 0, 0, 0)),
            ),
        ),
        out_shape=(
            jax.ShapeDtypeStruct((zs, place, rows, width), bf16),
            jax.ShapeDtypeStruct((zs, place, rows, PACK), bf16),
        ),
        input_output_aliases=aliases,
        compiler_params=pltpu.CompilerParams(vmem_limit_bytes=VMEM_LIMIT),
        cost_estimate=pl.CostEstimate(
            flops=2 * place * rows * width * PACK,
            bytes_accessed=4 * place * rows * width,
            transcendentals=0,
        ),
        name="project_in",
    )(meta, *args)


def attend_kernel(
    replicas,
    meta,
    qkv_ref,
    out_ref,
    qk_ref,
    v_ref,
    qkt_ref,
    stat_ref,
    vt_ref,
    wide_ref,
):
    zs, place, rows, _ = qkv_ref.shape
    total = qk_ref.shape[1]
    span = total // (zs * place)
    s = pl.program_id(0)
    seqs = rows // span
    source = pl.ds(pl.multiple_of(s * span, 32), span)
    for d in range(zs):
        for j in range(place):
            at = pl.multiple_of((meta[seqs + 1 + d] * place + meta[seqs + 1 + zs + j]) * span, 32)
            qk_ref[0, pl.ds(at, span), :] = qkv_ref[d, j, source, 0:LANES]
            v_ref[0, pl.ds(at, span), :] = qkv_ref[d, j, source, LANES:PACK]
    for lo in range(0, total, SLAB):
        at = slice(lo, lo + SLAB)
        qkt_ref[0, :, at] = qk_ref[0, at, :].astype(f32).T.astype(bf16)
        vt_ref[:, at] = v_ref[0, at, :].astype(f32).T.astype(bf16)

    key_row = lax.broadcasted_iota(jnp.int32, (WIDE, WIDE), 0)
    query_col = lax.broadcasted_iota(jnp.int32, (WIDE, WIDE), 1)

    def one_slab(lo):
        hi = lo + WIDE
        qt = qkt_ref[0, 0:HD, lo:hi]
        diag = dot(qk_ref[0, lo:hi, HD:LANES], qt)
        diag = jnp.where(key_row <= query_col, diag, -jnp.inf)
        top = jnp.max(diag, axis=0, keepdims=True)
        if lo:
            full = dot(qk_ref[0, 0:lo, HD:LANES], qt)
            top = jnp.maximum(top, jnp.max(full, axis=0, keepdims=True))
        p_diag = jnp.exp(diag - top)
        row_total = jnp.sum(p_diag, axis=0, keepdims=True)
        out = dot(vt_ref[:, lo:hi], p_diag.astype(bf16))
        if lo:
            p_full = jnp.exp(full - top)
            row_total = row_total + jnp.sum(p_full, axis=0, keepdims=True)
            out = out + dot(vt_ref[:, 0:lo], p_full.astype(bf16))
        out = out[0:HD] / row_total
        stat_ref[0, 0:HD, lo:hi] = out
        stat_ref[0, HD : HD + 8, lo:hi] = jnp.broadcast_to(top + jnp.log(row_total), (8, WIDE))
        wide_ref[lo:hi, :] = jnp.concatenate([out, out], axis=0).T

    def no_slab(lo):
        stat_ref[0, :, lo : lo + WIDE] = jnp.zeros((HD + 8, WIDE), f32)
        wide_ref[lo : lo + WIDE, :] = jnp.zeros((WIDE, LANES), f32)

    for i, lo in enumerate(range(0, total, WIDE)):
        if replicas > 1:
            mine = meta[seqs] == i % replicas
            pl.when(mine)(functools.partial(one_slab, lo))
            pl.when(jnp.logical_not(mine))(functools.partial(no_slab, lo))
        else:
            one_slab(lo)

    half = span // 2
    for e in range(total // span):
        upper = wide_ref[e * span : e * span + half, :]
        lower = wide_ref[e * span + half : (e + 1) * span, :]
        out_ref[e] = jnp.where(lanes_of(half) < HD, upper, lower).astype(bf16)


def attend(meta, qkv, seqs, replicas):
    zs, place, rows, _ = qkv.shape
    span = rows // seqs
    total = zs * place * span
    return pl.pallas_call(
        functools.partial(attend_kernel, replicas),
        grid=(seqs,),
        out_shape=(
            jax.ShapeDtypeStruct((total // span, seqs * (span // 2), LANES), bf16),
            jax.ShapeDtypeStruct((seqs, total, LANES), bf16),
            jax.ShapeDtypeStruct((seqs, total, LANES), bf16),
            jax.ShapeDtypeStruct((seqs, LANES, total), bf16),
            jax.ShapeDtypeStruct((seqs, HD + 8, total), f32),
        ),
        in_specs=[
            pl.BlockSpec(memory_space=pltpu.SMEM),
            pl.BlockSpec(qkv.shape, lambda s: (0, 0, 0, 0)),
        ],
        out_specs=(
            pl.BlockSpec((total // span, span // 2, LANES), lambda s: (0, s, 0)),
            pl.BlockSpec((1, total, LANES), lambda s: (s, 0, 0)),
            pl.BlockSpec((1, total, LANES), lambda s: (s, 0, 0)),
            pl.BlockSpec((1, LANES, total), lambda s: (s, 0, 0)),
            pl.BlockSpec((1, HD + 8, total), lambda s: (s, 0, 0)),
        ),
        scratch_shapes=[pltpu.VMEM((LANES, total), bf16), pltpu.VMEM((total, LANES), f32)],
        compiler_params=pltpu.CompilerParams(vmem_limit_bytes=VMEM_LIMIT),
        cost_estimate=pl.CostEstimate(
            flops=4 * seqs * total * total * LANES,
            bytes_accessed=4 * seqs * total * PACK,
            transcendentals=seqs * total * total // 2,
        ),
        name="attend_forward",
    )(meta, qkv)


def gates_of(normed, wr_ref, code):
    logits = jnp.where(code != 0, dot(normed, wr_ref[...]), -1e30)
    powers = jnp.exp(logits - jnp.max(logits, axis=-1, keepdims=True))
    return powers / jnp.sum(powers, axis=-1, keepdims=True)


def middle_kernel(
    seqs,
    recv_ref,
    hid_ref,
    wo_ref,
    gain_ref,
    wr_ref,
    code_ref,
    res_ref,
    pay_ref,
    mixed_ref,
    gate_ref,
):
    heads, half_rows, _ = recv_ref.shape
    width = hid_ref.shape[1]
    half = half_rows // seqs
    low = lanes_of(half_rows) < HD
    uppers, lowers = [], []
    for j in range(heads // 2):
        a = recv_ref[2 * j].astype(f32)
        b = recv_ref[2 * j + 1].astype(f32)
        uppers.append(jnp.where(low, a, pltpu.roll(b, HD, 1)).astype(bf16))
        lowers.append(jnp.where(low, pltpu.roll(a, HD, 1), b).astype(bf16))
    upper = jnp.concatenate(uppers, axis=1)
    lower = jnp.concatenate(lowers, axis=1)
    pieces = []
    for s in range(seqs):
        pieces += [upper[s * half : (s + 1) * half], lower[s * half : (s + 1) * half]]
    mixed = jnp.concatenate(pieces, axis=0)
    mixed_ref[...] = mixed
    res = hid_ref[...].astype(f32) + dot(mixed, wo_ref[...])
    res_ref[...] = res
    scale = lax.rsqrt(jnp.mean(res * res, axis=-1, keepdims=True) + eps)
    normed = (res * scale * gain_ref[...]).astype(bf16)
    gate_ref[...] = gates_of(normed, wr_ref, code_ref[...])
    pay_ref[...] = normed


def middle(seqs, recv, hid, wo, gain, wr, code):
    rows, width = hid.shape
    vmem = pl.BlockSpec(memory_space=pltpu.VMEM)
    return pl.pallas_call(
        functools.partial(middle_kernel, seqs),
        out_shape=(
            jax.ShapeDtypeStruct((rows, width), f32),
            jax.ShapeDtypeStruct((rows, width), bf16),
            jax.ShapeDtypeStruct((rows, width), bf16),
            jax.ShapeDtypeStruct((rows, LANES), f32),
        ),
        in_specs=[vmem] * 6,
        out_specs=(vmem,) * 4,
        compiler_params=pltpu.CompilerParams(vmem_limit_bytes=VMEM_LIMIT),
        cost_estimate=pl.CostEstimate(
            flops=4 * rows * width * width, bytes_accessed=4 * width * width, transcendentals=0
        ),
        name="project_out",
    )(recv, hid, wo, gain, wr, code)


def expert_kernel(place, cap, zs, dz, first, meta, *refs):
    pay_in = refs[0:place]
    up_in, wgu_in, wd_in, wr_ref = refs[place : place + 4]
    rest = refs[place + 4 + (0 if first else 6) :]
    near_out, far_out, mnear_out, mfar_out, x_out, pg_out, act_out, both_out = rest[:8]
    pay, up, code, wgu, wd, back_s, moe_s, x_s, pg_s, act_s, both_s, in_sem, out_sem = rest[8:]
    rows, width = pay_in[0].shape
    units = wd.shape[0]
    halves = place // 2
    expert = meta[0]
    plane = lax.rem(meta[1] + dz, zs)
    loads = {}
    order = []
    for j in range(place):
        loads["p", j] = pltpu.make_async_copy(pay_in[j], pay.at[j], in_sem.at[2 * j])
        source = up_in.at[plane * place + meta[2 + j]]
        loads["u", j] = pltpu.make_async_copy(
            source.at[pl.ds(0, rows)], up.at[j], in_sem.at[2 * j + 1]
        )
        loads["c", j] = pltpu.make_async_copy(
            source.at[pl.ds(rows, code.shape[1]), pl.ds(0, code.shape[2])],
            code.at[j],
            in_sem.at[2 * place + 2 + j],
        )
    loads["gu"] = pltpu.make_async_copy(wgu_in, wgu, in_sem.at[2 * place])
    loads["d"] = pltpu.make_async_copy(wd_in, wd, in_sem.at[2 * place + 1])
    order = [("c", j) for j in range(place)]
    order += [("p", j) for j in range(halves)] + ["gu", "d"]
    order += [("u", j) for j in range(halves)]
    order += [("p", j) for j in range(halves, place)] + [("u", j) for j in range(halves, place)]
    for key in order:
        loads[key].start()
    stores = []

    def store(src, dst):
        copy = pltpu.make_async_copy(src, dst, out_sem.at[len(stores)])
        copy.start()
        stores.append(copy)

    def save(h, value, buf, out):
        own = pl.ds(h * halves * cap, halves * cap)
        buf[own, :] = value
        store(buf.at[own], out.at[dz, own])

    lane = lanes_of(rows)
    slot_row = lax.broadcasted_iota(jnp.int32, (cap, rows), 0)
    slot_col = lax.broadcasted_iota(jnp.int32, (rows, cap), 1)
    code_row = lax.broadcasted_iota(jnp.int32, (code.shape[1], rows), 0)
    cap_lane = lanes_of(cap)
    line_row = lax.broadcasted_iota(jnp.int32, code.shape[1:], 0)
    slot_wide = lax.broadcasted_iota(jnp.int32, (cap, code.shape[2]), 0)
    for h in range(2):
        mine = range(h * halves, (h + 1) * halves)
        for j in mine:
            loads["c", j].wait()
            loads["p", j].wait()
        outs_of, xs, gates = [], [], []
        into, into_wide = [], []
        for j in mine:
            lines = code[j].astype(f32)
            blank = jnp.zeros((LANES - lines.shape[0], lines.shape[1]), f32)
            codes = jnp.concatenate([lines, blank], axis=0).T[0:rows]
            column = jnp.sum(jnp.where(lane == expert, codes, 0.0), axis=1, keepdims=True)
            line = jnp.sum(
                jnp.where(code_row == expert, lines[:, 0:rows], 0.0), axis=0, keepdims=True
            )
            into.append(jnp.where(line.astype(jnp.int32) == slot_row + 1, 1.0, 0.0).astype(bf16))
            line = jnp.sum(jnp.where(line_row == expert, lines, 0.0), axis=0, keepdims=True)
            into_wide.append(
                jnp.where(line.astype(jnp.int32) == slot_wide + 1, 1.0, 0.0).astype(bf16)
            )
            outs_of.append(
                jnp.where(column.astype(jnp.int32) == slot_col + 1, 1.0, 0.0).astype(bf16)
            )
            xs.append(dot(into[-1], pay[j]).astype(bf16))
            gate = gates_of(xs[-1], wr_ref, dot(into[-1], codes.astype(bf16)))
            gates.append(jnp.sum(jnp.where(cap_lane == expert, gate, 0.0), axis=1, keepdims=True))
        x = jnp.concatenate(xs, axis=0)
        gate_prob = jnp.concatenate(gates, axis=0)
        if h == 0:
            loads["gu"].wait()
        save(h, x, x_s, x_out)
        gate_up = dot(x, wgu[...])
        gate = gate_up[:, 0:units]
        high = gate_up[:, units:]
        sig = jax.nn.sigmoid(gate)
        silu = gate * sig
        act = (silu * high).astype(bf16)
        if h == 0:
            loads["d"].wait()
        save(h, act, act_s, act_out)
        made = dot(act, wd[...]).astype(bf16).astype(f32)
        for j in mine:
            loads["u", j].wait()
        upstream = jnp.concatenate([dot(into[k], up[j]) for k, j in enumerate(mine)], axis=0)
        gate_grad = jnp.sum(made * upstream, axis=-1, keepdims=True)
        moe = (made * gate_prob).astype(bf16)
        pair_grad = (upstream * gate_prob).astype(bf16)
        for k, j in enumerate(mine):
            part = slice(k * cap, (k + 1) * cap)
            moe_s[j] = dot(outs_of[k], moe[part]).astype(bf16)
        store(moe_s.at[pl.ds(h * halves, halves)], (mnear_out if h == 0 else mfar_out).at[dz])
        save(h, pair_grad, pg_s, pg_out)
        act_grad = dot_nt(pair_grad, wd[...])
        both = jnp.concatenate(
            [act_grad * high * (sig * (1.0 + gate * (1.0 - sig))), act_grad * silu], axis=1
        ).astype(bf16)
        save(h, both, both_s, both_out)
        back = dot_nt(both, wgu[...]).astype(bf16)
        upper = gate_grad.astype(bf16).astype(f32)
        pair_lane = lanes_of(halves * cap)
        pair = jnp.where(pair_lane == 0, upper, gate_grad - upper)
        for k, j in enumerate(mine):
            part = slice(k * cap, (k + 1) * cap)
            back_s[j, 0:rows, :] = dot(outs_of[k], back[part]).astype(bf16)
            found = dot(pair[part].T[0:16].astype(bf16), into_wide[k])
            back_s[j, rows:, :] = jnp.zeros((code.shape[1], width), bf16)
            for row, at in ((0, 0), (1, width // 2)):
                value = jnp.where(line_row == expert, found[row : row + 1], 0.0)
                back_s[j, rows:, at : at + code.shape[2]] = value.astype(bf16)
        store(back_s.at[pl.ds(h * halves, halves)], near_out if h == 0 else far_out)
    for copy in stores:
        copy.wait()


def experts(meta, pays, upstream, wgu, wd, wr, cap, zs, dz, carried):
    place = len(pays)
    rows, width = pays[0].shape
    units = wd.shape[0]
    first = carried is None
    anyspace = pl.BlockSpec(memory_space=pl.ANY)
    args = list(pays) + [upstream, wgu, wd, wr]
    code_rows = upstream.shape[1] - rows
    aliases = {}
    if not first:
        aliases = {1 + len(args) + k: 2 + k for k in range(6)}
        args += list(carried)
    half = jax.ShapeDtypeStruct((place // 2, rows + code_rows, width), bf16)
    slots = place * cap
    return pl.pallas_call(
        functools.partial(expert_kernel, place, cap, zs, dz, first),
        out_shape=(
            half,
            half,
            jax.ShapeDtypeStruct((zs, place // 2, rows, width), bf16),
            jax.ShapeDtypeStruct((zs, place // 2, rows, width), bf16),
            jax.ShapeDtypeStruct((zs, slots, width), bf16),
            jax.ShapeDtypeStruct((zs, slots, width), bf16),
            jax.ShapeDtypeStruct((zs, slots, units), bf16),
            jax.ShapeDtypeStruct((zs, slots, 2 * units), bf16),
        ),
        in_specs=[pl.BlockSpec(memory_space=pltpu.SMEM)]
        + [anyspace] * (place + 3)
        + [pl.BlockSpec(memory_space=pltpu.VMEM)]
        + [anyspace] * (len(args) - place - 4),
        out_specs=(anyspace,) * 8,
        scratch_shapes=[
            pltpu.VMEM((place, rows, width), bf16),
            pltpu.VMEM((place, rows, width), bf16),
            pltpu.VMEM((place, code_rows, -(-rows // LANES) * LANES), bf16),
            pltpu.VMEM(wgu.shape, bf16),
            pltpu.VMEM(wd.shape, bf16),
            pltpu.VMEM((place, rows + code_rows, width), bf16),
            pltpu.VMEM((place, rows, width), bf16),
            pltpu.VMEM((slots, width), bf16),
            pltpu.VMEM((slots, width), bf16),
            pltpu.VMEM((slots, units), bf16),
            pltpu.VMEM((slots, 2 * units), bf16),
            pltpu.SemaphoreType.DMA((3 * place + 2,)),
            pltpu.SemaphoreType.DMA((12,)),
        ],
        input_output_aliases=aliases,
        compiler_params=pltpu.CompilerParams(vmem_limit_bytes=VMEM_LIMIT),
        cost_estimate=pl.CostEstimate(
            flops=16 * slots * width * units, bytes_accessed=12 * slots * width, transcendentals=0
        ),
        name="experts",
    )(meta, *args)


def turn_kernel(nparts, seqs, meta, *refs):
    parts = refs[:nparts]
    (
        res_ref,
        up_ref,
        gate_ref,
        code_ref,
        wr_ref,
        gain_ref,
        wo_ref,
        resgrad_ref,
        branch_ref,
        out_ref,
        logit_ref,
        gaingrad_ref,
    ) = refs[nparts:]
    rows, width = res_ref.shape
    span = rows // seqs
    total = parts[0][...].astype(f32)
    for part in parts[1:]:
        total = total + part[...].astype(f32)
    held = -(-rows // LANES) * LANES
    lines = total[rows:, 0:held] + total[rows:, width // 2 : width // 2 + held]
    blank = jnp.zeros((LANES - lines.shape[0], held), f32)
    gate_grad = jnp.concatenate([lines, blank], axis=0).T[0:rows]
    gate_grad = jnp.where(code_ref[...] > 0, gate_grad, 0.0)
    gates = gate_ref[...]
    logit_grad = gates * (gate_grad - jnp.sum(gates * gate_grad, axis=-1, keepdims=True))
    logit_ref[...] = logit_grad
    normed_grad = total[0:rows] + lax.dot_general(
        logit_grad,
        wr_ref[...].astype(f32),
        (((1,), (1,)), ((), ())),
        preferred_element_type=f32,
        precision=lax.Precision.HIGHEST,
    )
    res = res_ref[...]
    scale = lax.rsqrt(jnp.mean(res * res, axis=-1, keepdims=True) + eps)
    gaingrad_ref[...] = jnp.sum(normed_grad * (res * scale), axis=0, keepdims=True)
    scaled = normed_grad * gain_ref[...]
    row = meta[seqs] + lax.broadcasted_iota(jnp.int32, (span, 1), 0)
    valid = jnp.concatenate([(row < meta[s]).astype(f32) for s in range(seqs)], axis=0)
    upstream = jnp.where(valid > 0, up_ref[...].astype(f32), 0.0)
    centre = jnp.mean(scaled * res, axis=-1, keepdims=True)
    res_grad = upstream + scaled * scale - res * (scale * scale * scale * centre)
    resgrad_ref[...] = res_grad
    branch = res_grad.astype(bf16)
    branch_ref[...] = branch
    mixed = dot_nt(branch, wo_ref[...]).astype(bf16).astype(f32)
    half = span // 2
    low = lanes_of(half) < HD
    for s in range(seqs):
        at = slice(s * half, (s + 1) * half)
        for j in range(out_ref.shape[0] // 2):
            cols = slice(j * LANES, (j + 1) * LANES)
            upper = mixed[s * span : s * span + half, cols]
            lower = mixed[s * span + half : (s + 1) * span, cols]
            out_ref[2 * j, at] = jnp.where(low, upper, pltpu.roll(lower, HD, 1)).astype(bf16)
            out_ref[2 * j + 1, at] = jnp.where(low, pltpu.roll(upper, HD, 1), lower).astype(bf16)


def turn(meta, seqs, parts, res, up, gates, code, wr, gain, wo):
    rows, width = res.shape
    heads = wo.shape[0] // HD
    vmem = pl.BlockSpec(memory_space=pltpu.VMEM)
    return pl.pallas_call(
        functools.partial(turn_kernel, len(parts), seqs),
        out_shape=(
            jax.ShapeDtypeStruct((rows, width), f32),
            jax.ShapeDtypeStruct((rows, width), bf16),
            jax.ShapeDtypeStruct((heads, rows // 2, LANES), bf16),
            jax.ShapeDtypeStruct((rows, LANES), f32),
            jax.ShapeDtypeStruct((1, width), f32),
        ),
        in_specs=[pl.BlockSpec(memory_space=pltpu.SMEM)] + [vmem] * (len(parts) + 7),
        out_specs=(vmem,) * 5,
        compiler_params=pltpu.CompilerParams(vmem_limit_bytes=VMEM_LIMIT),
        cost_estimate=pl.CostEstimate(
            flops=4 * rows * width * width, bytes_accessed=4 * width * width, transcendentals=0
        ),
        name="turn_back",
    )(meta, *parts, res, up, gates, code, wr, gain, wo)


def back_kernel(
    replicas,
    meta,
    grad_ref,
    qk_ref,
    v_ref,
    qkt_ref,
    stat_ref,
    cos_ref,
    sin_ref,
    out_ref,
    do_ref,
    dk_ref,
    dv_ref,
    dqt_ref,
):
    zs, place, rows, _ = out_ref.shape
    total = qk_ref.shape[1]
    span = total // (zs * place)
    seqs = rows // span
    s = pl.program_id(0)
    half = span // 2
    for e in range(total // span):
        chunk = grad_ref[e].astype(f32)
        do_ref[e * span : e * span + half, :] = chunk
        do_ref[e * span + half : (e + 1) * span, :] = pltpu.roll(chunk, HD, 1)
    dk_ref[...] = jnp.zeros_like(dk_ref)
    dv_ref[...] = jnp.zeros_like(dv_ref)
    key_row = lax.broadcasted_iota(jnp.int32, (SLAB, SLAB), 0)
    query_col = lax.broadcasted_iota(jnp.int32, (SLAB, SLAB), 1)
    def one_slab(lo):
        hi = lo + 2 * SLAB
        mid = lo + SLAB
        grad = do_ref[lo:hi, :]
        grad_low = grad.astype(bf16)
        grad_t = grad.T[0:HD]
        delta = jnp.sum(grad_t * stat_ref[0, 0:HD, lo:hi], axis=0, keepdims=True)
        grad_t = grad_t.astype(bf16)
        log_total = stat_ref[0, HD : HD + 1, lo:hi]

        def piece(start, stop, first, last, masked):
            cols = slice(first - lo, last - lo)
            scores = dot(qk_ref[0, start:stop, HD:LANES], qkt_ref[0, 0:HD, first:last])
            probs = jnp.exp(scores - log_total[:, cols])
            if masked:
                probs = jnp.where(key_row <= query_col, probs, 0.0)
            prob_grad = dot(v_ref[0, start:stop, 0:HD], grad_t[:, cols])
            score_grad = (probs * (prob_grad - delta[:, cols])).astype(bf16)
            dv_ref[start:stop, :] += dot(probs.astype(bf16), grad_low[cols])
            dk_ref[start:stop, :] += dot(score_grad, qk_ref[0, first:last, :])
            return dot(qkt_ref[0, :, start:stop], score_grad)

        moved = piece(lo, mid, lo, mid, True)
        moved_next = piece(mid, hi, mid, hi, True) + piece(lo, mid, mid, hi, False)
        if lo:
            full = piece(0, lo, lo, hi, False)
            moved = moved + full[:, 0:SLAB]
            moved_next = moved_next + full[:, SLAB:]
        dqt_ref[:, lo:mid] = moved
        dqt_ref[:, mid:hi] = moved_next

    def no_slab(lo):
        dqt_ref[:, lo : lo + 2 * SLAB] = jnp.zeros((LANES, 2 * SLAB), f32)

    for i, lo in enumerate(range(0, total, 2 * SLAB)):
        if replicas > 1:
            mine = meta[seqs] == i % replicas
            pl.when(mine)(functools.partial(one_slab, lo))
            pl.when(jnp.logical_not(mine))(functools.partial(no_slab, lo))
        else:
            one_slab(lo)

    low = lanes_of(SLAB) < HD
    for lo in range(0, total, SLAB):
        at = slice(lo, lo + SLAB)
        both = jnp.where(low, dk_ref[at, :], dqt_ref[:, at].T * HD ** (-0.5))
        both = pltpu.roll(both, HD, 1)
        dk_ref[at, :] = both * cos_ref[at, :] - half_swap(both) * sin_ref[at, :]
        dv_ref[at, :] = jnp.where(low, dv_ref[at, :], 0.0)
    dest = pl.ds(pl.multiple_of(s * span, 32), span)
    for d in range(zs):
        for j in range(place):
            at = pl.multiple_of((meta[seqs + 1 + d] * place + meta[seqs + 1 + zs + j]) * span, 32)
            out_ref[d, j, dest, 0:LANES] = dk_ref[pl.ds(at, span), :].astype(bf16)
            out_ref[d, j, dest, LANES:PACK] = dv_ref[pl.ds(at, span), :].astype(bf16)


def back(meta, grads, qk, v, qkt, stat, cos, sin, shape, seqs, replicas):
    total = qk.shape[1]
    span = total // grads.shape[0]
    return pl.pallas_call(
        functools.partial(back_kernel, replicas),
        grid=(seqs,),
        out_shape=jax.ShapeDtypeStruct(shape, bf16),
        in_specs=[
            pl.BlockSpec(memory_space=pltpu.SMEM),
            pl.BlockSpec((total // span, span // 2, LANES), lambda s: (0, s, 0)),
            pl.BlockSpec((1, total, LANES), lambda s: (s, 0, 0)),
            pl.BlockSpec((1, total, LANES), lambda s: (s, 0, 0)),
            pl.BlockSpec((1, LANES, total), lambda s: (s, 0, 0)),
            pl.BlockSpec((1, HD + 8, total), lambda s: (s, 0, 0)),
            pl.BlockSpec((total, LANES), lambda s: (0, 0)),
            pl.BlockSpec((total, LANES), lambda s: (0, 0)),
        ],
        out_specs=pl.BlockSpec(shape, lambda s: (0, 0, 0, 0)),
        scratch_shapes=[
            pltpu.VMEM((total, LANES), f32),
            pltpu.VMEM((total, LANES), f32),
            pltpu.VMEM((total, LANES), f32),
            pltpu.VMEM((LANES, total), f32),
        ],
        compiler_params=pltpu.CompilerParams(vmem_limit_bytes=VMEM_LIMIT),
        cost_estimate=pl.CostEstimate(
            flops=10 * seqs * total * total * LANES,
            bytes_accessed=6 * seqs * total * PACK,
            transcendentals=seqs * total * total // 2,
        ),
        name="attend_backward",
    )(meta, grads, qk, v, qkt, stat, cos, sin)


def expert_grads_kernel(x_ref, both_ref, act_ref, pg_ref, *refs):
    outs, acc_ref = refs[:-1], refs[-1]
    width = x_ref.shape[2]

    @pl.when(pl.program_id(0) == 0)
    def _():
        acc_ref[...] = jnp.zeros_like(acc_ref)

    acc_ref[0:width, :] += dot_tn(x_ref[0], both_ref[0])
    acc_ref[width:, :] += dot_tn(act_ref[0], pg_ref[0])

    @pl.when(pl.program_id(0) == pl.num_programs(0) - 1)
    def _():
        for k, out_ref in enumerate(outs):
            rows = out_ref.shape[0]
            out_ref[...] = acc_ref[k * rows : (k + 1) * rows, :].astype(bf16)


def expert_grads(x, both, act, pg):
    zs, slots, width = x.shape
    units = act.shape[2]
    pieces = 4
    piece = (width + units) // pieces

    def block(a):
        return pl.BlockSpec((1,) + a.shape[1:], lambda i: (i, 0, 0))

    return pl.pallas_call(
        expert_grads_kernel,
        grid=(zs,),
        out_shape=(jax.ShapeDtypeStruct((piece, width), bf16),) * pieces,
        in_specs=[block(a) for a in (x, both, act, pg)],
        out_specs=(pl.BlockSpec((piece, width), lambda i: (0, 0)),) * pieces,
        scratch_shapes=[pltpu.VMEM((width + units, width), f32)],
        compiler_params=pltpu.CompilerParams(vmem_limit_bytes=VMEM_LIMIT),
        cost_estimate=pl.CostEstimate(
            flops=6 * zs * slots * width * units, bytes_accessed=8 * zs * slots * width, transcendentals=0
        ),
        name="expert_grads",
    )(x, both, act, pg)


def late_kernel(column, mixed_ref, branch_ref, pay_ref, logit_ref, gain_ref, out_ref):
    width = mixed_ref.shape[1]
    out_ref[:, 0:width] = dot_tn(mixed_ref[...], branch_ref[...]).astype(bf16)
    logit = logit_ref[...]
    high = logit.astype(bf16)
    low = (logit - high.astype(f32)).astype(bf16)
    normed = pay_ref[...]
    side = dot_tn(normed, high) + dot_tn(normed, low)
    gain = jnp.broadcast_to(gain_ref[...], (LANES, width)).T
    out_ref[:, width:] = jnp.where(lanes_of(width) == column, gain, side).astype(bf16)


def late_grads(column, mixed, branch, pay, logit, gain):
    rows, width = mixed.shape
    vmem = pl.BlockSpec(memory_space=pltpu.VMEM)
    return pl.pallas_call(
        functools.partial(late_kernel, column),
        out_shape=jax.ShapeDtypeStruct((width, width + LANES), bf16),
        in_specs=[vmem] * 5,
        out_specs=vmem,
        compiler_params=pltpu.CompilerParams(vmem_limit_bytes=VMEM_LIMIT),
        cost_estimate=pl.CostEstimate(
            flops=2 * rows * width * width, bytes_accessed=4 * width * width, transcendentals=0
        ),
        name="late_grads",
    )(mixed, branch, pay, logit, gain)


def head_grads_kernel(dqkv_ref, normed_ref, out_ref, acc_ref):
    _, place, rows, pack = dqkv_ref.shape

    @pl.when(pl.program_id(0) == 0)
    def _():
        acc_ref[...] = jnp.zeros_like(acc_ref)

    left = dqkv_ref[0].reshape(place * rows, pack)
    acc_ref[...] += dot_tn(left, normed_ref[0].reshape(place * rows, normed_ref.shape[3]))

    @pl.when(pl.program_id(0) == pl.num_programs(0) - 1)
    def _():
        out_ref[...] = acc_ref[...].T.astype(bf16)


def head_grads(dqkv, normed):
    zs, place, rows, width = normed.shape
    return pl.pallas_call(
        head_grads_kernel,
        grid=(zs,),
        out_shape=jax.ShapeDtypeStruct((width, PACK), bf16),
        in_specs=[
            pl.BlockSpec((1, place, rows, PACK), lambda i: (i, 0, 0, 0)),
            pl.BlockSpec((1, place, rows, width), lambda i: (i, 0, 0, 0)),
        ],
        out_specs=pl.BlockSpec((width, PACK), lambda i: (0, 0)),
        scratch_shapes=[pltpu.VMEM((PACK, width), f32)],
        compiler_params=pltpu.CompilerParams(vmem_limit_bytes=VMEM_LIMIT),
        cost_estimate=pl.CostEstimate(
            flops=2 * zs * place * rows * width * PACK,
            bytes_accessed=2 * zs * place * rows * width,
            transcendentals=0,
        ),
        name="head_grads",
    )(dqkv, normed)


def spread_kernel(dqkv_ref, w_ref, near_ref, far_ref):
    _, place, rows, pack = dqkv_ref.shape
    for ref, first in ((near_ref, 0), (far_ref, place // 2)):
        for j in range(place // 2):
            ref[0, j] = dot_nt(dqkv_ref[0, first + j], w_ref[...]).astype(bf16)


def spread(dqkv, w, picked):
    _, place, rows, pack = dqkv.shape
    width = w.shape[0]
    first, step = picked[0], (picked[1] - picked[0] if len(picked) > 1 else 0)
    half = jax.ShapeDtypeStruct((len(picked), place // 2, rows, width), bf16)
    out = pl.BlockSpec((1, place // 2, rows, width), lambda i: (i, 0, 0, 0))
    return pl.pallas_call(
        spread_kernel,
        grid=(len(picked),),
        out_shape=(half, half),
        in_specs=[
            pl.BlockSpec((1, place, rows, pack), lambda i: (first + i * step, 0, 0, 0)),
            pl.BlockSpec(w.shape, lambda i: (0, 0)),
        ],
        out_specs=(out, out),
        compiler_params=pltpu.CompilerParams(vmem_limit_bytes=VMEM_LIMIT),
        cost_estimate=pl.CostEstimate(
            flops=2 * len(picked) * place * rows * pack * width,
            bytes_accessed=2 * len(picked) * place * rows * width,
            transcendentals=0,
        ),
        name="spread",
    )(dqkv, w)


def finish_kernel(nparts, *refs):
    hid_ref, gain_ref, resgrad_ref = refs[0:3]
    parts = refs[3 : 3 + nparts]
    out_ref = refs[-1]
    total = parts[0][...].astype(f32)
    for part in parts[1:]:
        total = total + part[...].astype(f32)
    x = hid_ref[...].astype(f32)
    scale = lax.rsqrt(jnp.mean(x * x, axis=-1, keepdims=True) + eps)
    scaled = total * gain_ref[...]
    centre = jnp.mean(scaled * x, axis=-1, keepdims=True)
    out_ref[...] = resgrad_ref[...] + scaled * scale - x * (scale * scale * scale * centre)


def finish(hidden, gain, resgrad, parts):
    vmem = pl.BlockSpec(memory_space=pltpu.VMEM)
    return pl.pallas_call(
        functools.partial(finish_kernel, len(parts)),
        out_shape=jax.ShapeDtypeStruct(hidden.shape, f32),
        in_specs=[vmem] * (3 + len(parts)),
        out_specs=vmem,
        compiler_params=pltpu.CompilerParams(vmem_limit_bytes=VMEM_LIMIT),
        name="input_grad",
    )(hidden, gain, resgrad, *parts)


def body(
    hidden,
    lengths,
    expert_ids,
    pair_keep,
    attn_gain,
    query_weight_matrix,
    key_weight_matrix,
    value_weight_matrix,
    attention_output_weight,
    moe_gain,
    router_weight_matrix,
    w_gate_up,
    w_down,
    out_grad,
):
    seqs, span, width = hidden.shape
    rows = seqs * span
    top_k = expert_ids.shape[2]
    ep = lax.axis_size("ep")
    dp = lax.axis_size("dp")
    zs, ys, _ = ep_shape(ep)
    place = 2 * ys
    me = lax.axis_index("ep").astype(jnp.int32)
    expert_count = w_gate_up.shape[0] * ep
    capacity = max(2, rows * top_k // expert_count)
    cap = -(-capacity // 16) * 16
    heads = query_weight_matrix.shape[1] // HD
    kv_heads = key_weight_matrix.shape[1] // HD
    replicas = ep // heads
    total = span * ep
    own_rows = query_weight_matrix.shape[0]
    hidden = hidden.reshape(rows, width)
    out_grad = out_grad.reshape(rows, width)

    def per_head(weight, count):
        split = weight.reshape(own_rows, count, HD).transpose(1, 0, 2)
        return jnp.repeat(split, heads // count, axis=0)

    small = jnp.concatenate(
        [router_weight_matrix, attn_gain[:, None], moe_gain[:, None]], axis=1
    )
    small = jnp.pad(small, ((0, 0), (0, PACK - 3 * HD - small.shape[1])))
    packed = jnp.concatenate(
        [
            per_head(query_weight_matrix, heads),
            per_head(key_weight_matrix, kv_heads),
            per_head(value_weight_matrix, kv_heads),
            jnp.broadcast_to(small[None], (heads,) + small.shape),
        ],
        axis=2,
    )
    packed = jnp.repeat(packed, replicas, axis=0)
    packed = jnp.broadcast_to(packed[None], (dp,) + packed.shape).reshape(
        dp * ep, own_rows, PACK
    )
    packed = lax.all_to_all(packed, ("dp", "ep"), split_axis=0, concat_axis=0, tiled=True)
    head_w = packed.reshape(dp * ep * own_rows, PACK)
    at = 3 * HD
    wr = jnp.pad(head_w[:, at : at + expert_count], ((0, 0), (0, LANES - expert_count)))
    gains = head_w[:, at + expert_count : at + expert_count + 2].astype(f32)
    gain_one = gains[:, 0].reshape(1, width)
    gain_two = gains[:, 1].reshape(1, width)
    head_w = jnp.where(jnp.arange(PACK)[None, :] < at, head_w, jnp.zeros((), bf16))

    positions = me * span + jnp.arange(span, dtype=jnp.int32)
    is_valid = positions[None, :] < lengths[:, None]

    def prepare(earlier_step):
        expert_range = jnp.arange(LANES, dtype=jnp.int32)
        hit = phase(expert_ids, earlier_step)[0][..., None] == expert_range
        chosen = jnp.any(hit, axis=2).reshape(rows, LANES).astype(f32)
        live = jnp.any(hit & (pair_keep[..., None] > 0), axis=2) & is_valid[..., None]
        live = live.reshape(rows, LANES).astype(bf16)
        earlier = jnp.arange(rows)[:, None] > jnp.arange(rows)[None, :]
        slot = jnp.dot(earlier.astype(bf16), live, preferred_element_type=f32)
        code = jnp.where((slot < capacity) & (live > 0), slot + 1.0, -chosen)
        code_rows = -(-expert_count // 16) * 16
        lines = jnp.pad(code[:, 0:code_rows].T.astype(bf16), ((0, 0), (0, width - rows)))
        lifted = jnp.concatenate([out_grad, lines])

        rates = theta_base ** (-2.0 * jnp.arange(HD // 2, dtype=f32) / HD)
        rates = phase(rates, earlier_step)[0]
        angle = jnp.arange(total, dtype=jnp.int32).astype(f32)[:, None] * rates[None, :]
        cos = jnp.tile(jnp.cos(angle), (1, 4))
        sin = jnp.sin(angle)
        sin = jnp.concatenate([-sin, sin, -sin, sin], axis=1)
        return code, lifted, cos, sin

    core = me % 2
    col = (me // 2) % ys
    plane = me // place
    planes = (plane + jnp.arange(zs, dtype=jnp.int32)) % zs
    rows_at = (col + jnp.arange(ys, dtype=jnp.int32)) % ys
    places = jnp.concatenate([rows_at * 2 + core, rows_at * 2 + 1 - core])
    replica = me % replicas if replicas > 1 else jnp.zeros((), jnp.int32)
    attend_meta = jnp.concatenate([lengths, replica[None], planes, places]).astype(jnp.int32)
    expert_meta = jnp.concatenate([jnp.stack([me, plane]), places]).astype(jnp.int32)
    project_meta = expert_meta[1:]
    turn_meta = jnp.concatenate([lengths, (me * span)[None]]).astype(jnp.int32)

    order = list(range(zs))

    def move(x, sender=False, **offset):
        return lax.ppermute(x, "ep", (send_to if sender else fetch_from)(ep, **offset))

    def steps(t):
        n = len(order)
        return t < n - 1, t < n, 1 <= t <= n, 2 <= t < n + 2

    columns, near, far, carried, x = [hidden], {}, {}, None, hidden
    wo_part = [attention_output_weight]
    for t in range(len(order) + 2):
        on_z, on_y, on_core, on_work = steps(t)
        z_new = [move(columns[t], dz=1)] if on_z else []
        y_new = [move(columns[t], dy=k) for k in range(1, ys)] if on_y else []
        c_new = [move(block, dc=1) for block in near[t - 1]] if on_core else []
        if on_work:
            d = order[t - 2]
            carried = project(
                project_meta, near[t - 2] + far[t - 2], head_w, gain_one, cos, sin, zs, d, carried
            )
        block = wo_part[0]
        wo_new = []
        if t == zs - 1:
            wo_new = [move(block, dz=k) for k in range(1, zs)]
        elif t == zs:
            wo_new = [move(block, dy=k) for k in range(1, ys)]
        x, columns, near, far, z_new, y_new, c_new, carried, wo_part, wo_new = phase_tree(
            x, columns, near, far, z_new, y_new, c_new, carried, wo_part, wo_new
        )
        if wo_new:
            wo_part = [jnp.stack(wo_part + wo_new)]
        columns = columns + z_new
        if on_y:
            near[t] = [columns[t]] + y_new
        if on_core:
            far[t - 1] = c_new
        if t == 0:
            code, lifted, cos, sin = prepare(columns[-1])
        if t == len(order) - 2:
            upstream = lax.all_gather(phase(lifted, columns[-1])[0], "ep", axis=0)
    wo_new = [
        lax.ppermute(wo_part[0], "dp", [((i + k) % dp, i) for i in range(dp)]) for k in range(1, dp)
    ]
    normed_all, qkv = carried
    made, qk, v, qkt, stat = attend(attend_meta, qkv, seqs, replicas)
    made, wo_new, wo_part = phase_tree(made, wo_new, wo_part)
    recv = lax.all_to_all(made, "ep", split_axis=0, concat_axis=0, tiled=True)
    wo_part = jnp.stack(wo_part + wo_new)
    wo_part = [jnp.stack([wo_part, move(wo_part, dc=1)])]
    line = jnp.arange(dp * ep, dtype=jnp.int32)
    away = (line % 2 - core) % 2
    away = away * dp + (line // ep - lax.axis_index("dp")) % dp
    away = away * ys + ((line // 2) % ys - col) % ys
    away = away * zs + ((line // place) % zs - plane) % zs
    wo = wo_part[0].reshape(dp * ep, own_rows, width)
    wo = jnp.take(wo, away, axis=0, mode="clip").reshape(heads * HD, width)
    if replicas > 1:
        recv = recv.reshape((heads, replicas) + recv.shape[1:]).sum(axis=1).astype(bf16)
    res, pay, mixed, gates = middle(seqs, recv, hidden, wo, gain_two, wr, code)

    count = zs
    columns, near, far, chips, totals = [pay], {}, {}, {}, {}
    outs, carried, extra, passed = {}, None, {}, None
    rings = [[(i, (i + d) % dp) for i in range(dp)] for d in range(1, dp)]
    cuts = ((1,), tuple(range(2, zs)), (0,))

    def hop(value):
        return lax.ppermute(value, "ep", fetch_from(ep, dz=1))

    def swap(piece):
        return [lax.ppermute(piece, "dp", ring) for ring in rings]

    for t in range(count + 5):
        on_z, on_y, on_core, on_work = steps(t)
        z_new = [move(columns[t], dz=1)] if on_z else []
        y_new = [move(columns[t], dy=k) for k in range(1, ys)] if on_y else []
        c_new = [move(block, dc=1) for block in near[t - 1]] if on_core else []
        rc, ry, rz = t - 3, t - 4, t - 5
        rc_new = [move(outs[rc][1], True, dc=1)] if 0 <= rc < count else []
        ry_new = [move(chips[ry][d], True, dy=d) for d in range(1, ys)] if 0 <= ry < count else []
        rz_new = []
        if 1 <= rz < count:
            rz_new = [hop(totals[rz] if rz == 1 else add_low(totals[rz], passed))]
        new = {}
        if on_work:
            d = order[t - 2]
            out = experts(
                expert_meta,
                near[t - 2] + far[t - 2],
                upstream,
                w_gate_up[0],
                w_down[0],
                wr,
                cap,
                zs,
                d,
                carried,
            )
            outs[t - 2], carried = out[:2], out[2:]
        if t == count + 2:
            new["got"] = move(carried[1], True, dc=1)
            new["grads"] = list(expert_grads(carried[2], carried[5], carried[4], carried[3]))
        if t == count + 3:
            new["chip"] = [
                [
                    add_low(
                        jnp.stack([carried[0][k, d] for k in cut]),
                        jnp.stack([extra["got"][k, d] for k in cut]),
                    )
                    for cut in cuts
                    if cut
                ]
                for d in range(ys)
            ]
        if t == count + 4:
            new["swap"] = swap(extra["grads"][0])
            new["first"] = [move(extra["chip"][d][0], True, dy=d) for d in range(1, ys)]
        state = (pay, columns, near, far, outs, chips, totals, carried, extra)
        state = phase_tree(state, z_new, y_new, c_new, rc_new, ry_new, rz_new, new)
        state, z_new, y_new, c_new, rc_new, ry_new, rz_new, new = state
        pay, columns, near, far, outs, chips, totals, carried, extra = state
        columns = columns + z_new
        if on_y:
            near[t] = [columns[t]] + y_new
        if on_core:
            far[t - 1] = c_new
        if rc_new:
            chips[rc] = [add_low(outs[rc][0][d], rc_new[0][d]) for d in range(ys)]
        if 0 <= ry < count:
            totals[ry] = add_low(chips[ry][0], *ry_new)
        if rz_new:
            passed = rz_new[0]
        extra.update(new)
    parts = [totals[0]] + ([passed] if zs > 1 else [])
    moe_chip = extra["chip"]
    grads_low = extra["grads"]

    res_grad, branch, grads, logit_grad, gain_two_grad = turn(
        turn_meta, seqs, parts, res, out_grad, gates, code, wr, gain_two, wo
    )
    if replicas > 1:
        grads = jnp.repeat(grads, replicas, axis=0)
    grads = lax.all_to_all(grads, "ep", split_axis=0, concat_axis=0, tiled=True)
    late = late_grads(expert_count, mixed, branch, pay, logit_grad, gain_two_grad)
    late = late.reshape(dp, zs * ys, 2, own_rows, late.shape[1])

    def stage_parts(value, axis, here_at, size):
        return [
            lax.dynamic_index_in_dim(value, (here_at + d) % size, axis, keepdims=False)
            for d in range(size)
        ]

    late_parts = stage_parts(late, 2, core, 2)
    moe = [add_low(moe_chip[0][0], *extra["first"])]
    moe_new = [move(moe_chip[d][1], True, dy=d) for d in range(1, ys)]
    grads_moved = [extra["swap"], swap(grads_low[1])]
    state = (grads, moe, moe_new, moe_chip, late_parts, grads_low, grads_moved)
    grads, moe, moe_new, moe_chip, late_parts, grads_low, grads_moved = phase_tree(*state)
    moe.append(add_low(moe_chip[0][1], *moe_new))

    dqkv = back(attend_meta, grads, qk, v, qkt, stat, cos, sin, qkv.shape, seqs, replicas)
    moe_new = [move(moe_chip[d][2], True, dy=d) for d in range(1, ys)]
    passed = hop(moe[0][0])
    late_got = [move(late_parts[1], True, dc=1)]
    swapped = swap(grads_low[2])
    state = (dqkv, moe, moe_new, passed, moe_chip, late_parts, late_got, grads_low, swapped)
    state = phase_tree(*state)
    dqkv, moe, moe_new, passed, moe_chip, late_parts, late_got, grads_low, swapped = state
    moe.append(add_low(moe_chip[0][2], *moe_new))
    grads_moved.append(swapped)
    late = add_low(late_parts[0], *late_got)
    late_parts = stage_parts(late, 0, lax.axis_index("dp"), dp)
    late_got = [lax.ppermute(part, "dp", ring) for part, ring in zip(late_parts[1:], rings)]

    halves = ((1, 2), (3, 0)) if zs == 4 else (tuple(range(1, zs)), (0,))
    turn_order = [d for half in halves for d in half]
    near, far = ([part] for part in spread(dqkv, head_w, halves[0]))
    near, far, dqkv = phase_tree(near, far, dqkv)

    got = [move(far[0], True, dc=1)]
    more = spread(dqkv, head_w, halves[1])
    near.append(more[0])
    far.append(more[1])
    passed = hop(add_low(moe[1][0], passed))
    head_grad = head_grads(dqkv, normed_all).reshape(dp * ep, own_rows, PACK)
    state = (near, far, got, moe, passed, head_grad, late_parts, late_got, grads_low)
    near, far, got, moe, passed, head_grad, late_parts, late_got, grads_low = phase_tree(*state)
    late = add_low(late_parts[0], *late_got)
    plane_groups = [[c + 2 * k for k in range(zs * ys)] for c in range(2)]
    late = lax.all_to_all(
        late, "ep", split_axis=0, concat_axis=0, tiled=True, axis_index_groups=plane_groups
    )

    head_grad = lax.all_to_all(head_grad, ("dp", "ep"), split_axis=0, concat_axis=0, tiled=True)
    totals, received = {}, None

    def chip_of(d):
        half = 0 if d in halves[0] else 1
        at = halves[half].index(d)
        return [add_low(near[half][at, y], got[half][at, y]) for y in range(ys)]

    chip = chip_of(turn_order[0])
    for k, d in enumerate(turn_order):
        ahead = chip_of(turn_order[k + 1]) if k + 1 < len(turn_order) else []
        moved = [move(chip[y], True, dy=y) for y in range(1, ys)]
        if k:
            last = totals[turn_order[k - 1]]
            received = hop(last if k == 1 else add_low(last, received))
        if k == 0:
            got.append(move(far[1], True, dc=1))
            passed = hop(add_low(moe[1][1], passed)) if zs == 4 else passed
            swapped = swap(grads_low[3])
            near, got, chip, ahead, moved, passed, swapped = phase_tree(
                near, got, chip, ahead, moved, passed, swapped
            )
            grads_moved.append(swapped)
        elif k == 2:
            near, got, chip, ahead, moved, received, totals, head_grad = phase_tree(
                near, got, chip, ahead, moved, received, totals, head_grad
            )
        else:
            near, got, chip, ahead, moved, received, totals = phase_tree(
                near, got, chip, ahead, moved, received, totals
            )
        totals[d] = add_low(chip[0], *moved)
        chip = ahead
    parts = [totals[0], received]
    late = phase(late, totals[0], received)[0]
    late = late.astype(f32).sum(axis=0)
    mparts = [moe[-1][0], passed]
    sums = []
    for own, moved in zip(grads_low, grads_moved):
        piece = own.astype(f32)
        for other in moved:
            piece = piece + other.astype(f32)
        sums.append(piece)
    grads_total = jnp.concatenate(sums)
    gu_total = grads_total[0:width]
    d_total = grads_total[width:]

    head_grad = head_grad.astype(f32).reshape(dp, heads, replicas, own_rows, PACK).sum(axis=(0, 2))

    def rows_of(part, count):
        part = part.reshape(count, heads // count, own_rows, HD).sum(axis=1)
        return part.transpose(1, 0, 2).reshape(own_rows, count * HD)

    query_w_grad = rows_of(head_grad[..., 0:HD], heads)
    key_w_grad = rows_of(head_grad[..., HD : 2 * HD], kv_heads)
    value_w_grad = rows_of(head_grad[..., 2 * HD : 3 * HD], kv_heads)
    gain_one_grad = (
        jnp.sum(query_w_grad * query_weight_matrix.astype(f32), axis=1)
        + jnp.sum(key_w_grad * key_weight_matrix.astype(f32), axis=1)
        + jnp.sum(value_w_grad * value_weight_matrix.astype(f32), axis=1)
    ) / attn_gain.astype(f32)

    moe_own = res
    for part in mparts:
        moe_own = moe_own + part.astype(f32)
    output = jnp.where(
        is_valid[..., None], moe_own.reshape(seqs, span, width), 0.0
    ).astype(bf16)
    input_grad = finish(hidden, gain_one, res_grad, parts)
    model = width
    return (
        output,
        input_grad.reshape(seqs, span, width),
        gain_one_grad,
        query_w_grad,
        key_w_grad,
        value_w_grad,
        late[:, 0:model],
        late[:, model + expert_count],
        late[:, model : model + expert_count],
        gu_total[None],
        d_total[None],
    )


def solution(mesh):
    return jax.shard_map(
        body,
        mesh=mesh,
        in_specs=(
            P("dp", "ep", None),
            P("dp"),
            P("dp", "ep", None),
            P("dp", "ep", None),
            P(("dp", "ep")),
            P(("dp", "ep"), None),
            P(("dp", "ep"), None),
            P(("dp", "ep"), None),
            P(("dp", "ep"), None),
            P(("dp", "ep")),
            P(("dp", "ep"), None),
            P("ep", None, None),
            P("ep", None, None),
            P("dp", "ep", None),
        ),
        out_specs=(
            P("dp", "ep", None),
            P("dp", "ep", None),
            P(("dp", "ep")),
            P(("dp", "ep"), None),
            P(("dp", "ep"), None),
            P(("dp", "ep"), None),
            P(("dp", "ep"), None),
            P(("dp", "ep")),
            P(("dp", "ep"), None),
            P("ep", None, None),
            P("ep", None, None),
        ),
        check_vma=False,
    )
```

```python
import functools

import jax
import jax.numpy as jnp
from jax import lax
from jax.experimental import pallas as pl
from jax.experimental.pallas import tpu as pltpu
from jax.sharding import PartitionSpec as P

HD = 64
LANES = 128
SLAB = 256
WIDE = 512
PACK = 256
eps = 1e-05
theta_base = 10000.0
f32 = jnp.float32
bf16 = jnp.bfloat16
VMEM_LIMIT = 56 * 1024 * 1024


def dot(a, b):
    return lax.dot_general(a, b, (((1,), (0,)), ((), ())), preferred_element_type=f32)


def dot_nt(a, b):
    return lax.dot_general(a, b, (((1,), (1,)), ((), ())), preferred_element_type=f32)


def dot_tn(a, b):
    return lax.dot_general(a, b, (((0,), (0,)), ((), ())), preferred_element_type=f32)


def lanes_of(rows, width=LANES):
    return lax.broadcasted_iota(jnp.int32, (rows, width), 1)


def half_swap(x):
    lane = lanes_of(x.shape[0])
    return jnp.where(lane % HD < HD // 2, pltpu.roll(x, LANES - HD // 2, 1), pltpu.roll(x, HD // 2, 1))


def ep_shape(ep):
    zs = 4 if ep % 8 == 0 else 1
    return zs, ep // (2 * zs), 2


def fetch_from(ep, dz=0, dy=0, dc=0):
    zs, ys, cs = ep_shape(ep)
    pairs = []
    for z in range(zs):
        for y in range(ys):
            for c in range(cs):
                src = (((z + dz) % zs) * ys + (y + dy) % ys) * cs + (c + dc) % cs
                pairs.append((src, (z * ys + y) * cs + c))
    return pairs


def send_to(ep, **offset):
    return [(dst, src) for src, dst in fetch_from(ep, **offset)]


def phase(*values):
    return lax.optimization_barrier(values)


def phase_tree(*values):
    flat, tree = jax.tree.flatten(values)
    return jax.tree.unflatten(tree, phase(*flat))


def add_low(*parts):
    total = parts[0].astype(f32)
    for part in parts[1:]:
        total = total + part.astype(f32)
    return total.astype(bf16)


def project_kernel(place, carry, meta, *refs):
    blocks = refs[:place]
    w_ref, gain_ref, cos_ref, sin_ref = refs[place : place + 4]
    normed_ref, qkv_ref = refs[-2:]
    rows, _ = blocks[0].shape
    span = cos_ref.shape[0] // place
    seqs = rows // span
    lane = lanes_of(rows)
    for j in range(place):
        x = blocks[j][...].astype(f32)
        scale = lax.rsqrt(jnp.mean(x * x, axis=-1, keepdims=True) + eps)
        normed = (x * scale * gain_ref[...]).astype(bf16)
        normed_ref[0, j] = normed
        raw = dot(normed, w_ref[...])
        at = pl.ds(pl.multiple_of(meta[1 + j] * span, 32), span)
        cos = jnp.concatenate([cos_ref[at, :]] * seqs, axis=0)
        sin = jnp.concatenate([sin_ref[at, :]] * seqs, axis=0)
        both = raw[:, 0:LANES]
        both = (both * cos + half_swap(both) * sin).astype(bf16).astype(f32)
        both = jnp.where(lane < HD, both * HD ** (-0.5), both)
        qkv_ref[0, j, :, 0:LANES] = both.astype(bf16)
        qkv_ref[0, j, :, LANES:PACK] = jnp.where(lane < HD, raw[:, LANES:PACK], 0.0).astype(bf16)


def project(meta, blocks, w, gain, cos, sin, zs, dz, carried):
    rows, width = blocks[0].shape
    place = len(blocks)
    span = cos.shape[0] // (zs * place)

    def whole(a):
        return pl.BlockSpec(a.shape, lambda i, m: (0,) * a.ndim)

    table = pl.BlockSpec((place * span, LANES), lambda i, m: (lax.rem(m[0] + dz, zs), 0))
    args = list(blocks) + [w, gain, cos, sin]
    in_specs = [whole(a) for a in blocks] + [whole(w), whole(gain), table, table]
    aliases = {}
    if carried is not None:
        aliases = {1 + len(args): 0, 2 + len(args): 1}
        args += list(carried)
        in_specs += [pl.BlockSpec(memory_space=pl.ANY)] * 2
    return pl.pallas_call(
        functools.partial(project_kernel, place, carried is not None),
        grid_spec=pltpu.PrefetchScalarGridSpec(
            num_scalar_prefetch=1,
            grid=(1,),
            in_specs=in_specs,
            out_specs=(
                pl.BlockSpec((1, place, rows, width), lambda i, m: (dz, 0, 0, 0)),
                pl.BlockSpec((1, place, rows, PACK), lambda i, m: (dz, 0, 0, 0)),
            ),
        ),
        out_shape=(
            jax.ShapeDtypeStruct((zs, place, rows, width), bf16),
            jax.ShapeDtypeStruct((zs, place, rows, PACK), bf16),
        ),
        input_output_aliases=aliases,
        compiler_params=pltpu.CompilerParams(vmem_limit_bytes=VMEM_LIMIT),
        cost_estimate=pl.CostEstimate(
            flops=2 * place * rows * width * PACK,
            bytes_accessed=4 * place * rows * width,
            transcendentals=0,
        ),
        name="project_in",
    )(meta, *args)


def attend_kernel(
    replicas,
    meta,
    qkv_ref,
    out_ref,
    qk_ref,
    v_ref,
    qkt_ref,
    stat_ref,
    vt_ref,
    wide_ref,
):
    zs, place, rows, _ = qkv_ref.shape
    total = qk_ref.shape[1]
    span = total // (zs * place)
    s = pl.program_id(0)
    seqs = rows // span
    source = pl.ds(pl.multiple_of(s * span, 32), span)
    for d in range(zs):
        for j in range(place):
            at = pl.multiple_of((meta[seqs + 1 + d] * place + meta[seqs + 1 + zs + j]) * span, 32)
            qk_ref[0, pl.ds(at, span), :] = qkv_ref[d, j, source, 0:LANES]
            v_ref[0, pl.ds(at, span), :] = qkv_ref[d, j, source, LANES:PACK]
    for lo in range(0, total, SLAB):
        at = slice(lo, lo + SLAB)
        qkt_ref[0, :, at] = qk_ref[0, at, :].astype(f32).T.astype(bf16)
        vt_ref[:, at] = v_ref[0, at, :].astype(f32).T.astype(bf16)

    key_row = lax.broadcasted_iota(jnp.int32, (WIDE, WIDE), 0)
    query_col = lax.broadcasted_iota(jnp.int32, (WIDE, WIDE), 1)

    def one_slab(lo):
        hi = lo + WIDE
        qt = qkt_ref[0, 0:HD, lo:hi]
        diag = dot(qk_ref[0, lo:hi, HD:LANES], qt)
        diag = jnp.where(key_row <= query_col, diag, -jnp.inf)
        top = jnp.max(diag, axis=0, keepdims=True)
        if lo:
            full = dot(qk_ref[0, 0:lo, HD:LANES], qt)
            top = jnp.maximum(top, jnp.max(full, axis=0, keepdims=True))
        p_diag = jnp.exp(diag - top)
        row_total = jnp.sum(p_diag, axis=0, keepdims=True)
        out = dot(vt_ref[:, lo:hi], p_diag.astype(bf16))
        if lo:
            p_full = jnp.exp(full - top)
            row_total = row_total + jnp.sum(p_full, axis=0, keepdims=True)
            out = out + dot(vt_ref[:, 0:lo], p_full.astype(bf16))
        out = out[0:HD] / row_total
        stat_ref[0, 0:HD, lo:hi] = out
        stat_ref[0, HD : HD + 8, lo:hi] = jnp.broadcast_to(top + jnp.log(row_total), (8, WIDE))
        wide_ref[lo:hi, :] = jnp.concatenate([out, out], axis=0).T

    def no_slab(lo):
        stat_ref[0, :, lo : lo + WIDE] = jnp.zeros((HD + 8, WIDE), f32)
        wide_ref[lo : lo + WIDE, :] = jnp.zeros((WIDE, LANES), f32)

    for i, lo in enumerate(range(0, total, WIDE)):
        if replicas > 1:
            mine = meta[seqs] == i % replicas
            pl.when(mine)(functools.partial(one_slab, lo))
            pl.when(jnp.logical_not(mine))(functools.partial(no_slab, lo))
        else:
            one_slab(lo)

    half = span // 2
    for e in range(total // span):
        upper = wide_ref[e * span : e * span + half, :]
        lower = wide_ref[e * span + half : (e + 1) * span, :]
        out_ref[e] = jnp.where(lanes_of(half) < HD, upper, lower).astype(bf16)


def attend(meta, qkv, seqs, replicas):
    zs, place, rows, _ = qkv.shape
    span = rows // seqs
    total = zs * place * span
    return pl.pallas_call(
        functools.partial(attend_kernel, replicas),
        grid=(seqs,),
        out_shape=(
            jax.ShapeDtypeStruct((total // span, seqs * (span // 2), LANES), bf16),
            jax.ShapeDtypeStruct((seqs, total, LANES), bf16),
            jax.ShapeDtypeStruct((seqs, total, LANES), bf16),
            jax.ShapeDtypeStruct((seqs, LANES, total), bf16),
            jax.ShapeDtypeStruct((seqs, HD + 8, total), f32),
        ),
        in_specs=[
            pl.BlockSpec(memory_space=pltpu.SMEM),
            pl.BlockSpec(qkv.shape, lambda s: (0, 0, 0, 0)),
        ],
        out_specs=(
            pl.BlockSpec((total // span, span // 2, LANES), lambda s: (0, s, 0)),
            pl.BlockSpec((1, total, LANES), lambda s: (s, 0, 0)),
            pl.BlockSpec((1, total, LANES), lambda s: (s, 0, 0)),
            pl.BlockSpec((1, LANES, total), lambda s: (s, 0, 0)),
            pl.BlockSpec((1, HD + 8, total), lambda s: (s, 0, 0)),
        ),
        scratch_shapes=[pltpu.VMEM((LANES, total), bf16), pltpu.VMEM((total, LANES), f32)],
        compiler_params=pltpu.CompilerParams(vmem_limit_bytes=VMEM_LIMIT),
        cost_estimate=pl.CostEstimate(
            flops=4 * seqs * total * total * LANES,
            bytes_accessed=4 * seqs * total * PACK,
            transcendentals=seqs * total * total // 2,
        ),
        name="attend_forward",
    )(meta, qkv)


def gates_of(normed, wr_ref, code):
    logits = jnp.where(code != 0, dot(normed, wr_ref[...]), -1e30)
    powers = jnp.exp(logits - jnp.max(logits, axis=-1, keepdims=True))
    return powers / jnp.sum(powers, axis=-1, keepdims=True)


def middle_kernel(
    seqs,
    recv_ref,
    hid_ref,
    wo_ref,
    gain_ref,
    wr_ref,
    code_ref,
    res_ref,
    pay_ref,
    mixed_ref,
    gate_ref,
):
    heads, half_rows, _ = recv_ref.shape
    width = hid_ref.shape[1]
    half = half_rows // seqs
    low = lanes_of(half_rows) < HD
    uppers, lowers = [], []
    for j in range(heads // 2):
        a = recv_ref[2 * j].astype(f32)
        b = recv_ref[2 * j + 1].astype(f32)
        uppers.append(jnp.where(low, a, pltpu.roll(b, HD, 1)).astype(bf16))
        lowers.append(jnp.where(low, pltpu.roll(a, HD, 1), b).astype(bf16))
    upper = jnp.concatenate(uppers, axis=1)
    lower = jnp.concatenate(lowers, axis=1)
    pieces = []
    for s in range(seqs):
        pieces += [upper[s * half : (s + 1) * half], lower[s * half : (s + 1) * half]]
    mixed = jnp.concatenate(pieces, axis=0)
    mixed_ref[...] = mixed
    res = hid_ref[...].astype(f32) + dot(mixed, wo_ref[...])
    res_ref[...] = res
    scale = lax.rsqrt(jnp.mean(res * res, axis=-1, keepdims=True) + eps)
    normed = (res * scale * gain_ref[...]).astype(bf16)
    gate_ref[...] = gates_of(normed, wr_ref, code_ref[...])
    pay_ref[...] = normed


def middle(seqs, recv, hid, wo, gain, wr, code):
    rows, width = hid.shape
    vmem = pl.BlockSpec(memory_space=pltpu.VMEM)
    return pl.pallas_call(
        functools.partial(middle_kernel, seqs),
        out_shape=(
            jax.ShapeDtypeStruct((rows, width), f32),
            jax.ShapeDtypeStruct((rows, width), bf16),
            jax.ShapeDtypeStruct((rows, width), bf16),
            jax.ShapeDtypeStruct((rows, LANES), f32),
        ),
        in_specs=[vmem] * 6,
        out_specs=(vmem,) * 4,
        compiler_params=pltpu.CompilerParams(vmem_limit_bytes=VMEM_LIMIT),
        cost_estimate=pl.CostEstimate(
            flops=4 * rows * width * width, bytes_accessed=4 * width * width, transcendentals=0
        ),
        name="project_out",
    )(recv, hid, wo, gain, wr, code)


def expert_kernel(place, cap, zs, dz, first, meta, *refs):
    pay_in = refs[0:place]
    up_in, wgu_in, wd_in, wr_ref = refs[place : place + 4]
    rest = refs[place + 4 + (0 if first else 6) :]
    near_out, far_out, mnear_out, mfar_out, x_out, pg_out, act_out, both_out = rest[:8]
    pay, up, code, wgu, wd, back_s, moe_s, x_s, pg_s, act_s, both_s, in_sem, out_sem = rest[8:]
    rows, width = pay_in[0].shape
    units = wd.shape[0]
    halves = place // 2
    expert = meta[0]
    plane = lax.rem(meta[1] + dz, zs)
    loads = {}
    order = []
    for j in range(place):
        loads["p", j] = pltpu.make_async_copy(pay_in[j], pay.at[j], in_sem.at[2 * j])
        source = up_in.at[plane * place + meta[2 + j]]
        loads["u", j] = pltpu.make_async_copy(
            source.at[pl.ds(0, rows)], up.at[j], in_sem.at[2 * j + 1]
        )
        loads["c", j] = pltpu.make_async_copy(
            source.at[pl.ds(rows, code.shape[1]), pl.ds(0, code.shape[2])],
            code.at[j],
            in_sem.at[2 * place + 2 + j],
        )
    loads["gu"] = pltpu.make_async_copy(wgu_in, wgu, in_sem.at[2 * place])
    loads["d"] = pltpu.make_async_copy(wd_in, wd, in_sem.at[2 * place + 1])
    order = [("c", j) for j in range(place)]
    order += [("p", j) for j in range(halves)] + ["gu", "d"]
    order += [("u", j) for j in range(halves)]
    order += [("p", j) for j in range(halves, place)] + [("u", j) for j in range(halves, place)]
    for key in order:
        loads[key].start()
    stores = []

    def store(src, dst):
        copy = pltpu.make_async_copy(src, dst, out_sem.at[len(stores)])
        copy.start()
        stores.append(copy)

    def save(h, value, buf, out):
        own = pl.ds(h * halves * cap, halves * cap)
        buf[own, :] = value
        store(buf.at[own], out.at[dz, own])

    lane = lanes_of(rows)
    slot_row = lax.broadcasted_iota(jnp.int32, (cap, rows), 0)
    slot_col = lax.broadcasted_iota(jnp.int32, (rows, cap), 1)
    code_row = lax.broadcasted_iota(jnp.int32, (code.shape[1], rows), 0)
    cap_lane = lanes_of(cap)
    line_row = lax.broadcasted_iota(jnp.int32, code.shape[1:], 0)
    slot_wide = lax.broadcasted_iota(jnp.int32, (cap, code.shape[2]), 0)
    for h in range(2):
        mine = range(h * halves, (h + 1) * halves)
        for j in mine:
            loads["c", j].wait()
            loads["p", j].wait()
        outs_of, xs, gates = [], [], []
        into, into_wide = [], []
        for j in mine:
            lines = code[j].astype(f32)
            blank = jnp.zeros((LANES - lines.shape[0], lines.shape[1]), f32)
            codes = jnp.concatenate([lines, blank], axis=0).T[0:rows]
            column = jnp.sum(jnp.where(lane == expert, codes, 0.0), axis=1, keepdims=True)
            line = jnp.sum(
                jnp.where(code_row == expert, lines[:, 0:rows], 0.0), axis=0, keepdims=True
            )
            into.append(jnp.where(line.astype(jnp.int32) == slot_row + 1, 1.0, 0.0).astype(bf16))
            line = jnp.sum(jnp.where(line_row == expert, lines, 0.0), axis=0, keepdims=True)
            into_wide.append(
                jnp.where(line.astype(jnp.int32) == slot_wide + 1, 1.0, 0.0).astype(bf16)
            )
            outs_of.append(
                jnp.where(column.astype(jnp.int32) == slot_col + 1, 1.0, 0.0).astype(bf16)
            )
            xs.append(dot(into[-1], pay[j]).astype(bf16))
            gate = gates_of(xs[-1], wr_ref, dot(into[-1], codes.astype(bf16)))
            gates.append(jnp.sum(jnp.where(cap_lane == expert, gate, 0.0), axis=1, keepdims=True))
        x = jnp.concatenate(xs, axis=0)
        gate_prob = jnp.concatenate(gates, axis=0)
        if h == 0:
            loads["gu"].wait()
        save(h, x, x_s, x_out)
        gate_up = dot(x, wgu[...])
        gate = gate_up[:, 0:units]
        high = gate_up[:, units:]
        sig = jax.nn.sigmoid(gate)
        silu = gate * sig
        act = (silu * high).astype(bf16)
        if h == 0:
            loads["d"].wait()
        save(h, act, act_s, act_out)
        made = dot(act, wd[...]).astype(bf16).astype(f32)
        for j in mine:
            loads["u", j].wait()
        upstream = jnp.concatenate([dot(into[k], up[j]) for k, j in enumerate(mine)], axis=0)
        gate_grad = jnp.sum(made * upstream, axis=-1, keepdims=True)
        moe = (made * gate_prob).astype(bf16)
        pair_grad = (upstream * gate_prob).astype(bf16)
        for k, j in enumerate(mine):
            part = slice(k * cap, (k + 1) * cap)
            moe_s[j] = dot(outs_of[k], moe[part]).astype(bf16)
        store(moe_s.at[pl.ds(h * halves, halves)], (mnear_out if h == 0 else mfar_out).at[dz])
        save(h, pair_grad, pg_s, pg_out)
        act_grad = dot_nt(pair_grad, wd[...])
        both = jnp.concatenate(
            [act_grad * high * (sig * (1.0 + gate * (1.0 - sig))), act_grad * silu], axis=1
        ).astype(bf16)
        save(h, both, both_s, both_out)
        back = dot_nt(both, wgu[...]).astype(bf16)
        upper = gate_grad.astype(bf16).astype(f32)
        pair_lane = lanes_of(halves * cap)
        pair = jnp.where(pair_lane == 0, upper, gate_grad - upper)
        for k, j in enumerate(mine):
            part = slice(k * cap, (k + 1) * cap)
            back_s[j, 0:rows, :] = dot(outs_of[k], back[part]).astype(bf16)
            found = dot(pair[part].T[0:16].astype(bf16), into_wide[k])
            back_s[j, rows:, :] = jnp.zeros((code.shape[1], width), bf16)
            for row, at in ((0, 0), (1, width // 2)):
                value = jnp.where(line_row == expert, found[row : row + 1], 0.0)
                back_s[j, rows:, at : at + code.shape[2]] = value.astype(bf16)
        store(back_s.at[pl.ds(h * halves, halves)], near_out if h == 0 else far_out)
    for copy in stores:
        copy.wait()


def experts(meta, pays, upstream, wgu, wd, wr, cap, zs, dz, carried):
    place = len(pays)
    rows, width = pays[0].shape
    units = wd.shape[0]
    first = carried is None
    anyspace = pl.BlockSpec(memory_space=pl.ANY)
    args = list(pays) + [upstream, wgu, wd, wr]
    code_rows = upstream.shape[1] - rows
    aliases = {}
    if not first:
        aliases = {1 + len(args) + k: 2 + k for k in range(6)}
        args += list(carried)
    half = jax.ShapeDtypeStruct((place // 2, rows + code_rows, width), bf16)
    slots = place * cap
    return pl.pallas_call(
        functools.partial(expert_kernel, place, cap, zs, dz, first),
        out_shape=(
            half,
            half,
            jax.ShapeDtypeStruct((zs, place // 2, rows, width), bf16),
            jax.ShapeDtypeStruct((zs, place // 2, rows, width), bf16),
            jax.ShapeDtypeStruct((zs, slots, width), bf16),
            jax.ShapeDtypeStruct((zs, slots, width), bf16),
            jax.ShapeDtypeStruct((zs, slots, units), bf16),
            jax.ShapeDtypeStruct((zs, slots, 2 * units), bf16),
        ),
        in_specs=[pl.BlockSpec(memory_space=pltpu.SMEM)]
        + [anyspace] * (place + 3)
        + [pl.BlockSpec(memory_space=pltpu.VMEM)]
        + [anyspace] * (len(args) - place - 4),
        out_specs=(anyspace,) * 8,
        scratch_shapes=[
            pltpu.VMEM((place, rows, width), bf16),
            pltpu.VMEM((place, rows, width), bf16),
            pltpu.VMEM((place, code_rows, -(-rows // LANES) * LANES), bf16),
            pltpu.VMEM(wgu.shape, bf16),
            pltpu.VMEM(wd.shape, bf16),
            pltpu.VMEM((place, rows + code_rows, width), bf16),
            pltpu.VMEM((place, rows, width), bf16),
            pltpu.VMEM((slots, width), bf16),
            pltpu.VMEM((slots, width), bf16),
            pltpu.VMEM((slots, units), bf16),
            pltpu.VMEM((slots, 2 * units), bf16),
            pltpu.SemaphoreType.DMA((3 * place + 2,)),
            pltpu.SemaphoreType.DMA((12,)),
        ],
        input_output_aliases=aliases,
        compiler_params=pltpu.CompilerParams(vmem_limit_bytes=VMEM_LIMIT),
        cost_estimate=pl.CostEstimate(
            flops=16 * slots * width * units, bytes_accessed=12 * slots * width, transcendentals=0
        ),
        name="experts",
    )(meta, *args)


def turn_kernel(nparts, seqs, meta, *refs):
    parts = refs[:nparts]
    (
        res_ref,
        up_ref,
        gate_ref,
        code_ref,
        wr_ref,
        gain_ref,
        wo_ref,
        resgrad_ref,
        branch_ref,
        out_ref,
        logit_ref,
        gaingrad_ref,
    ) = refs[nparts:]
    rows, width = res_ref.shape
    span = rows // seqs
    total = parts[0][...].astype(f32)
    for part in parts[1:]:
        total = total + part[...].astype(f32)
    held = -(-rows // LANES) * LANES
    lines = total[rows:, 0:held] + total[rows:, width // 2 : width // 2 + held]
    blank = jnp.zeros((LANES - lines.shape[0], held), f32)
    gate_grad = jnp.concatenate([lines, blank], axis=0).T[0:rows]
    gate_grad = jnp.where(code_ref[...] > 0, gate_grad, 0.0)
    gates = gate_ref[...]
    logit_grad = gates * (gate_grad - jnp.sum(gates * gate_grad, axis=-1, keepdims=True))
    logit_ref[...] = logit_grad
    normed_grad = total[0:rows] + lax.dot_general(
        logit_grad,
        wr_ref[...].astype(f32),
        (((1,), (1,)), ((), ())),
        preferred_element_type=f32,
        precision=lax.Precision.HIGHEST,
    )
    res = res_ref[...]
    scale = lax.rsqrt(jnp.mean(res * res, axis=-1, keepdims=True) + eps)
    gaingrad_ref[...] = jnp.sum(normed_grad * (res * scale), axis=0, keepdims=True)
    scaled = normed_grad * gain_ref[...]
    row = meta[seqs] + lax.broadcasted_iota(jnp.int32, (span, 1), 0)
    valid = jnp.concatenate([(row < meta[s]).astype(f32) for s in range(seqs)], axis=0)
    upstream = jnp.where(valid > 0, up_ref[...].astype(f32), 0.0)
    centre = jnp.mean(scaled * res, axis=-1, keepdims=True)
    res_grad = upstream + scaled * scale - res * (scale * scale * scale * centre)
    resgrad_ref[...] = res_grad
    branch = res_grad.astype(bf16)
    branch_ref[...] = branch
    mixed = dot_nt(branch, wo_ref[...]).astype(bf16).astype(f32)
    half = span // 2
    low = lanes_of(half) < HD
    for s in range(seqs):
        at = slice(s * half, (s + 1) * half)
        for j in range(out_ref.shape[0] // 2):
            cols = slice(j * LANES, (j + 1) * LANES)
            upper = mixed[s * span : s * span + half, cols]
            lower = mixed[s * span + half : (s + 1) * span, cols]
            out_ref[2 * j, at] = jnp.where(low, upper, pltpu.roll(lower, HD, 1)).astype(bf16)
            out_ref[2 * j + 1, at] = jnp.where(low, pltpu.roll(upper, HD, 1), lower).astype(bf16)


def turn(meta, seqs, parts, res, up, gates, code, wr, gain, wo):
    rows, width = res.shape
    heads = wo.shape[0] // HD
    vmem = pl.BlockSpec(memory_space=pltpu.VMEM)
    return pl.pallas_call(
        functools.partial(turn_kernel, len(parts), seqs),
        out_shape=(
            jax.ShapeDtypeStruct((rows, width), f32),
            jax.ShapeDtypeStruct((rows, width), bf16),
            jax.ShapeDtypeStruct((heads, rows // 2, LANES), bf16),
            jax.ShapeDtypeStruct((rows, LANES), f32),
            jax.ShapeDtypeStruct((1, width), f32),
        ),
        in_specs=[pl.BlockSpec(memory_space=pltpu.SMEM)] + [vmem] * (len(parts) + 7),
        out_specs=(vmem,) * 5,
        compiler_params=pltpu.CompilerParams(vmem_limit_bytes=VMEM_LIMIT),
        cost_estimate=pl.CostEstimate(
            flops=4 * rows * width * width, bytes_accessed=4 * width * width, transcendentals=0
        ),
        name="turn_back",
    )(meta, *parts, res, up, gates, code, wr, gain, wo)


def back_kernel(
    replicas,
    meta,
    grad_ref,
    qk_ref,
    v_ref,
    qkt_ref,
    stat_ref,
    cos_ref,
    sin_ref,
    out_ref,
    do_ref,
    dk_ref,
    dv_ref,
    dqt_ref,
):
    zs, place, rows, _ = out_ref.shape
    total = qk_ref.shape[1]
    span = total // (zs * place)
    seqs = rows // span
    s = pl.program_id(0)
    half = span // 2
    for e in range(total // span):
        chunk = grad_ref[e].astype(f32)
        do_ref[e * span : e * span + half, :] = chunk
        do_ref[e * span + half : (e + 1) * span, :] = pltpu.roll(chunk, HD, 1)
    dk_ref[...] = jnp.zeros_like(dk_ref)
    dv_ref[...] = jnp.zeros_like(dv_ref)
    key_row = lax.broadcasted_iota(jnp.int32, (SLAB, SLAB), 0)
    query_col = lax.broadcasted_iota(jnp.int32, (SLAB, SLAB), 1)
    def one_slab(lo):
        hi = lo + 2 * SLAB
        mid = lo + SLAB
        grad = do_ref[lo:hi, :]
        grad_low = grad.astype(bf16)
        grad_t = grad.T[0:HD]
        delta = jnp.sum(grad_t * stat_ref[0, 0:HD, lo:hi], axis=0, keepdims=True)
        grad_t = grad_t.astype(bf16)
        log_total = stat_ref[0, HD : HD + 1, lo:hi]

        def piece(start, stop, first, last, masked):
            cols = slice(first - lo, last - lo)
            scores = dot(qk_ref[0, start:stop, HD:LANES], qkt_ref[0, 0:HD, first:last])
            probs = jnp.exp(scores - log_total[:, cols])
            if masked:
                probs = jnp.where(key_row <= query_col, probs, 0.0)
            prob_grad = dot(v_ref[0, start:stop, 0:HD], grad_t[:, cols])
            score_grad = (probs * (prob_grad - delta[:, cols])).astype(bf16)
            dv_ref[start:stop, :] += dot(probs.astype(bf16), grad_low[cols])
            dk_ref[start:stop, :] += dot(score_grad, qk_ref[0, first:last, :])
            return dot(qkt_ref[0, :, start:stop], score_grad)

        moved = piece(lo, mid, lo, mid, True)
        moved_next = piece(mid, hi, mid, hi, True) + piece(lo, mid, mid, hi, False)
        if lo:
            full = piece(0, lo, lo, hi, False)
            moved = moved + full[:, 0:SLAB]
            moved_next = moved_next + full[:, SLAB:]
        dqt_ref[:, lo:mid] = moved
        dqt_ref[:, mid:hi] = moved_next

    def no_slab(lo):
        dqt_ref[:, lo : lo + 2 * SLAB] = jnp.zeros((LANES, 2 * SLAB), f32)

    for i, lo in enumerate(range(0, total, 2 * SLAB)):
        if replicas > 1:
            mine = meta[seqs] == i % replicas
            pl.when(mine)(functools.partial(one_slab, lo))
            pl.when(jnp.logical_not(mine))(functools.partial(no_slab, lo))
        else:
            one_slab(lo)

    low = lanes_of(SLAB) < HD
    for lo in range(0, total, SLAB):
        at = slice(lo, lo + SLAB)
        both = jnp.where(low, dk_ref[at, :], dqt_ref[:, at].T * HD ** (-0.5))
        both = pltpu.roll(both, HD, 1)
        dk_ref[at, :] = both * cos_ref[at, :] - half_swap(both) * sin_ref[at, :]
        dv_ref[at, :] = jnp.where(low, dv_ref[at, :], 0.0)
    dest = pl.ds(pl.multiple_of(s * span, 32), span)
    for d in range(zs):
        for j in range(place):
            at = pl.multiple_of((meta[seqs + 1 + d] * place + meta[seqs + 1 + zs + j]) * span, 32)
            out_ref[d, j, dest, 0:LANES] = dk_ref[pl.ds(at, span), :].astype(bf16)
            out_ref[d, j, dest, LANES:PACK] = dv_ref[pl.ds(at, span), :].astype(bf16)


def back(meta, grads, qk, v, qkt, stat, cos, sin, shape, seqs, replicas):
    total = qk.shape[1]
    span = total // grads.shape[0]
    return pl.pallas_call(
        functools.partial(back_kernel, replicas),
        grid=(seqs,),
        out_shape=jax.ShapeDtypeStruct(shape, bf16),
        in_specs=[
            pl.BlockSpec(memory_space=pltpu.SMEM),
            pl.BlockSpec((total // span, span // 2, LANES), lambda s: (0, s, 0)),
            pl.BlockSpec((1, total, LANES), lambda s: (s, 0, 0)),
            pl.BlockSpec((1, total, LANES), lambda s: (s, 0, 0)),
            pl.BlockSpec((1, LANES, total), lambda s: (s, 0, 0)),
            pl.BlockSpec((1, HD + 8, total), lambda s: (s, 0, 0)),
            pl.BlockSpec((total, LANES), lambda s: (0, 0)),
            pl.BlockSpec((total, LANES), lambda s: (0, 0)),
        ],
        out_specs=pl.BlockSpec(shape, lambda s: (0, 0, 0, 0)),
        scratch_shapes=[
            pltpu.VMEM((total, LANES), f32),
            pltpu.VMEM((total, LANES), f32),
            pltpu.VMEM((total, LANES), f32),
            pltpu.VMEM((LANES, total), f32),
        ],
        compiler_params=pltpu.CompilerParams(vmem_limit_bytes=VMEM_LIMIT),
        cost_estimate=pl.CostEstimate(
            flops=10 * seqs * total * total * LANES,
            bytes_accessed=6 * seqs * total * PACK,
            transcendentals=seqs * total * total // 2,
        ),
        name="attend_backward",
    )(meta, grads, qk, v, qkt, stat, cos, sin)


def expert_grads_kernel(x_ref, both_ref, act_ref, pg_ref, *refs):
    outs, acc_ref = refs[:-1], refs[-1]
    width = x_ref.shape[2]

    @pl.when(pl.program_id(0) == 0)
    def _():
        acc_ref[...] = jnp.zeros_like(acc_ref)

    acc_ref[0:width, :] += dot_tn(x_ref[0], both_ref[0])
    acc_ref[width:, :] += dot_tn(act_ref[0], pg_ref[0])

    @pl.when(pl.program_id(0) == pl.num_programs(0) - 1)
    def _():
        for k, out_ref in enumerate(outs):
            rows = out_ref.shape[0]
            out_ref[...] = acc_ref[k * rows : (k + 1) * rows, :].astype(bf16)


def expert_grads(x, both, act, pg):
    zs, slots, width = x.shape
    units = act.shape[2]
    pieces = 4
    piece = (width + units) // pieces

    def block(a):
        return pl.BlockSpec((1,) + a.shape[1:], lambda i: (i, 0, 0))

    return pl.pallas_call(
        expert_grads_kernel,
        grid=(zs,),
        out_shape=(jax.ShapeDtypeStruct((piece, width), bf16),) * pieces,
        in_specs=[block(a) for a in (x, both, act, pg)],
        out_specs=(pl.BlockSpec((piece, width), lambda i: (0, 0)),) * pieces,
        scratch_shapes=[pltpu.VMEM((width + units, width), f32)],
        compiler_params=pltpu.CompilerParams(vmem_limit_bytes=VMEM_LIMIT),
        cost_estimate=pl.CostEstimate(
            flops=6 * zs * slots * width * units, bytes_accessed=8 * zs * slots * width, transcendentals=0
        ),
        name="expert_grads",
    )(x, both, act, pg)


def late_kernel(column, mixed_ref, branch_ref, pay_ref, logit_ref, gain_ref, out_ref):
    width = mixed_ref.shape[1]
    out_ref[:, 0:width] = dot_tn(mixed_ref[...], branch_ref[...]).astype(bf16)
    logit = logit_ref[...]
    high = logit.astype(bf16)
    low = (logit - high.astype(f32)).astype(bf16)
    normed = pay_ref[...]
    side = dot_tn(normed, high) + dot_tn(normed, low)
    gain = jnp.broadcast_to(gain_ref[...], (LANES, width)).T
    out_ref[:, width:] = jnp.where(lanes_of(width) == column, gain, side).astype(bf16)


def late_grads(column, mixed, branch, pay, logit, gain):
    rows, width = mixed.shape
    vmem = pl.BlockSpec(memory_space=pltpu.VMEM)
    return pl.pallas_call(
        functools.partial(late_kernel, column),
        out_shape=jax.ShapeDtypeStruct((width, width + LANES), bf16),
        in_specs=[vmem] * 5,
        out_specs=vmem,
        compiler_params=pltpu.CompilerParams(vmem_limit_bytes=VMEM_LIMIT),
        cost_estimate=pl.CostEstimate(
            flops=2 * rows * width * width, bytes_accessed=4 * width * width, transcendentals=0
        ),
        name="late_grads",
    )(mixed, branch, pay, logit, gain)


def head_grads_kernel(dqkv_ref, normed_ref, out_ref, acc_ref):
    _, place, rows, pack = dqkv_ref.shape

    @pl.when(pl.program_id(0) == 0)
    def _():
        acc_ref[...] = jnp.zeros_like(acc_ref)

    left = dqkv_ref[0].reshape(place * rows, pack)
    acc_ref[...] += dot_tn(left, normed_ref[0].reshape(place * rows, normed_ref.shape[3]))

    @pl.when(pl.program_id(0) == pl.num_programs(0) - 1)
    def _():
        out_ref[...] = acc_ref[...].T.astype(bf16)


def head_grads(dqkv, normed):
    zs, place, rows, width = normed.shape
    return pl.pallas_call(
        head_grads_kernel,
        grid=(zs,),
        out_shape=jax.ShapeDtypeStruct((width, PACK), bf16),
        in_specs=[
            pl.BlockSpec((1, place, rows, PACK), lambda i: (i, 0, 0, 0)),
            pl.BlockSpec((1, place, rows, width), lambda i: (i, 0, 0, 0)),
        ],
        out_specs=pl.BlockSpec((width, PACK), lambda i: (0, 0)),
        scratch_shapes=[pltpu.VMEM((PACK, width), f32)],
        compiler_params=pltpu.CompilerParams(vmem_limit_bytes=VMEM_LIMIT),
        cost_estimate=pl.CostEstimate(
            flops=2 * zs * place * rows * width * PACK,
            bytes_accessed=2 * zs * place * rows * width,
            transcendentals=0,
        ),
        name="head_grads",
    )(dqkv, normed)


def spread_kernel(dqkv_ref, w_ref, near_ref, far_ref):
    _, place, rows, pack = dqkv_ref.shape
    for ref, first in ((near_ref, 0), (far_ref, place // 2)):
        for j in range(place // 2):
            ref[0, j] = dot_nt(dqkv_ref[0, first + j], w_ref[...]).astype(bf16)


def spread(dqkv, w, picked):
    _, place, rows, pack = dqkv.shape
    width = w.shape[0]
    first, step = picked[0], (picked[1] - picked[0] if len(picked) > 1 else 0)
    half = jax.ShapeDtypeStruct((len(picked), place // 2, rows, width), bf16)
    out = pl.BlockSpec((1, place // 2, rows, width), lambda i: (i, 0, 0, 0))
    return pl.pallas_call(
        spread_kernel,
        grid=(len(picked),),
        out_shape=(half, half),
        in_specs=[
            pl.BlockSpec((1, place, rows, pack), lambda i: (first + i * step, 0, 0, 0)),
            pl.BlockSpec(w.shape, lambda i: (0, 0)),
        ],
        out_specs=(out, out),
        compiler_params=pltpu.CompilerParams(vmem_limit_bytes=VMEM_LIMIT),
        cost_estimate=pl.CostEstimate(
            flops=2 * len(picked) * place * rows * pack * width,
            bytes_accessed=2 * len(picked) * place * rows * width,
            transcendentals=0,
        ),
        name="spread",
    )(dqkv, w)


def finish_kernel(nparts, *refs):
    hid_ref, gain_ref, resgrad_ref = refs[0:3]
    parts = refs[3 : 3 + nparts]
    out_ref = refs[-1]
    total = parts[0][...].astype(f32)
    for part in parts[1:]:
        total = total + part[...].astype(f32)
    x = hid_ref[...].astype(f32)
    scale = lax.rsqrt(jnp.mean(x * x, axis=-1, keepdims=True) + eps)
    scaled = total * gain_ref[...]
    centre = jnp.mean(scaled * x, axis=-1, keepdims=True)
    out_ref[...] = resgrad_ref[...] + scaled * scale - x * (scale * scale * scale * centre)


def finish(hidden, gain, resgrad, parts):
    vmem = pl.BlockSpec(memory_space=pltpu.VMEM)
    return pl.pallas_call(
        functools.partial(finish_kernel, len(parts)),
        out_shape=jax.ShapeDtypeStruct(hidden.shape, f32),
        in_specs=[vmem] * (3 + len(parts)),
        out_specs=vmem,
        compiler_params=pltpu.CompilerParams(vmem_limit_bytes=VMEM_LIMIT),
        name="input_grad",
    )(hidden, gain, resgrad, *parts)


def body(
    hidden,
    lengths,
    expert_ids,
    pair_keep,
    attn_gain,
    query_weight_matrix,
    key_weight_matrix,
    value_weight_matrix,
    attention_output_weight,
    moe_gain,
    router_weight_matrix,
    w_gate_up,
    w_down,
    out_grad,
):
    seqs, span, width = hidden.shape
    rows = seqs * span
    top_k = expert_ids.shape[2]
    ep = lax.axis_size("ep")
    dp = lax.axis_size("dp")
    zs, ys, _ = ep_shape(ep)
    place = 2 * ys
    me = lax.axis_index("ep").astype(jnp.int32)
    expert_count = w_gate_up.shape[0] * ep
    capacity = max(2, rows * top_k // expert_count)
    cap = -(-capacity // 16) * 16
    heads = query_weight_matrix.shape[1] // HD
    kv_heads = key_weight_matrix.shape[1] // HD
    replicas = ep // heads
    total = span * ep
    own_rows = query_weight_matrix.shape[0]
    hidden = hidden.reshape(rows, width)
    out_grad = out_grad.reshape(rows, width)

    def per_head(weight, count):
        split = weight.reshape(own_rows, count, HD).transpose(1, 0, 2)
        return jnp.repeat(split, heads // count, axis=0)

    small = jnp.concatenate(
        [router_weight_matrix, attn_gain[:, None], moe_gain[:, None]], axis=1
    )
    small = jnp.pad(small, ((0, 0), (0, PACK - 3 * HD - small.shape[1])))
    packed = jnp.concatenate(
        [
            per_head(query_weight_matrix, heads),
            per_head(key_weight_matrix, kv_heads),
            per_head(value_weight_matrix, kv_heads),
            jnp.broadcast_to(small[None], (heads,) + small.shape),
        ],
        axis=2,
    )
    packed = jnp.repeat(packed, replicas, axis=0)
    packed = jnp.broadcast_to(packed[None], (dp,) + packed.shape).reshape(
        dp * ep, own_rows, PACK
    )
    packed = lax.all_to_all(packed, ("dp", "ep"), split_axis=0, concat_axis=0, tiled=True)
    head_w = packed.reshape(dp * ep * own_rows, PACK)
    at = 3 * HD
    wr = jnp.pad(head_w[:, at : at + expert_count], ((0, 0), (0, LANES - expert_count)))
    gains = head_w[:, at + expert_count : at + expert_count + 2].astype(f32)
    gain_one = gains[:, 0].reshape(1, width)
    gain_two = gains[:, 1].reshape(1, width)
    head_w = jnp.where(jnp.arange(PACK)[None, :] < at, head_w, jnp.zeros((), bf16))

    positions = me * span + jnp.arange(span, dtype=jnp.int32)
    is_valid = positions[None, :] < lengths[:, None]

    def prepare(earlier_step):
        expert_range = jnp.arange(LANES, dtype=jnp.int32)
        hit = phase(expert_ids, earlier_step)[0][..., None] == expert_range
        chosen = jnp.any(hit, axis=2).reshape(rows, LANES).astype(f32)
        live = jnp.any(hit & (pair_keep[..., None] > 0), axis=2) & is_valid[..., None]
        live = live.reshape(rows, LANES).astype(bf16)
        earlier = jnp.arange(rows)[:, None] > jnp.arange(rows)[None, :]
        slot = jnp.dot(earlier.astype(bf16), live, preferred_element_type=f32)
        code = jnp.where((slot < capacity) & (live > 0), slot + 1.0, -chosen)
        code_rows = -(-expert_count // 16) * 16
        lines = jnp.pad(code[:, 0:code_rows].T.astype(bf16), ((0, 0), (0, width - rows)))
        lifted = jnp.concatenate([out_grad, lines])

        rates = theta_base ** (-2.0 * jnp.arange(HD // 2, dtype=f32) / HD)
        rates = phase(rates, earlier_step)[0]
        angle = jnp.arange(total, dtype=jnp.int32).astype(f32)[:, None] * rates[None, :]
        cos = jnp.tile(jnp.cos(angle), (1, 4))
        sin = jnp.sin(angle)
        sin = jnp.concatenate([-sin, sin, -sin, sin], axis=1)
        return code, lifted, cos, sin

    core = me % 2
    col = (me // 2) % ys
    plane = me // place
    planes = (plane + jnp.arange(zs, dtype=jnp.int32)) % zs
    rows_at = (col + jnp.arange(ys, dtype=jnp.int32)) % ys
    places = jnp.concatenate([rows_at * 2 + core, rows_at * 2 + 1 - core])
    replica = me % replicas if replicas > 1 else jnp.zeros((), jnp.int32)
    attend_meta = jnp.concatenate([lengths, replica[None], planes, places]).astype(jnp.int32)
    expert_meta = jnp.concatenate([jnp.stack([me, plane]), places]).astype(jnp.int32)
    project_meta = expert_meta[1:]
    turn_meta = jnp.concatenate([lengths, (me * span)[None]]).astype(jnp.int32)

    order = list(range(zs))

    def move(x, sender=False, **offset):
        return lax.ppermute(x, "ep", (send_to if sender else fetch_from)(ep, **offset))

    def steps(t):
        n = len(order)
        return t < n - 1, t < n, 1 <= t <= n, 2 <= t < n + 2

    columns, near, far, carried, x = [hidden], {}, {}, None, hidden
    wo_part = [attention_output_weight]
    for t in range(len(order) + 2):
        on_z, on_y, on_core, on_work = steps(t)
        z_new = [move(columns[t], dz=1)] if on_z else []
        y_new = [move(columns[t], dy=k) for k in range(1, ys)] if on_y else []
        c_new = [move(block, dc=1) for block in near[t - 1]] if on_core else []
        if on_work:
            d = order[t - 2]
            carried = project(
                project_meta, near[t - 2] + far[t - 2], head_w, gain_one, cos, sin, zs, d, carried
            )
        block = wo_part[0]
        wo_new = []
        if t == zs - 1:
            wo_new = [move(block, dz=k) for k in range(1, zs)]
        elif t == zs:
            wo_new = [move(block, dy=k) for k in range(1, ys)]
        x, columns, near, far, z_new, y_new, c_new, carried, wo_part, wo_new = phase_tree(
            x, columns, near, far, z_new, y_new, c_new, carried, wo_part, wo_new
        )
        if wo_new:
            wo_part = [jnp.stack(wo_part + wo_new)]
        columns = columns + z_new
        if on_y:
            near[t] = [columns[t]] + y_new
        if on_core:
            far[t - 1] = c_new
        if t == 0:
            code, lifted, cos, sin = prepare(columns[-1])
        if t == len(order) - 2:
            upstream = lax.all_gather(phase(lifted, columns[-1])[0], "ep", axis=0)
    wo_new = [
        lax.ppermute(wo_part[0], "dp", [((i + k) % dp, i) for i in range(dp)]) for k in range(1, dp)
    ]
    normed_all, qkv = carried
    made, qk, v, qkt, stat = attend(attend_meta, qkv, seqs, replicas)
    made, wo_new, wo_part = phase_tree(made, wo_new, wo_part)
    recv = lax.all_to_all(made, "ep", split_axis=0, concat_axis=0, tiled=True)
    wo_part = jnp.stack(wo_part + wo_new)
    wo_part = [jnp.stack([wo_part, move(wo_part, dc=1)])]
    line = jnp.arange(dp * ep, dtype=jnp.int32)
    away = (line % 2 - core) % 2
    away = away * dp + (line // ep - lax.axis_index("dp")) % dp
    away = away * ys + ((line // 2) % ys - col) % ys
    away = away * zs + ((line // place) % zs - plane) % zs
    wo = wo_part[0].reshape(dp * ep, own_rows, width)
    wo = jnp.take(wo, away, axis=0, mode="clip").reshape(heads * HD, width)
    if replicas > 1:
        recv = recv.reshape((heads, replicas) + recv.shape[1:]).sum(axis=1).astype(bf16)
    res, pay, mixed, gates = middle(seqs, recv, hidden, wo, gain_two, wr, code)

    count = zs
    columns, near, far, chips, totals = [pay], {}, {}, {}, {}
    outs, carried, extra, passed = {}, None, {}, None
    rings = [[(i, (i + d) % dp) for i in range(dp)] for d in range(1, dp)]
    cuts = ((1,), tuple(range(2, zs)), (0,))

    def hop(value):
        return lax.ppermute(value, "ep", fetch_from(ep, dz=1))

    def swap(piece):
        return [lax.ppermute(piece, "dp", ring) for ring in rings]

    for t in range(count + 5):
        on_z, on_y, on_core, on_work = steps(t)
        z_new = [move(columns[t], dz=1)] if on_z else []
        y_new = [move(columns[t], dy=k) for k in range(1, ys)] if on_y else []
        c_new = [move(block, dc=1) for block in near[t - 1]] if on_core else []
        rc, ry, rz = t - 3, t - 4, t - 5
        rc_new = [move(outs[rc][1], True, dc=1)] if 0 <= rc < count else []
        ry_new = [move(chips[ry][d], True, dy=d) for d in range(1, ys)] if 0 <= ry < count else []
        rz_new = []
        if 1 <= rz < count:
            rz_new = [hop(totals[rz] if rz == 1 else add_low(totals[rz], passed))]
        new = {}
        if on_work:
            d = order[t - 2]
            out = experts(
                expert_meta,
                near[t - 2] + far[t - 2],
                upstream,
                w_gate_up[0],
                w_down[0],
                wr,
                cap,
                zs,
                d,
                carried,
            )
            outs[t - 2], carried = out[:2], out[2:]
        if t == count + 2:
            new["got"] = move(carried[1], True, dc=1)
            new["grads"] = list(expert_grads(carried[2], carried[5], carried[4], carried[3]))
        if t == count + 3:
            new["chip"] = [
                [
                    add_low(
                        jnp.stack([carried[0][k, d] for k in cut]),
                        jnp.stack([extra["got"][k, d] for k in cut]),
                    )
                    for cut in cuts
                    if cut
                ]
                for d in range(ys)
            ]
        if t == count + 4:
            new["swap"] = swap(extra["grads"][0])
            new["first"] = [move(extra["chip"][d][0], True, dy=d) for d in range(1, ys)]
        state = (pay, columns, near, far, outs, chips, totals, carried, extra)
        state = phase_tree(state, z_new, y_new, c_new, rc_new, ry_new, rz_new, new)
        state, z_new, y_new, c_new, rc_new, ry_new, rz_new, new = state
        pay, columns, near, far, outs, chips, totals, carried, extra = state
        columns = columns + z_new
        if on_y:
            near[t] = [columns[t]] + y_new
        if on_core:
            far[t - 1] = c_new
        if rc_new:
            chips[rc] = [add_low(outs[rc][0][d], rc_new[0][d]) for d in range(ys)]
        if 0 <= ry < count:
            totals[ry] = add_low(chips[ry][0], *ry_new)
        if rz_new:
            passed = rz_new[0]
        extra.update(new)
    parts = [totals[0]] + ([passed] if zs > 1 else [])
    moe_chip = extra["chip"]
    grads_low = extra["grads"]

    res_grad, branch, grads, logit_grad, gain_two_grad = turn(
        turn_meta, seqs, parts, res, out_grad, gates, code, wr, gain_two, wo
    )
    if replicas > 1:
        grads = jnp.repeat(grads, replicas, axis=0)
    grads = lax.all_to_all(grads, "ep", split_axis=0, concat_axis=0, tiled=True)
    late = late_grads(expert_count, mixed, branch, pay, logit_grad, gain_two_grad)
    late = late.reshape(dp, zs * ys, 2, own_rows, late.shape[1])

    def stage_parts(value, axis, here_at, size):
        return [
            lax.dynamic_index_in_dim(value, (here_at + d) % size, axis, keepdims=False)
            for d in range(size)
        ]

    late_parts = stage_parts(late, 2, core, 2)
    moe = [add_low(moe_chip[0][0], *extra["first"])]
    moe_new = [move(moe_chip[d][1], True, dy=d) for d in range(1, ys)]
    grads_moved = [extra["swap"], swap(grads_low[1])]
    state = (grads, moe, moe_new, moe_chip, late_parts, grads_low, grads_moved)
    grads, moe, moe_new, moe_chip, late_parts, grads_low, grads_moved = phase_tree(*state)
    moe.append(add_low(moe_chip[0][1], *moe_new))

    dqkv = back(attend_meta, grads, qk, v, qkt, stat, cos, sin, qkv.shape, seqs, replicas)
    moe_new = [move(moe_chip[d][2], True, dy=d) for d in range(1, ys)]
    passed = hop(moe[0][0])
    late_got = [move(late_parts[1], True, dc=1)]
    swapped = swap(grads_low[2])
    state = (dqkv, moe, moe_new, passed, moe_chip, late_parts, late_got, grads_low, swapped)
    state = phase_tree(*state)
    dqkv, moe, moe_new, passed, moe_chip, late_parts, late_got, grads_low, swapped = state
    moe.append(add_low(moe_chip[0][2], *moe_new))
    grads_moved.append(swapped)
    late = add_low(late_parts[0], *late_got)
    late_parts = stage_parts(late, 0, lax.axis_index("dp"), dp)
    late_got = [lax.ppermute(part, "dp", ring) for part, ring in zip(late_parts[1:], rings)]

    halves = ((1, 2), (3, 0)) if zs == 4 else (tuple(range(1, zs)), (0,))
    turn_order = [d for half in halves for d in half]
    near, far = ([part] for part in spread(dqkv, head_w, halves[0]))
    near, far, dqkv = phase_tree(near, far, dqkv)

    got = [move(far[0], True, dc=1)]
    more = spread(dqkv, head_w, halves[1])
    near.append(more[0])
    far.append(more[1])
    passed = hop(add_low(moe[1][0], passed))
    head_grad = head_grads(dqkv, normed_all).reshape(dp * ep, own_rows, PACK)
    state = (near, far, got, moe, passed, head_grad, late_parts, late_got, grads_low)
    near, far, got, moe, passed, head_grad, late_parts, late_got, grads_low = phase_tree(*state)
    late = add_low(late_parts[0], *late_got)
    plane_groups = [[c + 2 * k for k in range(zs * ys)] for c in range(2)]
    late = lax.all_to_all(
        late, "ep", split_axis=0, concat_axis=0, tiled=True, axis_index_groups=plane_groups
    )

    head_grad = lax.all_to_all(head_grad, ("dp", "ep"), split_axis=0, concat_axis=0, tiled=True)
    totals, received = {}, None

    def chip_of(d, *earlier):
        half = 0 if d in halves[0] else 1
        at = halves[half].index(d)
        mine, theirs = phase(near[half], got[half], *earlier)[:2]
        return [add_low(mine[at, y], theirs[at, y]) for y in range(ys)]

    chip = chip_of(turn_order[0])
    for k, d in enumerate(turn_order):
        ahead = chip_of(turn_order[k + 1], *chip) if k + 1 < len(turn_order) else []
        moved = [move(chip[y], True, dy=y) for y in range(1, ys)]
        if k:
            last = totals[turn_order[k - 1]]
            received = hop(last if k == 1 else add_low(last, received))
        if k == 0:
            got.append(move(far[1], True, dc=1))
            passed = hop(add_low(moe[1][1], passed)) if zs == 4 else passed
            swapped = swap(grads_low[3])
            near, got, chip, ahead, moved, passed, swapped = phase_tree(
                near, got, chip, ahead, moved, passed, swapped
            )
            grads_moved.append(swapped)
        elif k == 2:
            near, got, chip, ahead, moved, received, totals, head_grad = phase_tree(
                near, got, chip, ahead, moved, received, totals, head_grad
            )
        else:
            near, got, chip, ahead, moved, received, totals = phase_tree(
                near, got, chip, ahead, moved, received, totals
            )
        totals[d] = add_low(chip[0], *moved)
        chip = ahead
    parts = [totals[0], received]
    late = phase(late, totals[0], received)[0]
    late = late.astype(f32).sum(axis=0)
    mparts = [moe[-1][0], passed]
    sums = []
    for own, moved in zip(grads_low, grads_moved):
        piece = own.astype(f32)
        for other in moved:
            piece = piece + other.astype(f32)
        sums.append(piece)
    grads_total = jnp.concatenate(sums)
    gu_total = grads_total[0:width]
    d_total = grads_total[width:]

    head_grad = head_grad.astype(f32).reshape(dp, heads, replicas, own_rows, PACK).sum(axis=(0, 2))

    def rows_of(part, count):
        part = part.reshape(count, heads // count, own_rows, HD).sum(axis=1)
        return part.transpose(1, 0, 2).reshape(own_rows, count * HD)

    query_w_grad = rows_of(head_grad[..., 0:HD], heads)
    key_w_grad = rows_of(head_grad[..., HD : 2 * HD], kv_heads)
    value_w_grad = rows_of(head_grad[..., 2 * HD : 3 * HD], kv_heads)
    gain_one_grad = (
        jnp.sum(query_w_grad * query_weight_matrix.astype(f32), axis=1)
        + jnp.sum(key_w_grad * key_weight_matrix.astype(f32), axis=1)
        + jnp.sum(value_w_grad * value_weight_matrix.astype(f32), axis=1)
    ) / attn_gain.astype(f32)

    moe_own = res
    for part in mparts:
        moe_own = moe_own + part.astype(f32)
    output = jnp.where(
        is_valid[..., None], moe_own.reshape(seqs, span, width), 0.0
    ).astype(bf16)
    input_grad = finish(hidden, gain_one, res_grad, parts)
    model = width
    return (
        output,
        input_grad.reshape(seqs, span, width),
        gain_one_grad,
        query_w_grad,
        key_w_grad,
        value_w_grad,
        late[:, 0:model],
        late[:, model + expert_count],
        late[:, model : model + expert_count],
        gu_total[None],
        d_total[None],
    )


def solution(mesh):
    return jax.shard_map(
        body,
        mesh=mesh,
        in_specs=(
            P("dp", "ep", None),
            P("dp"),
            P("dp", "ep", None),
            P("dp", "ep", None),
            P(("dp", "ep")),
            P(("dp", "ep"), None),
            P(("dp", "ep"), None),
            P(("dp", "ep"), None),
            P(("dp", "ep"), None),
            P(("dp", "ep")),
            P(("dp", "ep"), None),
            P("ep", None, None),
            P("ep", None, None),
            P("dp", "ep", None),
        ),
        out_specs=(
            P("dp", "ep", None),
            P("dp", "ep", None),
            P(("dp", "ep")),
            P(("dp", "ep"), None),
            P(("dp", "ep"), None),
            P(("dp", "ep"), None),
            P(("dp", "ep"), None),
            P(("dp", "ep")),
            P(("dp", "ep"), None),
            P("ep", None, None),
            P("ep", None, None),
        ),
        check_vma=False,
    )
```
